32 devices in a mesh: dp: 8 (over y, x, core), blk: 4 (over z).
Axes of the slice: x: 2, y: 2, z: 4, core: 2. Of those that a mesh axis runs over, the one named last changes fastest.
Arguments:
- tokens: bfloat16 [8192, 2048], P(('dp', 'blk')), may hold values from -6 to 6
- cotangent: bfloat16 [8192, 2048], P(('dp', 'blk')), may hold values from -6 to 6
- lengths: int32 [3, 4], replicated, may hold values from 0 to 4096, as said below
- branch_weight: bfloat16 [2048, 2560], P('dp', 'blk'), may hold values from -0.125 to 0.125
- mixer_weight: bfloat16 [2048, 2560], P('dp', 'blk'), may hold values from -0.125 to 0.125
- branch_bias: bfloat16 [2560], P('blk'), may hold values from -3 to 3
- mixer_bias: bfloat16 [2560], P('blk'), may hold values from -3 to 3
- conv_taps: bfloat16 [2560, 4], P('blk'), may hold values from -3 to 3
- conv_bias: bfloat16 [2560], P('blk'), may hold values from -2 to 2
- decay_weight: bfloat16 [2560, 160], P('blk'), may hold values from -0.5 to 0.5
- input_weight: bfloat16 [2560, 160], P('blk'), may hold values from -0.5 to 0.5
- decay_bias: bfloat16 [2560], P('blk'), may hold values from -4 to 4
- input_bias: bfloat16 [2560], P('blk'), may hold values from -4 to 4
- decay_param: bfloat16 [2560], P('blk'), may hold values from 4 to 11
- output_weight: bfloat16 [2560, 2048], P('blk', 'dp'), may hold values from -0.25 to 0.25
- first_gain: bfloat16 [2048], replicated, may hold values from 0.099609375 to 1.8984375
- second_gain: bfloat16 [2048], replicated, may hold values from 0.099609375 to 1.8984375
- gate_weight: bfloat16 [2048, 6144], P(None, ('dp', 'blk')), may hold values from -0.125 to 0.125
- up_weight: bfloat16 [2048, 6144], P(None, ('dp', 'blk')), may hold values from -0.125 to 0.125
- down_weight: bfloat16 [6144, 2048], P(('dp', 'blk')), may hold values from -0.15625 to 0.15625
Outputs:
- output: bfloat16 [8192, 2048], P(('dp', 'blk'))
- token_grad: bfloat16 [8192, 2048], P(('dp', 'blk'))
- branch_weight_grad: float32 [2048, 2560], P('dp', 'blk')
- mixer_weight_grad: float32 [2048, 2560], P('dp', 'blk')
- branch_bias_grad: float32 [2560], P('blk')
- mixer_bias_grad: float32 [2560], P('blk')
- conv_taps_grad: float32 [2560, 4], P('blk')
- conv_bias_grad: float32 [2560], P('blk')
- decay_weight_grad: float32 [2560, 160], P('blk')
- input_weight_grad: float32 [2560, 160], P('blk')
- decay_bias_grad: float32 [2560], P('blk')
- input_bias_grad: float32 [2560], P('blk')
- decay_param_grad: float32 [2560], P('blk')
- output_weight_grad: float32 [2560, 2048], P('blk', 'dp')
- first_gain_grad: float32 [2048], replicated
- second_gain_grad: float32 [2048], replicated
- gate_weight_grad: float32 [2048, 6144], P(None, ('dp', 'blk'))
- up_weight_grad: float32 [2048, 6144], P(None, ('dp', 'blk'))
- down_weight_grad: float32 [6144, 2048], P(('dp', 'blk'))
The draws below stay inside these ranges and needn't reach their ends.
Inputs may be any that keep to these rules, and one draw needn't show every extreme that they name: Row b holds the lengths of the 4 sequence slots of bucket b in packing order, a slot may be empty; they sum to at most the bucket's size (4096, or 2048 for the first and the last bucket) and the rest of the bucket is padding at its end.
All inputs are finite; a program needn't handle non-finite values.
Results may differ from the reference program's by a relative error of at most 0.02.
Values may be sent and summed in bfloat16 or wider, within the bound.
No kernel may reach another device: no remote copies, remote signals or barrier semaphores. Data moves between devices by JAX's collectives and lax.ppermute only.
A program may use at most 384 MiB of HBM per device.

```python
import jax
import jax.numpy as jnp
from jax import lax

D = 2048
R = 2560
H = 16
F = 6144
K = 4
BW = 160
ROWS_DP = 1024
BUCKET = 4096
NBUCKETS = 3
TOKENS = 8192


def draw_lengths(key, part):
    key = jax.random.fold_in(key, 11)
    subkeys = jax.random.split(key, 5)
    index = jnp.arange(NBUCKETS)
    edge = (index == 0) | (index == NBUCKETS - 1)
    capacity = jnp.where(edge, BUCKET // 2, BUCKET)
    opening = jax.random.randint(subkeys[0], (NBUCKETS,), 0, ROWS_DP // 2 + 1)
    closing = jax.random.randint(subkeys[1], (NBUCKETS,), capacity - ROWS_DP + 1, capacity + 1)
    chosen = jax.random.randint(subkeys[2], (), 1, NBUCKETS - 1)
    picked = index == chosen
    opening = jnp.where(picked, 0, opening)
    closing = jnp.where(picked, capacity, closing)
    remain = capacity - closing
    third_len = jax.random.randint(subkeys[3], (NBUCKETS,), 0, remain + 1)
    fourth_len = jax.random.randint(subkeys[4], (NBUCKETS,), 0, remain - third_len + 1)
    return jnp.stack([opening, closing - opening, third_len, fourth_len], axis=1).astype(jnp.int32)


def draw_decay_param(key, part):
    key = jax.random.fold_in(key, 23)
    subkeys = jax.random.split(key, 3)
    slow_share = 0.5
    slow_pick = jax.random.uniform(subkeys[0], (R,)) < slow_share
    slow_values = jax.random.uniform(subkeys[1], (R,), minval=9.0, maxval=11.0)
    fast_values = jax.random.uniform(subkeys[2], (R,), minval=4.0, maxval=5.5)
    return jnp.where(slow_pick, slow_values, fast_values).astype(jnp.bfloat16)


def block_levels(rng, shape, pieces, smallest, largest):
    def one(dim, parts):
        steps = jax.random.uniform(jax.random.fold_in(jax.random.fold_in(rng, 6), dim), (parts,), jnp.float32, smallest / len(pieces), largest / len(pieces))
        return jnp.repeat(jnp.exp(steps), shape[dim] // parts).reshape((-1,) + (1,) * (len(shape) - dim - 1))

    level = one(*pieces[0])
    for cut in pieces[1:]:
        level = level * one(*cut)
    return level


def bell_draw(rng, extent, scale, limit, cuts=(), kind=jnp.bfloat16):
    level = block_levels(rng, extent, cuts, -0.22, 0.18) if cuts else 1.0
    values = jax.random.normal(rng, extent, jnp.float32) * scale * level
    return jnp.minimum(jnp.maximum(values, -limit), limit).astype(kind)


def setup_inputs(seed: int = 0) -> dict:
    keys = jax.random.split(jax.random.key(seed), 21)
    return {
        "tokens": bell_draw(keys[0], (TOKENS, D), 1.0, 6.0, ((0, 32),)),
        "cotangent": bell_draw(keys[1], (TOKENS, D), 1.0, 6.0, ((0, 32),)),
        "lengths": draw_lengths(jax.random.fold_in(keys[20], 71), 0),
        "branch_weight": bell_draw(keys[3], (D, R), D ** -0.5, 0.125, ((0, 8), (1, 4))),
        "mixer_weight": bell_draw(keys[4], (D, R), D ** -0.5, 0.125, ((0, 8), (1, 4))),
        "branch_bias": bell_draw(keys[5], (R,), 0.5, 3.0, ((0, 4),)),
        "mixer_bias": bell_draw(keys[6], (R,), 0.5, 3.0, ((0, 4),)),
        "conv_taps": bell_draw(keys[7], (R, K), 0.5, 3.0, ((0, 4),)),
        "conv_bias": bell_draw(keys[8], (R,), 0.3, 2.0, ((0, 4),)),
        "decay_weight": bell_draw(keys[9], (R, BW), BW ** -0.5, 0.5, ((0, 4),)),
        "input_weight": bell_draw(keys[10], (R, BW), BW ** -0.5, 0.5, ((0, 4),)),
        "decay_bias": bell_draw(keys[11], (R,), 1.0, 4.0, ((0, 4),)),
        "input_bias": bell_draw(keys[12], (R,), 1.0, 4.0, ((0, 4),)),
        "decay_param": draw_decay_param(jax.random.fold_in(keys[20], 71), 0),
        "output_weight": bell_draw(keys[14], (R, D), (R // 4) ** -0.5, 0.25, ((0, 4), (1, 8))),
        "first_gain": jnp.clip(1.0 + 0.18 * jax.random.normal(keys[15], (D,), jnp.float32), 0.099609375, 1.8984375).astype(jnp.bfloat16),
        "second_gain": jnp.clip(1.0 + 0.18 * jax.random.normal(keys[16], (D,), jnp.float32), 0.099609375, 1.8984375).astype(jnp.bfloat16),
        "gate_weight": bell_draw(keys[17], (D, F), D ** -0.5, 0.125, ((1, 32),)),
        "up_weight": bell_draw(keys[18], (D, F), D ** -0.5, 0.125, ((1, 32),)),
        "down_weight": bell_draw(keys[19], (F, D), (F // 4) ** -0.5, 0.15625, ((0, 32),)),
    }


EPS = 1e-06
DECAY = 8.0

@jax.custom_vjp
def low(v):
    return lax.optimization_barrier(v.astype(jnp.bfloat16)).astype(jnp.float32)

@jax.custom_vjp
def low_back(v):
    return v

def low_keep(v):
    return (low(v), None)

def low_pass(kept, grad):
    return (grad,)

def back_keep(v):
    return (v, None)

def back_low(kept, grad):
    return (low(grad),)
low.defvjp(low_keep, low_pass)
low_back.defvjp(back_keep, back_low)

def affine(earlier, later):
    return (earlier[0] * later[0], later[0] * earlier[1] + later[1])

def normed(values, gain_vec):
    return values * lax.rsqrt(lax.optimization_barrier(jnp.mean(values * values, axis=-1, keepdims=True)) + EPS) * gain_vec

def coefficients(pre_decay, pre_input, conv_float, param_chan, carries, restart, filled):
    gate_decay = jax.nn.sigmoid(pre_decay)
    log_decay = -DECAY * gate_decay * jax.nn.softplus(-param_chan)
    square_root = jnp.sqrt(-jnp.expm1(2.0 * log_decay))
    factor = jnp.where(restart, 1.0, square_root)
    return (jnp.exp(log_decay) * carries, filled * factor * jax.nn.sigmoid(pre_input) * conv_float)

def matmul(former, latter):
    return jnp.dot(former, latter, precision=lax.Precision.HIGHEST, preferred_element_type=jnp.float32)

def segment_place(bucket_row, positions):
    first_end = bucket_row[0]
    second_end = first_end + bucket_row[1]
    third_end = second_end + bucket_row[2]
    final_end = third_end + bucket_row[3]
    begins = jnp.zeros_like(positions)
    for border in (first_end, second_end, third_end):
        begins = jnp.where(positions >= border, border, begins)
    return (positions - begins, (positions >= 0) & (positions < final_end))

def bucket_forward(params, inputs, bucket_row, anchor):
    branch_weight, mixer_weight, branch_bias, mixer_bias, conv_taps, conv_bias, decay_weight, input_weight, decay_bias, input_bias, decay_param, output_weight, first_gain, second_gain, gate_weight, up_weight, down_weight = params
    positions = jnp.arange(BUCKET, dtype=jnp.int32) - anchor
    seg_pos, filled = segment_place(bucket_row, positions)
    low_one = low(normed(inputs, first_gain))
    branch_pre = low_back(matmul(low_one, branch_weight) + branch_bias)
    branch_act = jax.nn.gelu(branch_pre)
    mixer_low = low_back(low(matmul(low_one, mixer_weight) + mixer_bias))
    conv_out = conv_bias + jnp.zeros_like(mixer_low)
    for lag in range(K):
        moved = jnp.concatenate([jnp.zeros((lag, R), jnp.float32), mixer_low[:BUCKET - lag]], axis=0)
        conv_out = conv_out + conv_taps[:, lag] * (seg_pos >= lag).astype(jnp.float32)[:, None] * moved
    conv_low = low(conv_out)
    blocks = conv_low.reshape(BUCKET, H, R // H)
    pre_decay = low_back(jnp.einsum('thc,hcd->thd', blocks, decay_weight.reshape(H, R // H, R // H), precision=lax.Precision.HIGHEST).reshape(BUCKET, R) + decay_bias)
    pre_input = low_back(jnp.einsum('thc,hcd->thd', blocks, input_weight.reshape(H, R // H, R // H), precision=lax.Precision.HIGHEST).reshape(BUCKET, R) + input_bias)
    restart = (seg_pos == 0)[:, None]
    carries = ((seg_pos != 0) & filled).astype(jnp.float32)[:, None]
    filled_col = filled.astype(jnp.float32)[:, None]
    decays, drives = coefficients(pre_decay, pre_input, conv_low, decay_param, carries, restart, filled_col)
    states = lax.associative_scan(affine, (decays, drives))[1]
    state_low = low_back(low(states))
    mixed_low = low(branch_act * state_low)
    resid = inputs + low_back(matmul(mixed_low, output_weight))
    low_two = low(normed(resid, second_gain))
    gate_pre = low_back(matmul(low_two, gate_weight))
    up_pre = low_back(matmul(low_two, up_weight))
    hidden = low(jax.nn.gelu(gate_pre) * up_pre)
    return resid + matmul(hidden, down_weight)

def reference(tokens, cotangent, lengths, branch_weight, mixer_weight, branch_bias, mixer_bias, conv_taps, conv_bias, decay_weight, input_weight, decay_bias, input_bias, decay_param, output_weight, first_gain, second_gain, gate_weight, up_weight, down_weight):
    params = tuple((weight.astype(jnp.float32) for weight in (branch_weight, mixer_weight, branch_bias, mixer_bias, conv_taps, conv_bias, decay_weight, input_weight, decay_bias, input_bias, decay_param, output_weight, first_gain, second_gain, gate_weight, up_weight, down_weight)))
    half = BUCKET // 2
    inputs = jnp.pad(tokens.astype(jnp.float32), ((half, half), (0, 0))).reshape(NBUCKETS, BUCKET, D)
    anchors = jnp.where(jnp.arange(NBUCKETS, dtype=jnp.int32) == 0, half, 0).astype(jnp.int32)

    def forward(weights, values):
        stepped = jax.checkpoint(bucket_forward)
        return lax.map(lambda bundle: stepped(weights, bundle[0], bundle[1], bundle[2]), (values, lengths, anchors))
    result, pullback = jax.vjp(forward, params, inputs)
    back_in = jnp.pad(cotangent.astype(jnp.float32), ((half, half), (0, 0))).reshape(NBUCKETS, BUCKET, D)
    grads, input_grads = pullback(back_in)
    result = result.reshape(NBUCKETS * BUCKET, D)[half:half + TOKENS]
    input_grads = input_grads.reshape(NBUCKETS * BUCKET, D)[half:half + TOKENS]
    return (result.astype(jnp.bfloat16), input_grads.astype(jnp.bfloat16), grads[0], grads[1], grads[2], grads[3], grads[4], grads[5], grads[6], grads[7], grads[8], grads[9], grads[10], grads[11], grads[12], grads[13], grads[14], grads[15], grads[16])
```

```python
from functools import partial

import jax
import jax.numpy as jnp
from jax import lax
from jax.experimental import pallas as pl
from jax.experimental.pallas import tpu as pltpu
from jax.sharding import PartitionSpec as P

BUCKET_DP = 4
EPS = 1e-06
DECAY = 8.0
TAPS = 4
QUARTERS = 4
TILE = 16
AXES = ("dp", "blk")
f32 = jnp.float32
bf16 = jnp.bfloat16
VMEM_BYTES = 40 * 2**20

BRANCH_BIAS, MIXER_BIAS, TAP_ROW, CONV_BIAS, DECAY_BIAS, INPUT_BIAS, PARAM = 0, 1, 2, 6, 7, 8, 9
SLOPE = 10


def plain(former, latter):
    return jnp.dot(former, latter, preferred_element_type=f32)


def trailing(former, latter):
    return lax.dot_general(former, latter, (((1,), (1,)), ((), ())), preferred_element_type=f32)


def leading(former, latter):
    return lax.dot_general(former, latter, (((0,), (0,)), ((), ())), preferred_element_type=f32)


class Places:
    def __init__(self, dp, blk):
        assert blk == QUARTERS and dp % (2 * QUARTERS) == 0
        self.n = dp * blk
        self.high = dp // (2 * QUARTERS)

    @staticmethod
    def split(i):
        return i // 32, i // 8 % 4, i // 4 % 2, i % 4

    @staticmethod
    def join(h, p, c, z):
        return ((h * 4 + p) * 2 + c) * 4 + z

    def send(self, x, route):
        pairs = []
        for i in range(self.n):
            to = route(*self.split(i))
            if to is not None:
                pairs.append((i, self.join(*to)))
        return jax.tree.map(lambda a: lax.ppermute(a, AXES, pairs), x)

    def one(self, x):
        return self.send(x, lambda h, p, c, z: (h, p ^ (1 + c), c, z))

    def two(self, x):
        return self.send(x, lambda h, p, c, z: (h, p ^ (2 - c), c, z))

    def flip_p(self, x, bit):
        return self.send(x, lambda h, p, c, z: (h, p ^ bit, c, z))

    def flip_z(self, x, bit):
        return self.send(x, lambda h, p, c, z: (h, p, c, z ^ bit))

    def core(self, x):
        return self.send(x, lambda h, p, c, z: (h, p, 1 - c, z))

    def along_z(self, x, by=1):
        return self.send(x, lambda h, p, c, z: (h, p, c, (z + by) % 4))

    def along_h(self, x):
        return self.send(x, lambda h, p, c, z: ((h + 1) % self.high, p, c, z))

    def turn(self, x):
        return self.send(x, lambda h, p, c, z: (h, z, c, p))

    def next_rows(self, x):
        def route(*at):
            i = self.join(*at) + 1
            return self.split(i) if i < self.n else None

        return self.send(x, route)

    def back_rows(self, x):
        def route(h, p, c, z):
            i = (c * 4 + z + 7) % 8
            return h, p, i // 4, i % 4

        return self.send(x, route)

    def back_high(self, x):
        return self.send(x, lambda h, p, c, z: (h - 1, p, c, z) if h else None)

    def gather_rows(self, x):
        first = self.one(x)
        second = self.two(x)
        return x, first, second, self.two(first)

    def scatter_rows(self, parts):
        far = self.two(parts[3]().astype(bf16))
        side = self.two(parts[2]().astype(bf16))
        near = self.one((parts[1]() + far.astype(f32)).astype(bf16))
        return parts[0]() + side.astype(f32) + near.astype(f32)

    def gather_high(self, x):
        held = [x]
        for _ in range(self.high - 1):
            held.append(self.along_h(held[-1]))
        return jnp.concatenate(held, axis=0) if len(held) > 1 else x

    def gather_column(self, x):
        x = self.gather_high(x)
        held = [x]
        for _ in range(3):
            held.append(self.along_z(held[-1]))
        return held, [self.core(a) for a in held]

    def scatter_high(self, x):
        if self.high == 1:
            return x
        rows = x.shape[0] // self.high
        piece = [x[k * rows : (k + 1) * rows] for k in range(self.high)]
        total = piece[1]
        for k in range(1, self.high):
            total = self.along_h(total.astype(bf16)).astype(f32) + piece[(k + 1) % self.high]
        return total

    def scatter_column(self, own, other):
        came = self.core(other)
        total = own(1).astype(f32) + came[1].astype(f32)
        for k in (2, 3, 0):
            total = (
                self.along_z(total.astype(bf16)).astype(f32)
                + own(k).astype(f32)
                + came[k].astype(f32)
            )
        return total

    def sum_plane(self, x):
        x = x + self.core(x)
        x = x + self.flip_p(x, 1)
        return x + self.flip_p(x, 2)

    def sum_all(self, x):
        x = self.sum_plane(x)
        x = x + self.flip_z(x, 1)
        x = x + self.flip_z(x, 2)
        total = x
        for _ in range(self.high - 1):
            x = self.along_h(x)
            total = total + x
        return total

    def sum_high(self, x):
        total = x
        for _ in range(self.high - 1):
            x = self.along_h(x)
            total = total + x
        return total


def swapped(offset):
    return (offset & 1) * 2 + offset // 2


def place_rows(info, chunk, first, shape):
    spot = info[chunk, 0] + first + lax.broadcasted_iota(jnp.int32, shape, 0)
    begin = jnp.zeros(shape, jnp.int32)
    for border in (1, 2, 3):
        begin = jnp.where(spot >= info[chunk, border], info[chunk, border], begin)
    return spot - begin, (spot >= 0) & (spot < info[chunk, 4])


def less_one(y):
    series = 1.0 + y * (1.0 / 6.0)
    for k in (5.0, 4.0, 3.0, 2.0):
        series = 1.0 + y * (1.0 / k) * series
    return jnp.where(y > -0.25, -y * series, 1.0 - jnp.exp(y))


def sigmoid(v):
    return 1.0 / (1.0 + jnp.exp(-v))


def scan_rows(a, b, back):
    rows = lax.broadcasted_iota(jnp.int32, a.shape, 0)
    count = a.shape[0]
    step = 1
    while step < count:
        by = count - step if back else step
        keep = rows < count - step if back else rows >= step
        b = jnp.where(keep, a * pltpu.roll(b, by, 0) + b, b)
        a = jnp.where(keep, a * pltpu.roll(a, by, 0), a)
        step *= 2
    return a, b


def forward_kernel(info, chan, rim, vec, dense, low, dec, state, reach, ext, pre):
    chunk = pl.program_id(0)
    rows, width = chan.shape[1:]
    ext[:TILE] = rim[0].astype(f32)
    ext[TILE:] = chan[0].astype(f32)

    def conv(t, _):
        base = pl.multiple_of(t * TILE, TILE)
        near = ext[pl.ds(base, 2 * TILE), :]
        seg, _filled = place_rows(info, chunk, base, (TILE, width))
        total = jnp.broadcast_to(vec[CONV_BIAS : CONV_BIAS + 1, :], (TILE, width))
        for lag in range(TAPS):
            moved = near[TILE - lag : 2 * TILE - lag]
            tap = vec[TAP_ROW + lag : TAP_ROW + lag + 1, :]
            total = total + jnp.where(seg >= lag, tap * moved, 0.0)
        low[0, pl.ds(base, TILE), :] = total.astype(bf16)
        return 0

    lax.fori_loop(0, rows // TILE, conv, 0)
    pre[...] = trailing(low[0], dense[...])

    def tile(t, held):
        base = pl.multiple_of(t * TILE, TILE)
        span = pl.ds(base, TILE)
        seg, filled = place_rows(info, chunk, base, (TILE, width))
        open_decay = sigmoid(pre[span, :width] + vec[DECAY_BIAS : DECAY_BIAS + 1, :])
        open_input = sigmoid(pre[span, width:] + vec[INPUT_BIAS : INPUT_BIAS + 1, :])
        log_decay = open_decay * vec[SLOPE : SLOPE + 1, :]
        decay = jnp.where((seg != 0) & filled, jnp.exp(log_decay), 0.0)
        factor = jnp.where(seg == 0, 1.0, jnp.sqrt(less_one(2.0 * log_decay)))
        drive = jnp.where(filled, factor * open_input * low[0, span, :].astype(f32), 0.0)
        dec[0, span, :] = decay
        entered, passed = held
        for half in range(TILE // 8):
            part = slice(half * 8, half * 8 + 8)
            a, b = scan_rows(decay[part], drive[part], False)
            b = b + a * entered
            a = a * passed
            at = pl.ds(pl.multiple_of(base + half * 8, 8), 8)
            state[0, at, :] = b
            reach[0, at, :] = a
            entered, passed = b[7:8], a[7:8]
        return entered, passed

    lax.fori_loop(
        0, rows // TILE, tile, (jnp.zeros((1, width), f32), jnp.ones((1, width), f32))
    )


def reverse_kernel(dec, grad, moved, reach):
    rows, width = dec.shape[1:]

    def tile(t, held):
        base = pl.multiple_of(rows - TILE - t * TILE, TILE)
        span = pl.ds(base, TILE)
        decay = dec[0, span, :]
        drive = decay * grad[0, span, :].astype(f32)
        entered, passed = held
        for half in reversed(range(TILE // 8)):
            part = slice(half * 8, half * 8 + 8)
            a, b = scan_rows(decay[part], drive[part], True)
            b = b + a * entered
            a = a * passed
            at = pl.ds(pl.multiple_of(base + half * 8, 8), 8)
            moved[0, at, :] = b
            reach[0, at, :] = a
            entered, passed = b[0:1], a[0:1]
        return entered, passed

    lax.fori_loop(
        0, rows // TILE, tile, (jnp.zeros((1, width), f32), jnp.ones((1, width), f32))
    )


def chain_kernel(back, spot, parts, own, total, every):
    p, c, z = spot[0], spot[1], spot[2]
    factor = jnp.ones((1, own.shape[-1]), f32)
    term = jnp.zeros((1, own.shape[-1]), f32)
    count = 8 * QUARTERS
    for i in reversed(range(count)) if back else range(count):
        j, cc, zz = i // 8, i // 4 % 2, i % 4
        every[i, 0:1, :] = factor
        every[i, 1:2, :] = term
        offset = j ^ p
        slot = swapped(offset) if cc else offset
        pair = parts[(z - zz + 4) % 4, c ^ cc, slot]
        term = pair[0:1] * term + pair[1:2]
        factor = pair[0:1] * factor
    total[0:1, :] = factor
    total[1:2, :] = term
    for r in range(QUARTERS):
        j = p ^ jnp.where(c == 0, r, (r & 1) * 2 + r // 2)
        own[r] = every[(j * 2 + c) * 4 + z]


def backward_kernel(
    info, chan, rim, vec, dense, low, state, reach, enter, grad, moved, span_back, leave,
    gates, chan_grad, rim_grad, sums,
    ext, pre, past, later, conv_grad,
):
    chunk = pl.program_id(0)
    rows, width = chan.shape[1:]
    ext[:TILE] = rim[0].astype(f32)
    ext[TILE:] = chan[0].astype(f32)
    pre[...] = trailing(low[0], dense[...])
    past[0:TILE] = jnp.broadcast_to(enter[0], (TILE, width))
    later[rows : rows + TILE] = jnp.broadcast_to(leave[0], (TILE, width))
    conv_grad[:TILE] = jnp.zeros((TILE, width), f32)
    conv_grad[rows + TILE :] = jnp.zeros((TILE, width), f32)

    @pl.when(chunk == 0)
    def _():
        sums[...] = jnp.zeros_like(sums)

    def fill(t, _):
        base = pl.multiple_of(t * TILE, TILE)
        span = pl.ds(base, TILE)
        past[pl.ds(pl.multiple_of(base + TILE, TILE), TILE), :] = (
            state[0, span, :] + reach[0, span, :] * enter[0]
        )
        later[span, :] = moved[0, span, :] + span_back[0, span, :] * leave[0]
        return 0

    lax.fori_loop(0, rows // TILE, fill, 0)

    def add(row, value):
        sums[row : row + 1, :] += jnp.sum(value, axis=0, keepdims=True)

    def tile(t, _):
        base = pl.multiple_of(t * TILE, TILE)
        span = pl.ds(base, TILE)
        seg, filled = place_rows(info, chunk, base, (TILE, width))
        restart = seg == 0
        before = past[pl.ds(base, 2 * TILE), :][TILE - 1 : 2 * TILE - 1]
        adjoint = grad[0, span, :].astype(f32) + later[pl.ds(base, 2 * TILE), :][1 : TILE + 1]
        open_decay = sigmoid(pre[span, :width] + vec[DECAY_BIAS : DECAY_BIAS + 1, :])
        open_input = sigmoid(pre[span, width:] + vec[INPUT_BIAS : INPUT_BIAS + 1, :])
        slope = vec[SLOPE : SLOPE + 1, :]
        log_decay = open_decay * slope
        decay = jnp.exp(log_decay)
        square = less_one(2.0 * log_decay)
        value = low[0, span, :].astype(f32)
        root = lax.rsqrt(square)
        factor = jnp.where(restart, 1.0, square * root)
        factor = jnp.where(square == 0.0, jnp.where(restart, 1.0, 0.0), factor)
        opened = jnp.where(filled, open_input * adjoint, 0.0)
        direct = factor * opened
        input_grad = direct * value * (1.0 - open_input)
        log_grad = jnp.where(restart | ~filled, 0.0, adjoint * before * decay) - jnp.where(
            restart, 0.0, opened * value * decay * decay * root
        )
        decay_grad = log_grad * slope * open_decay * (1.0 - open_decay)
        decay_low = decay_grad.astype(bf16)
        input_low = input_grad.astype(bf16)
        gates[0, span, :width] = decay_low
        gates[0, span, width:] = input_low
        conv_grad[pl.ds(pl.multiple_of(base + TILE, TILE), TILE), :] = direct
        add(0, decay_low.astype(f32))
        add(1, input_low.astype(f32))
        add(2, log_grad * open_decay)
        return 0

    lax.fori_loop(0, rows // TILE, tile, 0)
    conv_grad[TILE : rows + TILE] += plain(gates[0], dense[...])

    def taps(t, _):
        base = pl.multiple_of(t * TILE, TILE)
        near = conv_grad[pl.ds(base, 2 * TILE), :]
        back = jnp.zeros((TILE, width), f32)
        for lag in range(TAPS):
            seg, _filled = place_rows(info, chunk, base - TILE + lag, (TILE, width))
            tap = vec[TAP_ROW + lag : TAP_ROW + lag + 1, :]
            back = back + jnp.where(seg >= lag, tap * near[lag : TILE + lag], 0.0)

        @pl.when(t == 0)
        def _():
            rim_grad[0] = back[TILE - 8 :]

        @pl.when(t > 0)
        def _():
            at = pl.multiple_of(base - TILE, TILE)
            chan_grad[0, pl.ds(at, TILE), :] = back
            around = ext[pl.ds(at, 2 * TILE), :]
            seg, _filled = place_rows(info, chunk, at, (TILE, width))
            own = near[:TILE]
            add(3, own)
            for lag in range(TAPS):
                moved_in = around[TILE - lag : 2 * TILE - lag]
                add(4 + lag, jnp.where(seg >= lag, own * moved_in, 0.0))

        return 0

    lax.fori_loop(0, rows // TILE + 1, taps, 0)


def per_chunk(array):
    shape = array.shape
    return pl.BlockSpec((1, *shape[1:]), lambda i: (i,) + (0,) * (len(shape) - 1))


def whole(array):
    return pl.BlockSpec(array.shape, lambda i: (0,) * len(array.shape))


def in_smem():
    return pl.BlockSpec(memory_space=pltpu.SMEM)


def params():
    return pltpu.CompilerParams(vmem_limit_bytes=VMEM_BYTES)


def run_forward(info, chan, rim, vec, dense):
    count, rows, width = chan.shape
    shape = jax.ShapeDtypeStruct
    outs = [shape(chan.shape, bf16)] + [shape(chan.shape, f32)] * 3
    return pl.pallas_call(
        forward_kernel,
        grid=(count,),
        out_shape=outs,
        in_specs=[in_smem(), per_chunk(chan), per_chunk(rim), whole(vec), whole(dense)],
        out_specs=[per_chunk(o) for o in outs],
        scratch_shapes=[
            pltpu.VMEM((rows + TILE, width), f32),
            pltpu.VMEM((rows, 2 * width), f32),
        ],
        compiler_params=params(),
        cost_estimate=pl.CostEstimate(
            flops=4 * count * rows * width * width,
            bytes_accessed=count * rows * width * 16,
            transcendentals=count * rows * width * 5,
        ),
    )(info, chan, rim, vec, dense)


def run_reverse(dec, grad):
    count, rows, width = dec.shape
    outs = [jax.ShapeDtypeStruct(dec.shape, f32)] * 2
    return pl.pallas_call(
        reverse_kernel,
        grid=(count,),
        out_shape=outs,
        in_specs=[per_chunk(dec), per_chunk(grad)],
        out_specs=[per_chunk(o) for o in outs],
        compiler_params=params(),
        cost_estimate=pl.CostEstimate(
            flops=20 * count * rows * width,
            bytes_accessed=count * rows * width * 14,
            transcendentals=0,
        ),
    )(dec, grad)


def run_chain(spot, parts, back):
    width = parts.shape[-1]
    vmem = pl.BlockSpec(memory_space=pltpu.VMEM)
    return pl.pallas_call(
        partial(chain_kernel, back),
        out_shape=[
            jax.ShapeDtypeStruct((QUARTERS, 2, width), f32),
            jax.ShapeDtypeStruct((2, width), f32),
        ],
        in_specs=[in_smem(), vmem],
        out_specs=[vmem, vmem],
        scratch_shapes=[pltpu.VMEM((8 * QUARTERS, 2, width), f32)],
        compiler_params=params(),
    )(spot, parts)


def run_backward(info, chan, rim, vec, dense, low, state, reach, enter, grad, moved, span, leave):
    count, rows, width = chan.shape
    shape = jax.ShapeDtypeStruct
    outs = [
        shape((count, rows, 2 * width), bf16),
        shape((count, rows, width), f32),
        shape((count, 8, width), f32),
        shape((8, width), f32),
    ]
    cut = [chan, rim, vec, dense, low, state, reach, enter, grad, moved, span, leave]
    specs = [whole(a) if a is vec or a is dense else per_chunk(a) for a in cut]
    return pl.pallas_call(
        backward_kernel,
        grid=(count,),
        out_shape=outs,
        in_specs=[in_smem(), *specs],
        out_specs=[per_chunk(o) for o in outs[:3]] + [whole(outs[3])],
        scratch_shapes=[
            pltpu.VMEM((rows + TILE, width), f32),
            pltpu.VMEM((rows, 2 * width), f32),
            pltpu.VMEM((rows + TILE, width), f32),
            pltpu.VMEM((rows + TILE, width), f32),
            pltpu.VMEM((rows + 2 * TILE, width), f32),
        ],
        compiler_params=params(),
        cost_estimate=pl.CostEstimate(
            flops=8 * count * rows * width * width,
            bytes_accessed=count * rows * width * 32,
            transcendentals=count * rows * width * 6,
        ),
    )(info, *cut)


def laid_kernel(rows, at, *refs):
    count = len(refs) - 2
    pieces, out, sems = refs[:count], refs[count], refs[count + 1]
    each = pieces[0].shape[0] // rows
    copies = []
    for i, piece in enumerate(pieces):
        for k in range(each):
            n = i * each + k
            to = pl.ds(pl.multiple_of(at[n] * rows, rows), rows)
            copies.append(
                pltpu.make_async_copy(piece.at[pl.ds(k * rows, rows)], out.at[to], sems.at[n])
            )
    for copy in copies:
        copy.start()
    for copy in copies:
        copy.wait()


def lay(pieces, at, rows):
    count = at.shape[0]
    width = pieces[0].shape[1]
    anywhere = pl.BlockSpec(memory_space=pl.ANY)
    return pl.pallas_call(
        partial(laid_kernel, rows),
        out_shape=jax.ShapeDtypeStruct((count * rows, width), pieces[0].dtype),
        in_specs=[in_smem(), *[anywhere for _ in pieces]],
        out_specs=anywhere,
        scratch_shapes=[pltpu.SemaphoreType.DMA((count,))],
    )(at, *pieces)


def normed(values):
    rs = lax.rsqrt(jnp.mean(values * values, axis=-1, keepdims=True) + EPS)
    return rs, values * rs


def norm_back(rs, xs, gain, grad):
    scaled = gain * grad
    return rs * (scaled - xs * jnp.mean(xs * scaled, axis=-1, keepdims=True))


def body(
    places,
    tokens,
    cotangent,
    lengths,
    branch_weight,
    mixer_weight,
    branch_bias,
    mixer_bias,
    conv_taps,
    conv_bias,
    decay_weight,
    input_weight,
    decay_bias,
    input_bias,
    decay_param,
    output_weight,
    first_gain,
    second_gain,
    gate_weight,
    up_weight,
    down_weight,
):
    rows, features = tokens.shape
    slab, width = mixer_weight.shape
    block_width = decay_weight.shape[1]
    heads = width // block_width
    high = places.high
    dp_at, z = lax.axis_index("dp"), lax.axis_index("blk")
    h, p, c = dp_at // 8, dp_at // 2 % 4, dp_at % 2
    spot = jnp.stack([p, c, z]).astype(jnp.int32)

    straight = jnp.arange(QUARTERS, dtype=jnp.int32)
    order = p ^ jnp.where(c == 0, straight, (straight & 1) * 2 + straight // 2)
    chunk = ((h * 4 + order) * 2 + c) * 4 + z
    bucket_rows = BUCKET_DP * QUARTERS * rows
    start = chunk * rows
    bucket = (start + bucket_rows // 2) // bucket_rows
    begin = jnp.maximum(0, bucket * bucket_rows - bucket_rows // 2)
    ends = jnp.cumsum(jnp.take(lengths, bucket, axis=0), axis=1)
    info = jnp.concatenate([(start - begin)[:, None], ends], axis=1).astype(jnp.int32)

    inputs = tokens.astype(f32)
    gain_one, gain_two = first_gain.astype(f32), second_gain.astype(f32)
    rs_one, xs_one = normed(inputs)
    low_one = (xs_one * gain_one).astype(bf16)
    rim_rows = places.next_rows(low_one[rows - TILE :])

    def quarter(piece):
        own, other = places.gather_column(places.turn(piece))
        back = jnp.arange(high, dtype=jnp.int32)
        at = []
        for core in (c, 1 - c):
            for k in range(4):
                at.append((((h - back + high) % high) * 4 + (z - k + 4) % 4) * 2 + core)
        return lay([*own, *other], jnp.concatenate(at), slab)

    packed = jnp.concatenate(
        [
            jnp.stack([branch_bias, mixer_bias]),
            conv_taps.T,
            jnp.stack([conv_bias, decay_bias, input_bias, decay_param]),
            jnp.zeros((6, width), bf16),
        ],
        axis=0,
    )
    gate_flat = jnp.concatenate([decay_weight.T, input_weight.T], axis=0)
    mixer_own = quarter(mixer_weight)
    vectors = places.turn(packed).astype(f32)
    low_rows = jnp.stack(places.gather_rows(low_one)).reshape(QUARTERS * rows, features)
    rim_low = jnp.stack(places.gather_rows(rim_rows)).reshape(QUARTERS * TILE, features)
    gate_turned = places.turn(gate_flat)
    branch_own = quarter(branch_weight)
    output_own = quarter(output_weight.T)

    param = vectors[PARAM]
    vec = jnp.concatenate(
        [vectors[:SLOPE], -DECAY * jax.nn.softplus(-param)[None], vectors[SLOPE + 1 :]], axis=0
    )
    block_of = jnp.arange(width, dtype=jnp.int32) // block_width
    same = block_of[:, None] == block_of[None, :]
    dense = jnp.concatenate(
        [
            jnp.where(same, jnp.tile(gate_turned[:block_width], (heads, 1)), 0),
            jnp.where(same, jnp.tile(gate_turned[block_width:], (heads, 1)), 0),
        ],
        axis=0,
    ).astype(bf16)

    gate_col = places.gather_column(gate_weight.T)
    up_col = places.gather_column(up_weight.T)
    down_col = places.gather_column(down_weight)
    gate_use, up_use, down_use = (
        jnp.concatenate([*own, *other], axis=0) for own, other in (gate_col, up_col, down_col)
    )
    feed_grad = jnp.stack(places.gather_rows(cotangent)).reshape(QUARTERS * rows, features)

    channels = (plain(low_rows, mixer_own) + vec[MIXER_BIAS]).astype(bf16)
    rim = (plain(rim_low, mixer_own) + vec[MIXER_BIAS]).astype(bf16)
    channels = channels.reshape(QUARTERS, rows, width)
    rim = rim.reshape(QUARTERS, TILE, width)
    conv_low, decays, state_local, reach = run_forward(info, channels, rim, vec, dense)
    branch_pre = plain(low_rows, branch_own) + vec[BRANCH_BIAS]

    def entering(parts, back):
        pair = jnp.stack([parts, places.core(parts)])
        every = jnp.stack([pair] + [places.along_z(pair, k) for k in (1, 2, 3)])
        own, total = run_chain(spot, every, back)
        if high == 1:
            return own[:, 1:2]
        held = [total]
        for _ in range(high - 1):
            held.append(places.along_h(held[-1]))
        state = jnp.zeros((1, width), f32)
        for hop in range(high - 1):
            source = high - 1 - hop if back else hop
            far = (h - source + high) % high
            picked = lax.dynamic_index_in_dim(jnp.stack(held), far, 0, False)
            ahead = source > h if back else source < h
            state = jnp.where(ahead, picked[0:1] * state + picked[1:2], state)
        return own[:, 1:2] + own[:, 0:1] * state[None]

    enter = entering(jnp.stack([reach[:, -1], state_local[:, -1]], axis=1), False)
    branch_act, gelu_back_one = jax.vjp(jax.nn.gelu, branch_pre)
    state_low = (state_local + reach * enter).astype(bf16).reshape(QUARTERS * rows, width)
    mixed_low = (branch_act * state_low.astype(f32)).astype(bf16)

    def rows_of(array, k):
        return array[k * rows : (k + 1) * rows]

    resid = inputs + places.scatter_rows(
        [lambda k=k: trailing(rows_of(mixed_low, k), output_own) for k in range(QUARTERS)]
    )

    rs_two, xs_two = normed(resid)
    low_two = (xs_two * gain_two).astype(bf16)
    feed_rows = jnp.stack(places.gather_rows(low_two)).reshape(QUARTERS * rows, features)
    gate_pre = trailing(feed_rows, gate_use)
    up_pre = trailing(feed_rows, up_use)
    gate_act, gelu_back_two = jax.vjp(jax.nn.gelu, gate_pre)
    hidden = (gate_act * up_pre).astype(bf16)
    hidden_grad = trailing(feed_grad, down_use)
    gate_grad = gelu_back_two(hidden_grad * up_pre)[0].astype(bf16)
    up_grad = (hidden_grad * gate_act).astype(bf16)
    norm_grad = places.scatter_rows(
        [
            lambda k=k: plain(rows_of(gate_grad, k), gate_use) + plain(rows_of(up_grad, k), up_use)
            for k in range(QUARTERS)
        ]
    )

    def column_sum(term):
        term = term.astype(bf16).reshape(2, 4, -1, features)
        return places.scatter_high(places.scatter_column(lambda k: term[0, k], term[1]))

    down_sum = column_sum(leading(hidden, feed_grad))
    gate_sum = column_sum(leading(gate_grad, feed_rows)).T
    up_sum = column_sum(leading(up_grad, feed_rows)).T
    second_term = jnp.sum(norm_grad * xs_two, axis=0)
    resid_grad = cotangent.astype(f32) + norm_back(rs_two, xs_two, gain_two, norm_grad)

    resid_rows = jnp.stack(places.gather_rows(resid_grad.astype(bf16)))
    resid_rows = resid_rows.reshape(QUARTERS * rows, features)
    mixed_grad = plain(resid_rows, output_own)
    state_grad = (mixed_grad * branch_act).astype(bf16).reshape(QUARTERS, rows, width)
    branch_grad = gelu_back_one(mixed_grad * state_low.astype(f32))[0].astype(bf16)
    moved, span_back = run_reverse(decays, state_grad)
    leave = entering(jnp.stack([span_back[:, 0], moved[:, 0]], axis=1), True)
    gates, chan_grad, rim_grad, sums = run_backward(
        info, channels, rim, vec, dense, conv_low, state_local, reach, enter, state_grad, moved,
        span_back, leave,
    )

    came = places.back_rows(rim_grad)
    last = (c == 1) & (z == 3)
    wanted = order + jnp.where(last, 1, 0)
    from_core = jnp.where(z == 3, 1 - c, c)
    offset = (wanted % 4) ^ p
    slot = jnp.where(from_core == 0, offset, (offset & 1) * 2 + offset // 2)
    pick = (slot[:, None] == straight[None, :]).astype(f32)
    here = jnp.where(wanted < 4, 1.0, 0.0)[:, None]

    def picked(select, array):
        return jnp.sum(select[:, :, None, None] * array[None], axis=1)

    returned = picked(pick * here, came)
    if high > 1:
        returned = returned + picked(pick * (1.0 - here), places.back_high(came))
    chan_grad = chan_grad + jnp.pad(returned, ((0, 0), (rows - 8, 0), (0, 0)))
    mixer_grad = chan_grad.astype(bf16).reshape(QUARTERS * rows, width)

    branch_term = leading(low_rows, branch_grad)
    mixer_term = leading(low_rows, mixer_grad)
    output_term = leading(resid_rows, mixed_low)

    def quarter_sum(term):
        term = term.astype(bf16).reshape(high, 4, 2, slab, width)
        own = lax.dynamic_index_in_dim(term, c, 2, False)
        other = lax.dynamic_index_in_dim(term, 1 - c, 2, False)

        def by(array, k):
            return lax.dynamic_index_in_dim(array, (z - k + 4) % 4, 1, False)

        came_over = places.core(other)
        total = by(own, 1).astype(f32) + by(came_over, 1).astype(f32)
        for k in (2, 3, 0):
            total = (
                places.along_z(total.astype(bf16)).astype(f32)
                + by(own, k).astype(f32)
                + by(came_over, k).astype(f32)
            )
        if high > 1:
            back = (h - jnp.arange(high)) % high
            total = places.scatter_high(
                jnp.take(total, back, axis=0).reshape(high * slab, width)
            )
        return places.turn(total.astype(bf16).reshape(slab, width)).astype(f32)

    output_sum = quarter_sum(output_term).T
    branch_sum = quarter_sum(branch_term)
    mixer_sum = quarter_sum(mixer_term)

    low_grad = places.scatter_rows(
        [
            lambda k=k: trailing(rows_of(branch_grad, k), branch_own)
            + trailing(rows_of(mixer_grad, k), mixer_own)
            for k in range(QUARTERS)
        ]
    )
    token_grad = (resid_grad + norm_back(rs_one, xs_one, gain_one, low_grad)).astype(bf16)

    first_term = (
        jnp.sum(branch_term * branch_own.astype(f32), axis=1)
        + jnp.sum(mixer_term * mixer_own.astype(f32), axis=1)
    ) / gain_one
    gain_sums = places.sum_all(jnp.stack([first_term, second_term]))

    crossed = leading(gates.reshape(QUARTERS * rows, 2 * width), conv_low.reshape(-1, width))
    picked_blocks = block_of[None, :] == jnp.arange(heads)[:, None]
    gate_terms = jnp.sum(
        jnp.where(picked_blocks[None, :, None, :], crossed.reshape(2, heads, block_width, width), 0),
        axis=1,
    ).astype(bf16)
    vector_terms = jnp.concatenate(
        [
            sums,
            jnp.sum(branch_grad.astype(f32), axis=0)[None],
            jnp.sum(mixer_grad.astype(f32), axis=0)[None],
            jnp.zeros((6, width), f32),
        ],
        axis=0,
    )
    slope_back = DECAY * jax.nn.sigmoid(-param)
    vector_terms = vector_terms.at[2].multiply(slope_back)
    gate_total = places.sum_high(
        places.sum_plane(places.turn(gate_terms.reshape(2 * block_width, width)))
    ).astype(f32)
    vector_total = places.sum_high(places.sum_plane(places.turn(vector_terms)))
    return (
        (resid + feed_part(places, hidden, down_use, rows)).astype(bf16),
        token_grad,
        branch_sum,
        mixer_sum,
        vector_total[8],
        vector_total[9],
        vector_total[4:8].T,
        vector_total[3],
        gate_total[:block_width].T,
        gate_total[block_width:].T,
        vector_total[0],
        vector_total[1],
        vector_total[2],
        output_sum,
        gain_sums[0],
        gain_sums[1],
        gate_sum,
        up_sum,
        down_sum,
    )


def feed_part(places, hidden, down_use, rows):
    return places.scatter_rows(
        [
            lambda k=k: plain(hidden[k * rows : (k + 1) * rows], down_use)
            for k in range(QUARTERS)
        ]
    )


def solution(mesh):
    places = Places(mesh.shape["dp"], mesh.shape["blk"])
    return jax.shard_map(
        partial(body, places),
        mesh=mesh,
        in_specs=(
            P(("dp", "blk"), None),
            P(("dp", "blk"), None),
            P(),
            P("dp", "blk"),
            P("dp", "blk"),
            P("blk"),
            P("blk"),
            P("blk", None),
            P("blk"),
            P("blk", None),
            P("blk", None),
            P("blk"),
            P("blk"),
            P("blk"),
            P("blk", "dp"),
            P(),
            P(),
            P(None, ("dp", "blk")),
            P(None, ("dp", "blk")),
            P(("dp", "blk"), None),
        ),
        out_specs=(
            P(("dp", "blk"), None),
            P(("dp", "blk"), None),
            P("dp", "blk"),
            P("dp", "blk"),
            P("blk"),
            P("blk"),
            P("blk", None),
            P("blk"),
            P("blk", None),
            P("blk", None),
            P("blk"),
            P("blk"),
            P("blk"),
            P("blk", "dp"),
            P(),
            P(),
            P(None, ("dp", "blk")),
            P(None, ("dp", "blk")),
            P(("dp", "blk"), None),
        ),
        check_vma=False,
    )
```

```python
from functools import partial

import jax
import jax.numpy as jnp
from jax import lax
from jax.experimental import pallas as pl
from jax.experimental.pallas import tpu as pltpu
from jax.sharding import PartitionSpec as P

BUCKET_DP = 4
EPS = 1e-06
DECAY = 8.0
TAPS = 4
QUARTERS = 4
TILE = 16
AXES = ("dp", "blk")
f32 = jnp.float32
bf16 = jnp.bfloat16
VMEM_BYTES = 40 * 2**20

BRANCH_BIAS, MIXER_BIAS, TAP_ROW, CONV_BIAS, DECAY_BIAS, INPUT_BIAS, PARAM = 0, 1, 2, 6, 7, 8, 9
SLOPE = 10


def plain(former, latter):
    return jnp.dot(former, latter, preferred_element_type=f32)


def trailing(former, latter):
    return lax.dot_general(former, latter, (((1,), (1,)), ((), ())), preferred_element_type=f32)


def leading(former, latter):
    return lax.dot_general(former, latter, (((0,), (0,)), ((), ())), preferred_element_type=f32)


class Places:
    def __init__(self, dp, blk):
        assert blk == QUARTERS and dp % (2 * QUARTERS) == 0
        self.n = dp * blk
        self.high = dp // (2 * QUARTERS)

    @staticmethod
    def split(i):
        return i // 32, i // 8 % 4, i // 4 % 2, i % 4

    @staticmethod
    def join(h, p, c, z):
        return ((h * 4 + p) * 2 + c) * 4 + z

    def send(self, x, route):
        pairs = []
        for i in range(self.n):
            to = route(*self.split(i))
            if to is not None:
                pairs.append((i, self.join(*to)))
        return jax.tree.map(lambda a: lax.ppermute(a, AXES, pairs), x)

    def one(self, x):
        return self.send(x, lambda h, p, c, z: (h, p ^ (1 + c), c, z))

    def two(self, x):
        return self.send(x, lambda h, p, c, z: (h, p ^ (2 - c), c, z))

    def flip_p(self, x, bit):
        return x if bit == 0 else self.send(x, lambda h, p, c, z: (h, p ^ bit, c, z))

    def flip_z(self, x, bit):
        return self.send(x, lambda h, p, c, z: (h, p, c, z ^ bit))

    def core(self, x):
        return self.send(x, lambda h, p, c, z: (h, p, 1 - c, z))

    def along_z(self, x, by=1):
        return self.send(x, lambda h, p, c, z: (h, p, c, (z + by) % 4))

    def along_h(self, x):
        return self.send(x, lambda h, p, c, z: ((h + 1) % self.high, p, c, z))

    def next_rows(self, x):
        def route(*at):
            i = self.join(*at) + 1
            return self.split(i) if i < self.n else None

        return self.send(x, route)

    def back_rows(self, x):
        def route(h, p, c, z):
            i = (c * 4 + z + 7) % 8
            return h, p, i // 4, i % 4

        return self.send(x, route)

    def back_high(self, x):
        return self.send(x, lambda h, p, c, z: (h - 1, p, c, z) if h else None)

    def gather_rows(self, x):
        first = self.one(x)
        second = self.two(x)
        return x, first, second, self.two(first)

    def gather_rows_direct(self, x):
        return x, self.one(x), self.two(x), self.flip_p(x, 3)

    def scatter_rows(self, parts):
        far = self.two(parts[3].astype(bf16))
        side = self.two(parts[2].astype(bf16))
        joined = (parts[1] + far.astype(f32)).astype(bf16)
        return parts[0] + side.astype(f32) + self.one(joined).astype(f32), joined

    def spread(self, x, p):
        groups = [
            [self.join(h, q, c, z) for h in range(self.high) for z in range(4)]
            for q in range(QUARTERS)
            for c in range(2)
        ]
        every = lax.all_gather(x, AXES, axis_index_groups=groups, axis=0, tiled=True)
        slab, width = x.shape

        def pick(m):
            if self.high == 1:
                return lax.dynamic_slice_in_dim(every, (p ^ m) * slab, slab, 0)[None]
            return lax.dynamic_index_in_dim(
                every.reshape(self.high, 4, slab, width), p ^ m, 1, False
            )

        own = [self.flip_p(pick(m), m) for m in range(4)]
        return every, [own, [self.core(a) for a in own]]

    def gather_rest(self, x, axis=0):
        groups = [
            [self.join(h, p, c, z) for c in range(2) for z in range(4) for h in range(self.high)]
            for p in range(QUARTERS)
        ]
        return lax.all_gather(x, AXES, axis_index_groups=groups, axis=axis, tiled=True)

    def scatter_high(self, x):
        if self.high == 1:
            return x
        rows = x.shape[0] // self.high
        piece = [x[k * rows : (k + 1) * rows] for k in range(self.high)]
        total = piece[1]
        for k in range(1, self.high):
            total = self.along_h(total.astype(bf16)).astype(f32) + piece[(k + 1) % self.high]
        return total

    def sum_all(self, x):
        x = x + self.core(x)
        x = x + self.flip_p(x, 1)
        x = x + self.flip_p(x, 2)
        x = x + self.flip_z(x, 1)
        x = x + self.flip_z(x, 2)
        total = x
        for _ in range(self.high - 1):
            x = self.along_h(x)
            total = total + x
        return total


def after(x, *others):
    return lax.optimization_barrier((x, *others))[0]


def swapped(offset):
    return (offset & 1) * 2 + offset // 2


def place_rows(info, chunk, first, shape):
    spot = info[chunk, 0] + first + lax.broadcasted_iota(jnp.int32, shape, 0)
    begin = jnp.zeros(shape, jnp.int32)
    for border in (1, 2, 3):
        begin = jnp.where(spot >= info[chunk, border], info[chunk, border], begin)
    return spot - begin, (spot >= 0) & (spot < info[chunk, 4])


def less_one(y):
    series = 1.0 + y * (1.0 / 6.0)
    for k in (5.0, 4.0, 3.0, 2.0):
        series = 1.0 + y * (1.0 / k) * series
    return jnp.where(y > -0.25, -y * series, 1.0 - jnp.exp(y))


def sigmoid(v):
    return 1.0 / (1.0 + jnp.exp(-v))


def scan_rows(a, b, back):
    rows = lax.broadcasted_iota(jnp.int32, a.shape, 0)
    count = a.shape[0]
    step = 1
    while step < count:
        by = count - step if back else step
        keep = rows < count - step if back else rows >= step
        b = jnp.where(keep, a * pltpu.roll(b, by, 0) + b, b)
        a = jnp.where(keep, a * pltpu.roll(a, by, 0), a)
        step *= 2
    return a, b


def forward_kernel(info, chan, rim, vec, dense, low, dec, state, reach, ext, pre):
    chunk = pl.program_id(0)
    rows, width = chan.shape[1:]
    ext[:TILE] = rim[0].astype(f32)
    ext[TILE:] = chan[0].astype(f32)

    def conv(t, _):
        base = pl.multiple_of(t * TILE, TILE)
        near = ext[pl.ds(base, 2 * TILE), :]
        seg, _filled = place_rows(info, chunk, base, (TILE, width))
        total = jnp.broadcast_to(vec[CONV_BIAS : CONV_BIAS + 1, :], (TILE, width))
        for lag in range(TAPS):
            moved = near[TILE - lag : 2 * TILE - lag]
            tap = vec[TAP_ROW + lag : TAP_ROW + lag + 1, :]
            total = total + jnp.where(seg >= lag, tap * moved, 0.0)
        low[0, pl.ds(base, TILE), :] = total.astype(bf16)
        return 0

    lax.fori_loop(0, rows // TILE, conv, 0)
    pre[...] = trailing(low[0], dense[...])

    def tile(t, held):
        base = pl.multiple_of(t * TILE, TILE)
        span = pl.ds(base, TILE)
        seg, filled = place_rows(info, chunk, base, (TILE, width))
        open_decay = sigmoid(pre[span, :width] + vec[DECAY_BIAS : DECAY_BIAS + 1, :])
        open_input = sigmoid(pre[span, width:] + vec[INPUT_BIAS : INPUT_BIAS + 1, :])
        log_decay = open_decay * vec[SLOPE : SLOPE + 1, :]
        decay = jnp.where((seg != 0) & filled, jnp.exp(log_decay), 0.0)
        factor = jnp.where(seg == 0, 1.0, jnp.sqrt(less_one(2.0 * log_decay)))
        drive = jnp.where(filled, factor * open_input * low[0, span, :].astype(f32), 0.0)
        dec[0, span, :] = decay
        entered, passed = held
        for half in range(TILE // 8):
            part = slice(half * 8, half * 8 + 8)
            a, b = scan_rows(decay[part], drive[part], False)
            b = b + a * entered
            a = a * passed
            at = pl.ds(pl.multiple_of(base + half * 8, 8), 8)
            state[0, at, :] = b
            reach[0, at, :] = a
            entered, passed = b[7:8], a[7:8]
        return entered, passed

    lax.fori_loop(
        0, rows // TILE, tile, (jnp.zeros((1, width), f32), jnp.ones((1, width), f32))
    )


def reverse_kernel(dec, grad, moved, reach):
    rows, width = dec.shape[1:]

    def tile(t, held):
        base = pl.multiple_of(rows - TILE - t * TILE, TILE)
        span = pl.ds(base, TILE)
        decay = dec[0, span, :]
        drive = decay * grad[0, span, :].astype(f32)
        entered, passed = held
        for half in reversed(range(TILE // 8)):
            part = slice(half * 8, half * 8 + 8)
            a, b = scan_rows(decay[part], drive[part], True)
            b = b + a * entered
            a = a * passed
            at = pl.ds(pl.multiple_of(base + half * 8, 8), 8)
            moved[0, at, :] = b
            reach[0, at, :] = a
            entered, passed = b[0:1], a[0:1]
        return entered, passed

    lax.fori_loop(
        0, rows // TILE, tile, (jnp.zeros((1, width), f32), jnp.ones((1, width), f32))
    )


def chain_kernel(back, spot, parts, own, total, every):
    p, c, z = spot[0], spot[1], spot[2]
    factor = jnp.ones((1, own.shape[-1]), f32)
    term = jnp.zeros((1, own.shape[-1]), f32)
    count = 8 * QUARTERS
    for i in reversed(range(count)) if back else range(count):
        j, cc, zz = i // 8, i // 4 % 2, i % 4
        every[i, 0:1, :] = factor
        every[i, 1:2, :] = term
        offset = j ^ p
        slot = swapped(offset) if cc else offset
        pair = parts[(z - zz + 4) % 4, c ^ cc, slot]
        term = pair[0:1] * term + pair[1:2]
        factor = pair[0:1] * factor
    total[0:1, :] = factor
    total[1:2, :] = term
    for r in range(QUARTERS):
        j = p ^ jnp.where(c == 0, r, (r & 1) * 2 + r // 2)
        own[r] = every[(j * 2 + c) * 4 + z]


def backward_kernel(
    info, chan, rim, vec, dense, low, state, reach, enter, grad, moved, span_back, leave,
    gates, chan_grad, rim_grad, sums,
    ext, pre, past, later, conv_grad,
):
    chunk = pl.program_id(0)
    rows, width = chan.shape[1:]
    ext[:TILE] = rim[0].astype(f32)
    ext[TILE:] = chan[0].astype(f32)
    pre[...] = trailing(low[0], dense[...])
    past[0:TILE] = jnp.broadcast_to(enter[0], (TILE, width))
    later[rows : rows + TILE] = jnp.broadcast_to(leave[0], (TILE, width))
    conv_grad[:TILE] = jnp.zeros((TILE, width), f32)
    conv_grad[rows + TILE :] = jnp.zeros((TILE, width), f32)

    @pl.when(chunk == 0)
    def _():
        sums[...] = jnp.zeros_like(sums)

    def fill(t, _):
        base = pl.multiple_of(t * TILE, TILE)
        span = pl.ds(base, TILE)
        past[pl.ds(pl.multiple_of(base + TILE, TILE), TILE), :] = (
            state[0, span, :] + reach[0, span, :] * enter[0]
        )
        later[span, :] = moved[0, span, :] + span_back[0, span, :] * leave[0]
        return 0

    lax.fori_loop(0, rows // TILE, fill, 0)

    def add(row, value):
        sums[row : row + 1, :] += jnp.sum(value, axis=0, keepdims=True)

    def tile(t, _):
        base = pl.multiple_of(t * TILE, TILE)
        span = pl.ds(base, TILE)
        seg, filled = place_rows(info, chunk, base, (TILE, width))
        restart = seg == 0
        before = past[pl.ds(base, 2 * TILE), :][TILE - 1 : 2 * TILE - 1]
        adjoint = grad[0, span, :].astype(f32) + later[pl.ds(base, 2 * TILE), :][1 : TILE + 1]
        open_decay = sigmoid(pre[span, :width] + vec[DECAY_BIAS : DECAY_BIAS + 1, :])
        open_input = sigmoid(pre[span, width:] + vec[INPUT_BIAS : INPUT_BIAS + 1, :])
        slope = vec[SLOPE : SLOPE + 1, :]
        log_decay = open_decay * slope
        decay = jnp.exp(log_decay)
        square = less_one(2.0 * log_decay)
        value = low[0, span, :].astype(f32)
        root = lax.rsqrt(square)
        factor = jnp.where(restart, 1.0, square * root)
        factor = jnp.where(square == 0.0, jnp.where(restart, 1.0, 0.0), factor)
        opened = jnp.where(filled, open_input * adjoint, 0.0)
        direct = factor * opened
        input_grad = direct * value * (1.0 - open_input)
        log_grad = jnp.where(restart | ~filled, 0.0, adjoint * before * decay) - jnp.where(
            restart, 0.0, opened * value * decay * decay * root
        )
        decay_grad = log_grad * slope * open_decay * (1.0 - open_decay)
        decay_low = decay_grad.astype(bf16)
        input_low = input_grad.astype(bf16)
        gates[0, span, :width] = decay_low
        gates[0, span, width:] = input_low
        conv_grad[pl.ds(pl.multiple_of(base + TILE, TILE), TILE), :] = direct
        add(0, decay_low.astype(f32))
        add(1, input_low.astype(f32))
        add(2, log_grad * open_decay)
        return 0

    lax.fori_loop(0, rows // TILE, tile, 0)
    conv_grad[TILE : rows + TILE] += plain(gates[0], dense[...])

    def taps(t, _):
        base = pl.multiple_of(t * TILE, TILE)
        near = conv_grad[pl.ds(base, 2 * TILE), :]
        back = jnp.zeros((TILE, width), f32)
        for lag in range(TAPS):
            seg, _filled = place_rows(info, chunk, base - TILE + lag, (TILE, width))
            tap = vec[TAP_ROW + lag : TAP_ROW + lag + 1, :]
            back = back + jnp.where(seg >= lag, tap * near[lag : TILE + lag], 0.0)

        @pl.when(t == 0)
        def _():
            rim_grad[0] = back[TILE - 8 :]

        @pl.when(t > 0)
        def _():
            at = pl.multiple_of(base - TILE, TILE)
            chan_grad[0, pl.ds(at, TILE), :] = back
            around = ext[pl.ds(at, 2 * TILE), :]
            seg, _filled = place_rows(info, chunk, at, (TILE, width))
            own = near[:TILE]
            add(3, own)
            for lag in range(TAPS):
                moved_in = around[TILE - lag : 2 * TILE - lag]
                add(4 + lag, jnp.where(seg >= lag, own * moved_in, 0.0))

        return 0

    lax.fori_loop(0, rows // TILE + 1, taps, 0)


def per_chunk(array):
    shape = array.shape
    return pl.BlockSpec((1, *shape[1:]), lambda i: (i,) + (0,) * (len(shape) - 1))


def whole(array):
    return pl.BlockSpec(array.shape, lambda i: (0,) * len(array.shape))


def in_smem():
    return pl.BlockSpec(memory_space=pltpu.SMEM)


def params():
    return pltpu.CompilerParams(vmem_limit_bytes=VMEM_BYTES)


def run_forward(info, chan, rim, vec, dense):
    count, rows, width = chan.shape
    shape = jax.ShapeDtypeStruct
    outs = [shape(chan.shape, bf16)] + [shape(chan.shape, f32)] * 3
    return pl.pallas_call(
        forward_kernel,
        grid=(count,),
        out_shape=outs,
        in_specs=[in_smem(), per_chunk(chan), per_chunk(rim), whole(vec), whole(dense)],
        out_specs=[per_chunk(o) for o in outs],
        scratch_shapes=[
            pltpu.VMEM((rows + TILE, width), f32),
            pltpu.VMEM((rows, 2 * width), f32),
        ],
        compiler_params=params(),
        cost_estimate=pl.CostEstimate(
            flops=4 * count * rows * width * width,
            bytes_accessed=count * rows * width * 84,
            transcendentals=count * rows * width * 5,
        ),
    )(info, chan, rim, vec, dense)


def run_reverse(dec, grad):
    count, rows, width = dec.shape
    outs = [jax.ShapeDtypeStruct(dec.shape, f32)] * 2
    return pl.pallas_call(
        reverse_kernel,
        grid=(count,),
        out_shape=outs,
        in_specs=[per_chunk(dec), per_chunk(grad)],
        out_specs=[per_chunk(o) for o in outs],
        compiler_params=params(),
        cost_estimate=pl.CostEstimate(
            flops=20 * count * rows * width,
            bytes_accessed=count * rows * width * 14,
            transcendentals=0,
        ),
    )(dec, grad)


def run_chain(spot, parts, back):
    width = parts.shape[-1]
    vmem = pl.BlockSpec(memory_space=pltpu.VMEM)
    return pl.pallas_call(
        partial(chain_kernel, back),
        out_shape=[
            jax.ShapeDtypeStruct((QUARTERS, 2, width), f32),
            jax.ShapeDtypeStruct((2, width), f32),
        ],
        in_specs=[in_smem(), vmem],
        out_specs=[vmem, vmem],
        scratch_shapes=[pltpu.VMEM((8 * QUARTERS, 2, width), f32)],
        compiler_params=params(),
    )(spot, parts)


def run_backward(info, chan, rim, vec, dense, low, state, reach, enter, grad, moved, span, leave):
    count, rows, width = chan.shape
    shape = jax.ShapeDtypeStruct
    outs = [
        shape((count, rows, 2 * width), bf16),
        shape((count, rows, width), f32),
        shape((count, 8, width), f32),
        shape((8, width), f32),
    ]
    cut = [chan, rim, vec, dense, low, state, reach, enter, grad, moved, span, leave]
    specs = [whole(a) if a is vec or a is dense else per_chunk(a) for a in cut]
    return pl.pallas_call(
        backward_kernel,
        grid=(count,),
        out_shape=outs,
        in_specs=[in_smem(), *specs],
        out_specs=[per_chunk(o) for o in outs[:3]] + [whole(outs[3])],
        scratch_shapes=[
            pltpu.VMEM((rows + TILE, width), f32),
            pltpu.VMEM((rows, 2 * width), f32),
            pltpu.VMEM((rows + TILE, width), f32),
            pltpu.VMEM((rows + TILE, width), f32),
            pltpu.VMEM((rows + 2 * TILE, width), f32),
        ],
        compiler_params=params(),
        cost_estimate=pl.CostEstimate(
            flops=8 * count * rows * width * width,
            bytes_accessed=count * rows * width * 144,
            transcendentals=count * rows * width * 6,
        ),
    )(info, *cut)


def laid_kernel(cuts, at, *refs):
    pieces, outs = refs[: -len(cuts)], refs[-len(cuts) :]
    each = pieces[0].shape[0]
    for i, piece in enumerate(pieces):
        for k in range(each):
            first = 0
            for rows, out in zip(cuts, outs):
                to = pl.multiple_of(at[i * each + k] * rows, TILE)

                def move(t, _, piece=piece, k=k, to=to, first=first, out=out):
                    step = pl.multiple_of(t * TILE, TILE)
                    out[pl.ds(pl.multiple_of(to + step, TILE), TILE), :] = piece[
                        k, pl.ds(pl.multiple_of(first + step, TILE), TILE), :
                    ]
                    return 0

                lax.fori_loop(0, rows // TILE, move, 0)
                first += rows


def lay(pieces, at, cuts):
    count = at.shape[0]
    width = pieces[0].shape[-1]
    vmem = pl.BlockSpec(memory_space=pltpu.VMEM)
    return pl.pallas_call(
        partial(laid_kernel, cuts),
        out_shape=[jax.ShapeDtypeStruct((count * rows, width), pieces[0].dtype) for rows in cuts],
        in_specs=[in_smem(), *[vmem for _ in pieces]],
        out_specs=[vmem for _ in cuts],
        compiler_params=params(),
        cost_estimate=pl.CostEstimate(
            flops=0, bytes_accessed=4 * count * sum(cuts) * width, transcendentals=0
        ),
    )(at, *pieces)


def normed(values):
    rs = lax.rsqrt(jnp.mean(values * values, axis=-1, keepdims=True) + EPS)
    return rs, values * rs


def norm_back(rs, xs, gain, grad):
    scaled = gain * grad
    return rs * (scaled - xs * jnp.mean(xs * scaled, axis=-1, keepdims=True))


def body(
    places,
    tokens,
    cotangent,
    lengths,
    branch_weight,
    mixer_weight,
    branch_bias,
    mixer_bias,
    conv_taps,
    conv_bias,
    decay_weight,
    input_weight,
    decay_bias,
    input_bias,
    decay_param,
    output_weight,
    first_gain,
    second_gain,
    gate_weight,
    up_weight,
    down_weight,
):
    rows, features = tokens.shape
    slab, width = mixer_weight.shape
    block_width = decay_weight.shape[1]
    heads = width // block_width
    high = places.high
    dp_at, z = lax.axis_index("dp"), lax.axis_index("blk")
    h, p, c = dp_at // 8, dp_at // 2 % 4, dp_at % 2
    spot = jnp.stack([p, c, z]).astype(jnp.int32)

    straight = jnp.arange(QUARTERS, dtype=jnp.int32)
    order = p ^ jnp.where(c == 0, straight, (straight & 1) * 2 + straight // 2)
    chunk = ((h * 4 + order) * 2 + c) * 4 + z
    bucket_rows = BUCKET_DP * QUARTERS * rows
    start = chunk * rows
    bucket = (start + bucket_rows // 2) // bucket_rows
    begin = jnp.maximum(0, bucket * bucket_rows - bucket_rows // 2)
    ends = jnp.cumsum(jnp.take(lengths, bucket, axis=0), axis=1)
    info = jnp.concatenate([(start - begin)[:, None], ends], axis=1).astype(jnp.int32)

    inputs = tokens.astype(f32)
    gain_one, gain_two = first_gain.astype(f32), second_gain.astype(f32)
    rs_one, xs_one = normed(inputs)
    low_one = (xs_one * gain_one).astype(bf16)
    rim_rows = places.next_rows(low_one[rows - TILE :])

    def quarter(x, cuts):
        every, pieces = places.spread(x, p)
        at = [
            (jnp.arange(high) * 4 + (p ^ m)) * 2 + core for core in (c, 1 - c) for m in range(4)
        ]
        return every, lay([*pieces[0], *pieces[1]], jnp.concatenate(at).astype(jnp.int32), cuts)

    small = jnp.concatenate(
        [
            jnp.stack([branch_bias, mixer_bias]),
            conv_taps.T,
            jnp.stack([conv_bias, decay_bias, input_bias, decay_param]),
            jnp.zeros((TILE - PARAM - 1, width), bf16),
            decay_weight.T,
            input_weight.T,
        ],
        axis=0,
    )
    total_dp = 8 * high
    share = -(-small.shape[0] // (total_dp * TILE)) * TILE
    small = jnp.pad(small, ((0, share * total_dp - small.shape[0]), (0, 0)))
    small = lax.dynamic_slice_in_dim(small, dp_at * share, share, 0)
    early, (mixer_own, small) = quarter(
        jnp.concatenate([mixer_weight, small], axis=0), (slab, share)
    )
    vectors = small[:TILE].astype(f32)
    gate_turned = small[TILE : TILE + 2 * block_width]
    held = places.gather_rows(jnp.concatenate([rim_rows, low_one], axis=0))
    low_rows = jnp.concatenate([a[TILE:] for a in held], axis=0)
    rim_low = jnp.concatenate([a[:TILE] for a in held], axis=0)
    middle, (branch_own, output_own) = quarter(
        after(jnp.concatenate([branch_weight, output_weight.T], axis=0), early, held[3]),
        (slab, slab),
    )
    param = vectors[PARAM]
    vec = jnp.concatenate(
        [vectors[:SLOPE], -DECAY * jax.nn.softplus(-param)[None], vectors[SLOPE + 1 :]], axis=0
    )
    block_of = jnp.arange(width, dtype=jnp.int32) // block_width
    same = block_of[:, None] == block_of[None, :]
    dense = jnp.concatenate(
        [
            jnp.where(same, jnp.tile(gate_turned[:block_width], (heads, 1)), 0),
            jnp.where(same, jnp.tile(gate_turned[block_width:], (heads, 1)), 0),
        ],
        axis=0,
    ).astype(bf16)

    channels = (plain(low_rows, mixer_own) + vec[MIXER_BIAS]).astype(bf16)
    rim = (plain(rim_low, mixer_own) + vec[MIXER_BIAS]).astype(bf16)
    feed_held = places.gather_rows_direct(after(cotangent, mixer_own))
    feed_grad = jnp.concatenate(feed_held, axis=0)
    channels = channels.reshape(QUARTERS, rows, width)
    rim = rim.reshape(QUARTERS, TILE, width)
    conv_low, decays, state_local, reach = run_forward(info, channels, rim, vec, dense)
    gate_use = places.gather_rest(after(gate_weight.T, mixer_own))
    up_use = places.gather_rest(after(up_weight.T, conv_low))
    branch_pre = plain(low_rows, branch_own) + vec[BRANCH_BIAS]

    def entering(parts, back, others=()):
        pair = jnp.stack([parts, places.core(parts)])
        every = jnp.stack([pair] + [places.along_z(pair, k) for k in (1, 2, 3)])
        own, total = run_chain(spot, after(every, *others), back)
        if high == 1:
            return own[:, 1:2]
        held = [total]
        for _ in range(high - 1):
            held.append(places.along_h(held[-1]))
        state = jnp.zeros((1, width), f32)
        for hop in range(high - 1):
            source = high - 1 - hop if back else hop
            far = (h - source + high) % high
            picked = lax.dynamic_index_in_dim(jnp.stack(held), far, 0, False)
            ahead = source > h if back else source < h
            state = jnp.where(ahead, picked[0:1] * state + picked[1:2], state)
        return own[:, 1:2] + own[:, 0:1] * state[None]

    enter = entering(jnp.stack([reach[:, -1], state_local[:, -1]], axis=1), False, feed_held)
    down_use = places.gather_rest(after(down_weight, enter))
    branch_act, gelu_back_one = jax.vjp(jax.nn.gelu, branch_pre)
    state_low = (state_local + reach * enter).astype(bf16).reshape(QUARTERS * rows, width)
    mixed_low = (branch_act * state_low.astype(f32)).astype(bf16)

    def rows_of(array, k):
        return array[k * rows : (k + 1) * rows]

    resid_sum, _ = places.scatter_rows(
        [trailing(rows_of(mixed_low, k), output_own) for k in range(QUARTERS)]
    )
    resid = inputs + resid_sum

    rs_two, xs_two = normed(resid)
    low_two = (xs_two * gain_two).astype(bf16)
    feed_rows = jnp.concatenate(places.gather_rows(low_two), axis=0)
    gate_pre = trailing(feed_rows, gate_use)
    up_pre = trailing(feed_rows, up_use)
    gate_act, gelu_back_two = jax.vjp(jax.nn.gelu, gate_pre)
    hidden = (gate_act * up_pre).astype(bf16)
    half = hidden.shape[1] // 2

    def columns(array, core):
        return lax.dynamic_slice_in_dim(array, core * half, half, 1)

    def column_far(grad, rows_in):
        return leading(columns(grad, 1 - c), rows_in).astype(bf16)

    def column_own(grad, rows_in, far):
        total = leading(columns(grad, c), rows_in) + places.core(far).astype(f32)
        return total.astype(bf16)

    def column_scatter(total):
        return lax.psum_scatter(total, "blk", scatter_dimension=0, tiled=True)

    def column_sum(total):
        if high > 1:
            total = total.reshape(high, -1, features)
            total = jnp.take(total, (h - jnp.arange(high)) % high, axis=0)
            total = places.scatter_high(total.reshape(-1, features))
        return total.astype(f32)

    down_far = column_far(hidden, feed_grad)
    down_own = column_own(hidden, feed_grad, down_far)
    down_scattered = column_scatter(down_own)
    hidden_grad = trailing(feed_grad, after(down_use, down_own))
    gate_grad = gelu_back_two(hidden_grad * up_pre)[0].astype(bf16)
    up_grad = (hidden_grad * gate_act).astype(bf16)
    def norm_part(k, gate_in, up_in):
        return plain(rows_of(gate_in, k), gate_use) + plain(rows_of(up_in, k), up_use)

    norm_parts = [norm_part(k, gate_grad, up_grad) for k in range(QUARTERS)]
    norm_grad, _ = places.scatter_rows(norm_parts)
    gate_late, *_ = lax.optimization_barrier((gate_grad, *norm_parts))
    gate_far = column_far(gate_late, feed_rows)
    norm_grad = after(norm_grad, gate_far)
    second_term = jnp.sum(norm_grad * xs_two, axis=0)
    resid_grad = cotangent.astype(f32) + norm_back(rs_two, xs_two, gain_two, norm_grad)

    resid_low = resid_grad.astype(bf16)
    resid_rows = jnp.concatenate(places.gather_rows(resid_low), axis=0)
    gate_last, up_late, hidden_last, _ = lax.optimization_barrier(
        (gate_late, up_grad, hidden, resid_low)
    )
    gate_own = column_own(gate_last, feed_rows, gate_far)
    gate_scattered = column_scatter(gate_own)
    up_far = column_far(up_late, feed_rows)
    output_terms = [plain(rows_of(hidden_last, k), down_use) for k in range(QUARTERS)]
    resid_rows, *output_terms = lax.optimization_barrier(
        (resid_rows, *output_terms, up_far, gate_own, down_scattered)
    )[:-3]
    output, output_joined = places.scatter_rows(output_terms)
    output = (resid + output).astype(bf16)
    mixed_grad = plain(resid_rows, output_own)
    state_grad = (mixed_grad * branch_act).astype(bf16).reshape(QUARTERS, rows, width)
    branch_grad = gelu_back_one(mixed_grad * state_low.astype(f32))[0].astype(bf16)
    moved, span_back = run_reverse(decays, state_grad)
    resid_late, mixed_late, low_late, branch_late, up_last, _ = lax.optimization_barrier(
        (resid_rows, mixed_low, low_rows, branch_grad, up_late, moved)
    )
    leave = entering(jnp.stack([span_back[:, 0], moved[:, 0]], axis=1), True)
    def quarter_half(term):
        slab_in = term.shape[0] // total_dp
        term = term.astype(bf16).reshape(high * 4, 2 * slab_in, width)
        own = lax.dynamic_slice_in_dim(term, c * slab_in, slab_in, 1)
        came = places.core(lax.dynamic_slice_in_dim(term, (1 - c) * slab_in, slab_in, 1))
        return (own + came).reshape(high, 4, slab_in, width), came

    def quarter_rows(half):
        return [
            places.flip_p(lax.dynamic_index_in_dim(half, p ^ m, 1, False), m) for m in range(4)
        ]

    def quarter_high(total):
        if high > 1:
            total = jnp.take(total, (h - jnp.arange(high)) % high, axis=0)
            return places.scatter_high(total.reshape(-1, width))
        return total[0].astype(f32)

    def quarter_near(parts):
        stacked = jnp.stack(parts)

        def by(k):
            return lax.dynamic_index_in_dim(stacked, p ^ ((z + k) % 4), 0, False)

        total = by(0).astype(f32)
        for k in (1, 2, 3):
            total = total + places.along_z(by(k), k).astype(f32)
        return quarter_high(total)

    def quarter_far(parts, gates):
        *parts, _ = lax.optimization_barrier((*parts, gates))
        stacked = jnp.take(jnp.stack(parts), p ^ straight, axis=0)
        return quarter_high(lax.psum_scatter(stacked, "blk", scatter_dimension=0, tiled=True)[0])

    output_term = leading(resid_late, mixed_late)
    branch_term = leading(low_late, branch_late)
    up_own = column_own(up_last, feed_rows, up_far)
    up_scattered = column_scatter(up_own)
    output_half, output_came = quarter_half(output_term)
    branch_half, branch_came = quarter_half(branch_term)
    leave = after(leave, output_came, branch_came, output_joined, up_own, gate_scattered)
    output_parts = quarter_rows(output_half)
    branch_parts = quarter_rows(branch_half)
    gates, chan_grad, rim_grad, sums = run_backward(
        info, channels, rim, vec, dense, conv_low, state_local, reach, enter, state_grad, moved,
        span_back, leave,
    )

    output_sum = quarter_far(output_parts, gates).T
    branch_sum = quarter_far(branch_parts, gates)

    came = places.back_rows(rim_grad)
    last = (c == 1) & (z == 3)
    wanted = order + jnp.where(last, 1, 0)
    from_core = jnp.where(z == 3, 1 - c, c)
    offset = (wanted % 4) ^ p
    slot = jnp.where(from_core == 0, offset, (offset & 1) * 2 + offset // 2)
    pick = (slot[:, None] == straight[None, :]).astype(f32)
    here = jnp.where(wanted < 4, 1.0, 0.0)[:, None]

    def picked(select, array):
        return jnp.sum(select[:, :, None, None] * array[None], axis=1)

    returned = picked(pick * here, came)
    if high > 1:
        returned = returned + picked(pick * (1.0 - here), places.back_high(came))
    chan_grad = chan_grad + jnp.pad(returned, ((0, 0), (rows - 8, 0), (0, 0)))
    mixer_grad = after(chan_grad, *output_parts, *branch_parts, up_scattered).astype(bf16)
    mixer_grad = mixer_grad.reshape(QUARTERS * rows, width)

    low_parts = [
        trailing(rows_of(branch_grad, k), branch_own) + trailing(rows_of(mixer_grad, k), mixer_own)
        for k in range(QUARTERS)
    ]
    low_grad, _ = places.scatter_rows(low_parts)
    mixer_late, *_ = lax.optimization_barrier((mixer_grad, *low_parts))
    mixer_term = leading(low_rows, mixer_late)
    mixer_half, mixer_came = quarter_half(mixer_term)
    mixer_sum = quarter_near(quarter_rows(mixer_half))
    gates, mixer_term, _ = lax.optimization_barrier((gates, mixer_term, mixer_came))
    token_grad = (resid_grad + norm_back(rs_one, xs_one, gain_one, low_grad)).astype(bf16)

    first_term = (
        jnp.sum(branch_term * branch_own.astype(f32), axis=1)
        + jnp.sum(mixer_term * mixer_own.astype(f32), axis=1)
    ) / gain_one
    gain_sums = places.sum_all(jnp.stack([first_term, second_term]))

    crossed = leading(gates.reshape(QUARTERS * rows, 2 * width), conv_low.reshape(-1, width))
    picked_blocks = block_of[None, :] == jnp.arange(heads)[:, None]
    gate_terms = jnp.sum(
        jnp.where(picked_blocks[None, :, None, :], crossed.reshape(2, heads, block_width, width), 0),
        axis=1,
    )
    vector_terms = jnp.concatenate(
        [
            sums,
            jnp.sum(branch_grad.astype(f32), axis=0)[None],
            jnp.sum(mixer_grad.astype(f32), axis=0)[None],
            jnp.zeros((6, width), f32),
        ],
        axis=0,
    )
    slope_back = DECAY * jax.nn.sigmoid(-param)
    vector_terms = vector_terms.at[2].multiply(slope_back)
    small_terms = jnp.concatenate(
        [vector_terms, gate_terms.reshape(2 * block_width, width)], axis=0
    )
    small_terms = jnp.pad(small_terms, ((0, share * total_dp - small_terms.shape[0]), (0, 0)))
    small_sum = quarter_near(quarter_rows(quarter_half(small_terms)[0]))
    small_held = [small_sum]
    for _ in range(high - 1):
        small_held.append(places.along_h(small_held[-1]))
    small_held = jnp.stack(small_held)
    small_held = jnp.stack(places.gather_rows(small_held))
    small_held = jnp.stack([small_held, places.core(small_held)])
    where = []
    for hh in range(high):
        for a in range(4):
            for core in range(2):
                offset = p ^ a
                crossed_at = (offset & 1) * 2 + offset // 2
                slot = offset if core == 0 else crossed_at
                where.append((((c ^ core) * 4 + slot) * high) + (h - hh + high) % high)
    small_total = jnp.take(
        small_held.reshape(-1, share, width), jnp.stack(where), axis=0
    ).reshape(-1, width)
    vector_total = small_total[:TILE]
    gate_total = small_total[TILE : TILE + 2 * block_width]
    gate_sum, up_sum = column_sum(gate_scattered).T, column_sum(up_scattered).T
    down_sum = column_sum(down_scattered)
    return (
        output,
        token_grad,
        branch_sum,
        mixer_sum,
        vector_total[8],
        vector_total[9],
        vector_total[4:8].T,
        vector_total[3],
        gate_total[:block_width].T,
        gate_total[block_width:].T,
        vector_total[0],
        vector_total[1],
        vector_total[2],
        output_sum,
        gain_sums[0],
        gain_sums[1],
        gate_sum,
        up_sum,
        down_sum,
    )


def solution(mesh):
    places = Places(mesh.shape["dp"], mesh.shape["blk"])
    return jax.shard_map(
        partial(body, places),
        mesh=mesh,
        in_specs=(
            P(("dp", "blk"), None),
            P(("dp", "blk"), None),
            P(),
            P("dp", "blk"),
            P("dp", "blk"),
            P("blk"),
            P("blk"),
            P("blk", None),
            P("blk"),
            P("blk", None),
            P("blk", None),
            P("blk"),
            P("blk"),
            P("blk"),
            P("blk", "dp"),
            P(),
            P(),
            P(None, ("dp", "blk")),
            P(None, ("dp", "blk")),
            P(("dp", "blk"), None),
        ),
        out_specs=(
            P(("dp", "blk"), None),
            P(("dp", "blk"), None),
            P("dp", "blk"),
            P("dp", "blk"),
            P("blk"),
            P("blk"),
            P("blk", None),
            P("blk"),
            P("blk", None),
            P("blk", None),
            P("blk"),
            P("blk"),
            P("blk"),
            P("blk", "dp"),
            P(),
            P(),
            P(None, ("dp", "blk")),
            P(None, ("dp", "blk")),
            P(("dp", "blk"), None),
        ),
        check_vma=False,
    )
```

```python
from functools import partial

import jax
import jax.numpy as jnp
from jax import lax
from jax.experimental import pallas as pl
from jax.experimental.pallas import tpu as pltpu
from jax.sharding import PartitionSpec as P

BUCKET_DP = 4
EPS = 1e-06
DECAY = 8.0
TAPS = 4
QUARTERS = 4
TILE = 16
AXES = ("dp", "blk")
f32 = jnp.float32
bf16 = jnp.bfloat16
VMEM_BYTES = 40 * 2**20

BRANCH_BIAS, MIXER_BIAS, TAP_ROW, CONV_BIAS, DECAY_BIAS, INPUT_BIAS, PARAM = 0, 1, 2, 6, 7, 8, 9
SLOPE = 10


def plain(former, latter):
    return jnp.dot(former, latter, preferred_element_type=f32)


def trailing(former, latter):
    return lax.dot_general(former, latter, (((1,), (1,)), ((), ())), preferred_element_type=f32)


def leading(former, latter):
    return lax.dot_general(former, latter, (((0,), (0,)), ((), ())), preferred_element_type=f32)


class Places:
    def __init__(self, dp, blk):
        assert blk == QUARTERS and dp % (2 * QUARTERS) == 0
        self.n = dp * blk
        self.high = dp // (2 * QUARTERS)

    @staticmethod
    def split(i):
        return i // 32, i // 8 % 4, i // 4 % 2, i % 4

    @staticmethod
    def join(h, p, c, z):
        return ((h * 4 + p) * 2 + c) * 4 + z

    def send(self, x, route):
        pairs = []
        for i in range(self.n):
            to = route(*self.split(i))
            if to is not None:
                pairs.append((i, self.join(*to)))
        return jax.tree.map(lambda a: lax.ppermute(a, AXES, pairs), x)

    def one(self, x):
        return self.send(x, lambda h, p, c, z: (h, p ^ (1 + c), c, z))

    def two(self, x):
        return self.send(x, lambda h, p, c, z: (h, p ^ (2 - c), c, z))

    def flip_p(self, x, bit):
        return x if bit == 0 else self.send(x, lambda h, p, c, z: (h, p ^ bit, c, z))

    def flip_z(self, x, bit):
        return self.send(x, lambda h, p, c, z: (h, p, c, z ^ bit))

    def core(self, x):
        return self.send(x, lambda h, p, c, z: (h, p, 1 - c, z))

    def along_z(self, x, by=1):
        return self.send(x, lambda h, p, c, z: (h, p, c, (z + by) % 4))

    def along_h(self, x):
        return self.send(x, lambda h, p, c, z: ((h + 1) % self.high, p, c, z))

    def next_rows(self, x):
        def route(*at):
            i = self.join(*at) + 1
            return self.split(i) if i < self.n else None

        return self.send(x, route)

    def back_rows(self, x):
        def route(h, p, c, z):
            i = (c * 4 + z + 7) % 8
            return h, p, i // 4, i % 4

        return self.send(x, route)

    def back_high(self, x):
        return self.send(x, lambda h, p, c, z: (h - 1, p, c, z) if h else None)

    def gather_rows(self, x):
        first = self.one(x)
        second = self.two(jnp.concatenate([x, first], axis=0))
        return x, first, second

    def gather_rows_early(self, x):
        first = self.one(x)
        second = self.two(x)
        return x, first, second, self.two(first)

    def scatter_rows(self, far, near):
        rows = near.shape[0] // 2
        came = self.two(far.astype(bf16)).astype(f32)
        joined = (near[rows:] + came[rows:]).astype(bf16)
        return near[:rows] + came[:rows] + self.one(joined).astype(f32), joined

    def scatter_rows_early(self, parts):
        far = self.two(parts[3].astype(bf16))
        side = self.two(parts[2].astype(bf16))
        near = self.one((parts[1] + far.astype(f32)).astype(bf16))
        return parts[0] + side.astype(f32) + near.astype(f32)

    def spread(self, x, p, *others):
        groups = [
            [self.join(h, q, c, z) for h in range(self.high) for z in range(4)]
            for q in range(QUARTERS)
            for c in range(2)
        ]
        every = lax.all_gather(x, AXES, axis_index_groups=groups, axis=0, tiled=True)
        slab, width = x.shape

        def pick(m):
            if self.high == 1:
                return lax.dynamic_slice_in_dim(every, (p ^ m) * slab, slab, 0)[None]
            return lax.dynamic_index_in_dim(
                every.reshape(self.high, 4, slab, width), p ^ m, 1, False
            )

        own = [self.flip_p(pick(m), m) for m in range(4)]
        return every, [own, [self.core(after(a, *others)) for a in own]]

    def gather_rest(self, x, axis=0):
        groups = [
            [self.join(h, p, c, z) for c in range(2) for z in range(4) for h in range(self.high)]
            for p in range(QUARTERS)
        ]
        return lax.all_gather(x, AXES, axis_index_groups=groups, axis=axis, tiled=True)

    def scatter_high(self, x):
        if self.high == 1:
            return x
        rows = x.shape[0] // self.high
        piece = [x[k * rows : (k + 1) * rows] for k in range(self.high)]
        total = piece[1]
        for k in range(1, self.high):
            total = self.along_h(total.astype(bf16)).astype(f32) + piece[(k + 1) % self.high]
        return total

    def sum_all(self, x):
        x = x + self.core(x)
        x = x + self.flip_p(x, 1)
        x = x + self.flip_p(x, 2)
        x = x + self.flip_z(x, 1)
        x = x + self.flip_z(x, 2)
        total = x
        for _ in range(self.high - 1):
            x = self.along_h(x)
            total = total + x
        return total


def after(x, *others):
    return lax.optimization_barrier((x, *others))[0]


def swapped(offset):
    return (offset & 1) * 2 + offset // 2


LANES = 128


def wide(mask, width):
    mask = jnp.where(mask, 1.0, 0.0)
    return jnp.concatenate([mask] * (width // LANES), axis=1)


def place_rows(info, chunk, first, count):
    shape = (count, LANES)
    spot = info[chunk, 0] + first + lax.broadcasted_iota(jnp.int32, shape, 0)
    begin = jnp.zeros(shape, jnp.int32)
    for border in (1, 2, 3):
        begin = jnp.where(spot >= info[chunk, border], info[chunk, border], begin)
    return spot - begin, (spot >= 0) & (spot < info[chunk, 4])


def less_one(y):
    series = 1.0 + y * (1.0 / 6.0)
    for k in (5.0, 4.0, 3.0, 2.0):
        series = 1.0 + y * (1.0 / k) * series
    return jnp.where(y > -0.25, -y * series, 1.0 - jnp.exp(y))


def sigmoid(v):
    return 1.0 / (1.0 + jnp.exp(-v))


def scan_rows(a, b, back):
    rows = lax.broadcasted_iota(jnp.int32, a.shape, 0)
    count = a.shape[0]
    step = 1
    while step < count:
        by = count - step if back else step
        keep = rows < count - step if back else rows >= step
        b = jnp.where(keep, a * pltpu.roll(b, by, 0) + b, b)
        a = jnp.where(keep, a * pltpu.roll(a, by, 0), a)
        step *= 2
    return a, b


def forward_kernel(info, chan, rim, vec, dense, low, dec, state, reach, ext, pre):
    chunk = pl.program_id(0)
    rows, width = chan.shape[1:]
    ext[:TILE] = rim[0].astype(f32)
    ext[TILE:] = chan[0].astype(f32)

    def conv(t, _):
        base = pl.multiple_of(t * TILE, TILE)
        near = ext[pl.ds(base, 2 * TILE), :]
        seg, _filled = place_rows(info, chunk, base, TILE)
        total = jnp.broadcast_to(vec[CONV_BIAS : CONV_BIAS + 1, :], (TILE, width))
        for lag in range(TAPS):
            moved = near[TILE - lag : 2 * TILE - lag]
            tap = vec[TAP_ROW + lag : TAP_ROW + lag + 1, :]
            moved = tap * moved
            total = total + (wide(seg >= lag, width) * moved if lag else moved)
        low[0, pl.ds(base, TILE), :] = total.astype(bf16)
        return 0

    lax.fori_loop(0, rows // TILE, conv, 0)
    pre[...] = trailing(low[0], dense[...])

    def tile(t, held):
        base = pl.multiple_of(t * TILE, TILE)
        span = pl.ds(base, TILE)
        seg, filled = place_rows(info, chunk, base, TILE)
        open_decay = sigmoid(pre[span, :width] + vec[DECAY_BIAS : DECAY_BIAS + 1, :])
        open_input = sigmoid(pre[span, width:] + vec[INPUT_BIAS : INPUT_BIAS + 1, :])
        log_decay = open_decay * vec[SLOPE : SLOPE + 1, :]
        decay = wide((seg != 0) & filled, width) * jnp.exp(log_decay)
        factor = wide((seg == 0) & filled, width) + wide((seg != 0) & filled, width) * jnp.sqrt(
            less_one(2.0 * log_decay)
        )
        drive = factor * open_input * low[0, span, :].astype(f32)
        dec[0, span, :] = decay
        entered, passed = held
        for half in range(TILE // 8):
            part = slice(half * 8, half * 8 + 8)
            a, b = scan_rows(decay[part], drive[part], False)
            b = b + a * entered
            a = a * passed
            at = pl.ds(pl.multiple_of(base + half * 8, 8), 8)
            state[0, at, :] = b
            reach[0, at, :] = a
            entered, passed = b[7:8], a[7:8]
        return entered, passed

    lax.fori_loop(
        0, rows // TILE, tile, (jnp.zeros((1, width), f32), jnp.ones((1, width), f32))
    )


def reverse_kernel(dec, grad, moved, reach):
    rows, width = dec.shape[1:]

    def tile(t, held):
        base = pl.multiple_of(rows - TILE - t * TILE, TILE)
        span = pl.ds(base, TILE)
        decay = dec[0, span, :]
        drive = decay * grad[0, span, :].astype(f32)
        entered, passed = held
        for half in reversed(range(TILE // 8)):
            part = slice(half * 8, half * 8 + 8)
            a, b = scan_rows(decay[part], drive[part], True)
            b = b + a * entered
            a = a * passed
            at = pl.ds(pl.multiple_of(base + half * 8, 8), 8)
            moved[0, at, :] = b
            reach[0, at, :] = a
            entered, passed = b[0:1], a[0:1]
        return entered, passed

    lax.fori_loop(
        0, rows // TILE, tile, (jnp.zeros((1, width), f32), jnp.ones((1, width), f32))
    )


def chain_kernel(back, spot, parts, own, total, every):
    p, c, z = spot[0], spot[1], spot[2]
    factor = jnp.ones((1, own.shape[-1]), f32)
    term = jnp.zeros((1, own.shape[-1]), f32)
    count = 8 * QUARTERS
    for i in reversed(range(count)) if back else range(count):
        j, cc, zz = i // 8, i // 4 % 2, i % 4
        every[i, 0:1, :] = factor
        every[i, 1:2, :] = term
        offset = j ^ p
        slot = swapped(offset) if cc else offset
        pair = parts[(z - zz + 4) % 4, c ^ cc, slot]
        term = pair[0:1] * term + pair[1:2]
        factor = pair[0:1] * factor
    total[0:1, :] = factor
    total[1:2, :] = term
    for r in range(QUARTERS):
        j = p ^ jnp.where(c == 0, r, (r & 1) * 2 + r // 2)
        own[r] = every[(j * 2 + c) * 4 + z]


def backward_kernel(
    info, chan, rim, vec, dense, low, state, reach, enter, grad, moved, span_back, leave,
    crossed, chan_grad, rim_grad, sums,
    ext, pre, past, later, conv_grad, gates,
):
    chunk = pl.program_id(0)
    rows, width = chan.shape[1:]
    ext[:TILE] = rim[0].astype(f32)
    ext[TILE:] = chan[0].astype(f32)
    pre[...] = trailing(low[0], dense[...])
    past[0:TILE] = jnp.broadcast_to(enter[0], (TILE, width))
    later[rows : rows + TILE] = jnp.broadcast_to(leave[0], (TILE, width))
    conv_grad[:TILE] = jnp.zeros((TILE, width), f32)
    conv_grad[rows + TILE :] = jnp.zeros((TILE, width), f32)

    @pl.when(chunk == 0)
    def _():
        sums[...] = jnp.zeros_like(sums)
        crossed[...] = jnp.zeros_like(crossed)

    def fill(t, _):
        base = pl.multiple_of(t * TILE, TILE)
        span = pl.ds(base, TILE)
        past[pl.ds(pl.multiple_of(base + TILE, TILE), TILE), :] = (
            state[0, span, :] + reach[0, span, :] * enter[0]
        )
        later[span, :] = moved[0, span, :] + span_back[0, span, :] * leave[0]
        return 0

    lax.fori_loop(0, rows // TILE, fill, 0)

    def add(row, value):
        sums[row : row + 1, :] += jnp.sum(value, axis=0, keepdims=True)

    def tile(t, _):
        base = pl.multiple_of(t * TILE, TILE)
        span = pl.ds(base, TILE)
        seg, filled = place_rows(info, chunk, base, TILE)
        restart = wide((seg == 0) & filled, width)
        going = wide((seg != 0) & filled, width)
        before = past[pl.ds(base, 2 * TILE), :][TILE - 1 : 2 * TILE - 1]
        adjoint = grad[0, span, :].astype(f32) + later[pl.ds(base, 2 * TILE), :][1 : TILE + 1]
        open_decay = sigmoid(pre[span, :width] + vec[DECAY_BIAS : DECAY_BIAS + 1, :])
        open_input = sigmoid(pre[span, width:] + vec[INPUT_BIAS : INPUT_BIAS + 1, :])
        slope = vec[SLOPE : SLOPE + 1, :]
        log_decay = open_decay * slope
        decay = jnp.exp(log_decay)
        square = less_one(2.0 * log_decay)
        value = low[0, span, :].astype(f32)
        root = lax.rsqrt(square)
        root = jnp.where(going > 0.0, root, 0.0)
        opened = open_input * adjoint
        direct = (restart + square * root) * opened
        input_grad = direct * value * (1.0 - open_input)
        log_grad = going * decay * (adjoint * before - opened * value * decay * root)
        decay_grad = log_grad * slope * open_decay * (1.0 - open_decay)
        decay_low = decay_grad.astype(bf16)
        input_low = input_grad.astype(bf16)
        gates[span, :width] = decay_low
        gates[span, width:] = input_low
        conv_grad[pl.ds(pl.multiple_of(base + TILE, TILE), TILE), :] = direct
        add(0, decay_low.astype(f32))
        add(1, input_low.astype(f32))
        add(2, log_grad * open_decay)
        return 0

    lax.fori_loop(0, rows // TILE, tile, 0)
    conv_grad[TILE : rows + TILE] += plain(gates[...], dense[...])
    crossed[...] += leading(gates[...], low[0])

    def taps(t, _):
        base = pl.multiple_of(t * TILE, TILE)
        near = conv_grad[pl.ds(base, 2 * TILE), :]
        back = jnp.zeros((TILE, width), f32)
        for lag in range(TAPS):
            seg, _filled = place_rows(info, chunk, base - TILE + lag, TILE)
            tap = vec[TAP_ROW + lag : TAP_ROW + lag + 1, :] * near[lag : TILE + lag]
            back = back + (wide(seg >= lag, width) * tap if lag else tap)

        @pl.when(t == 0)
        def _():
            rim_grad[0] = back[TILE - 8 :]

        @pl.when(t > 0)
        def _():
            at = pl.multiple_of(base - TILE, TILE)
            chan_grad[0, pl.ds(at, TILE), :] = back
            around = ext[pl.ds(at, 2 * TILE), :]
            seg, _filled = place_rows(info, chunk, at, TILE)
            own = near[:TILE]
            add(3, own)
            for lag in range(TAPS):
                moved_in = around[TILE - lag : 2 * TILE - lag]
                moved_in = own * moved_in
                add(4 + lag, wide(seg >= lag, width) * moved_in if lag else moved_in)

        return 0

    lax.fori_loop(0, rows // TILE + 1, taps, 0)


def per_chunk(array):
    shape = array.shape
    return pl.BlockSpec((1, *shape[1:]), lambda i: (i,) + (0,) * (len(shape) - 1))


def whole(array):
    return pl.BlockSpec(array.shape, lambda i: (0,) * len(array.shape))


def in_smem():
    return pl.BlockSpec(memory_space=pltpu.SMEM)


def params():
    return pltpu.CompilerParams(vmem_limit_bytes=VMEM_BYTES)


def run_forward(info, chan, rim, vec, dense):
    count, rows, width = chan.shape
    shape = jax.ShapeDtypeStruct
    outs = [shape(chan.shape, bf16)] + [shape(chan.shape, f32)] * 3
    return pl.pallas_call(
        forward_kernel,
        grid=(count,),
        out_shape=outs,
        in_specs=[in_smem(), per_chunk(chan), per_chunk(rim), whole(vec), whole(dense)],
        out_specs=[per_chunk(o) for o in outs],
        scratch_shapes=[
            pltpu.VMEM((rows + TILE, width), f32),
            pltpu.VMEM((rows, 2 * width), f32),
        ],
        compiler_params=params(),
        cost_estimate=pl.CostEstimate(
            flops=4 * count * rows * width * width,
            bytes_accessed=count * rows * width * 84,
            transcendentals=count * rows * width * 5,
        ),
    )(info, chan, rim, vec, dense)


def run_reverse(dec, grad):
    count, rows, width = dec.shape
    outs = [jax.ShapeDtypeStruct(dec.shape, f32)] * 2
    return pl.pallas_call(
        reverse_kernel,
        grid=(count,),
        out_shape=outs,
        in_specs=[per_chunk(dec), per_chunk(grad)],
        out_specs=[per_chunk(o) for o in outs],
        compiler_params=params(),
        cost_estimate=pl.CostEstimate(
            flops=20 * count * rows * width,
            bytes_accessed=count * rows * width * 14,
            transcendentals=0,
        ),
    )(dec, grad)


def run_chain(spot, parts, back):
    width = parts.shape[-1]
    vmem = pl.BlockSpec(memory_space=pltpu.VMEM)
    return pl.pallas_call(
        partial(chain_kernel, back),
        out_shape=[
            jax.ShapeDtypeStruct((QUARTERS, 2, width), f32),
            jax.ShapeDtypeStruct((2, width), f32),
        ],
        in_specs=[in_smem(), vmem],
        out_specs=[vmem, vmem],
        scratch_shapes=[pltpu.VMEM((8 * QUARTERS, 2, width), f32)],
        compiler_params=params(),
    )(spot, parts)


def run_backward(info, chan, rim, vec, dense, low, state, reach, enter, grad, moved, span, leave):
    count, rows, width = chan.shape
    shape = jax.ShapeDtypeStruct
    outs = [
        shape((2 * width, width), f32),
        shape((count, rows, width), f32),
        shape((count, 8, width), f32),
        shape((8, width), f32),
    ]
    cut = [chan, rim, vec, dense, low, state, reach, enter, grad, moved, span, leave]
    specs = [whole(a) if a is vec or a is dense else per_chunk(a) for a in cut]
    return pl.pallas_call(
        backward_kernel,
        grid=(count,),
        out_shape=outs,
        in_specs=[in_smem(), *specs],
        out_specs=[whole(outs[0]), per_chunk(outs[1]), per_chunk(outs[2]), whole(outs[3])],
        scratch_shapes=[
            pltpu.VMEM((rows + TILE, width), f32),
            pltpu.VMEM((rows, 2 * width), f32),
            pltpu.VMEM((rows + TILE, width), f32),
            pltpu.VMEM((rows + TILE, width), f32),
            pltpu.VMEM((rows + 2 * TILE, width), f32),
            pltpu.VMEM((rows, 2 * width), bf16),
        ],
        compiler_params=params(),
        cost_estimate=pl.CostEstimate(
            flops=8 * count * rows * width * width,
            bytes_accessed=count * rows * width * 144,
            transcendentals=count * rows * width * 6,
        ),
    )(info, *cut)


def laid_kernel(cuts, at, *refs):
    pieces, outs = refs[: -len(cuts)], refs[-len(cuts) :]
    each = pieces[0].shape[0]
    for i, piece in enumerate(pieces):
        for k in range(each):
            first = 0
            for rows, out in zip(cuts, outs):
                to = pl.multiple_of(at[i * each + k] * rows, TILE)

                def move(t, _, piece=piece, k=k, to=to, first=first, out=out):
                    step = pl.multiple_of(t * TILE, TILE)
                    out[pl.ds(pl.multiple_of(to + step, TILE), TILE), :] = piece[
                        k, pl.ds(pl.multiple_of(first + step, TILE), TILE), :
                    ]
                    return 0

                lax.fori_loop(0, rows // TILE, move, 0)
                first += rows


def lay(pieces, at, cuts):
    count = at.shape[0]
    width = pieces[0].shape[-1]
    vmem = pl.BlockSpec(memory_space=pltpu.VMEM)
    return pl.pallas_call(
        partial(laid_kernel, cuts),
        out_shape=[jax.ShapeDtypeStruct((count * rows, width), pieces[0].dtype) for rows in cuts],
        in_specs=[in_smem(), *[vmem for _ in pieces]],
        out_specs=[vmem for _ in cuts],
        compiler_params=params(),
        cost_estimate=pl.CostEstimate(
            flops=0, bytes_accessed=4 * count * sum(cuts) * width, transcendentals=0
        ),
    )(at, *pieces)


def normed(values):
    rs = lax.rsqrt(jnp.mean(values * values, axis=-1, keepdims=True) + EPS)
    return rs, values * rs


def norm_back(rs, xs, gain, grad):
    scaled = gain * grad
    return rs * (scaled - xs * jnp.mean(xs * scaled, axis=-1, keepdims=True))


def body(
    places,
    tokens,
    cotangent,
    lengths,
    branch_weight,
    mixer_weight,
    branch_bias,
    mixer_bias,
    conv_taps,
    conv_bias,
    decay_weight,
    input_weight,
    decay_bias,
    input_bias,
    decay_param,
    output_weight,
    first_gain,
    second_gain,
    gate_weight,
    up_weight,
    down_weight,
):
    rows, features = tokens.shape
    slab, width = mixer_weight.shape
    block_width = decay_weight.shape[1]
    heads = width // block_width
    high = places.high
    dp_at, z = lax.axis_index("dp"), lax.axis_index("blk")
    h, p, c = dp_at // 8, dp_at // 2 % 4, dp_at % 2
    spot = jnp.stack([p, c, z]).astype(jnp.int32)

    straight = jnp.arange(QUARTERS, dtype=jnp.int32)
    order = p ^ jnp.where(c == 0, straight, (straight & 1) * 2 + straight // 2)
    chunk = ((h * 4 + order) * 2 + c) * 4 + z
    bucket_rows = BUCKET_DP * QUARTERS * rows
    start = chunk * rows
    bucket = (start + bucket_rows // 2) // bucket_rows
    begin = jnp.maximum(0, bucket * bucket_rows - bucket_rows // 2)
    ends = jnp.cumsum(jnp.take(lengths, bucket, axis=0), axis=1)
    info = jnp.concatenate([(start - begin)[:, None], ends], axis=1).astype(jnp.int32)

    inputs = tokens.astype(f32)
    gain_one, gain_two = first_gain.astype(f32), second_gain.astype(f32)
    rs_one, xs_one = normed(inputs)
    low_one = (xs_one * gain_one).astype(bf16)
    rim_rows = places.next_rows(low_one[rows - TILE :])

    def quarter(x, cuts, *others):
        every, pieces = places.spread(x, p, *others)
        at = [
            (jnp.arange(high) * 4 + (p ^ m)) * 2 + core for core in (c, 1 - c) for m in range(4)
        ]
        return every, lay([*pieces[0], *pieces[1]], jnp.concatenate(at).astype(jnp.int32), cuts)

    small = jnp.concatenate(
        [
            jnp.stack([branch_bias, mixer_bias]),
            conv_taps.T,
            jnp.stack([conv_bias, decay_bias, input_bias, decay_param]),
            jnp.zeros((TILE - PARAM - 1, width), bf16),
            decay_weight.T,
            input_weight.T,
        ],
        axis=0,
    )
    total_dp = 8 * high
    share = -(-small.shape[0] // (total_dp * TILE)) * TILE
    small = jnp.pad(small, ((0, share * total_dp - small.shape[0]), (0, 0)))
    small = lax.dynamic_slice_in_dim(small, dp_at * share, share, 0)
    held = places.gather_rows_early(jnp.concatenate([rim_rows, low_one], axis=0))
    low_rows = jnp.concatenate([a[TILE:] for a in held], axis=0)
    rim_low = jnp.concatenate([a[:TILE] for a in held], axis=0)
    early, (mixer_own, small) = quarter(
        jnp.concatenate([mixer_weight, small], axis=0), (slab, share), held[2]
    )
    vectors = small[:TILE].astype(f32)
    gate_turned = small[TILE : TILE + 2 * block_width]
    middle, (branch_own, output_own) = quarter(
        after(jnp.concatenate([branch_weight, output_weight.T], axis=0), early, held[3]),
        (slab, slab),
    )
    param = vectors[PARAM]
    vec = jnp.concatenate(
        [vectors[:SLOPE], -DECAY * jax.nn.softplus(-param)[None], vectors[SLOPE + 1 :]], axis=0
    )
    block_of = jnp.arange(width, dtype=jnp.int32) // block_width
    same = block_of[:, None] == block_of[None, :]
    dense = jnp.concatenate(
        [
            jnp.where(same, jnp.tile(gate_turned[:block_width], (heads, 1)), 0),
            jnp.where(same, jnp.tile(gate_turned[block_width:], (heads, 1)), 0),
        ],
        axis=0,
    ).astype(bf16)

    channels = (plain(low_rows, mixer_own) + vec[MIXER_BIAS]).astype(bf16)
    rim = (plain(rim_low, mixer_own) + vec[MIXER_BIAS]).astype(bf16)
    grad_near = places.one(after(cotangent, mixer_own))
    channels = after(channels, grad_near).reshape(QUARTERS, rows, width)
    rim = rim.reshape(QUARTERS, TILE, width)
    conv_low, decays, state_local, reach = run_forward(info, channels, rim, vec, dense)
    grad_late = after(cotangent, conv_low)
    grad_held = (cotangent, grad_near, places.two(grad_late), places.flip_p(grad_late, 3))
    feed_grad = jnp.concatenate(grad_held, axis=0)
    gate_use = places.gather_rest(after(gate_weight.T, mixer_own))
    up_use = places.gather_rest(after(up_weight.T, mixer_own))
    down_use = places.gather_rest(after(down_weight, conv_low))
    branch_pre = plain(low_rows, branch_own) + vec[BRANCH_BIAS]

    def entering(parts, back):
        other = places.core(parts)
        pair = jnp.stack([parts, other])
        every = jnp.stack([pair] + [places.along_z(pair, k) for k in (1, 2, 3)])
        own, total = run_chain(spot, every, back)
        if high == 1:
            return own[:, 1:2], other
        held = [total]
        for _ in range(high - 1):
            held.append(places.along_h(held[-1]))
        state = jnp.zeros((1, width), f32)
        for hop in range(high - 1):
            source = high - 1 - hop if back else hop
            far = (h - source + high) % high
            picked = lax.dynamic_index_in_dim(jnp.stack(held), far, 0, False)
            ahead = source > h if back else source < h
            state = jnp.where(ahead, picked[0:1] * state + picked[1:2], state)
        return own[:, 1:2] + own[:, 0:1] * state[None], other

    enter, _ = entering(jnp.stack([reach[:, -1], state_local[:, -1]], axis=1), False)
    state_low = (state_local + reach * enter).astype(bf16).reshape(QUARTERS * rows, width)
    mixed_low = (jax.nn.gelu(branch_pre) * state_low.astype(f32)).astype(bf16)

    two_rows = 2 * rows
    mixed_low = after(mixed_low, grad_held[2], grad_held[3])
    resid_sum = places.scatter_rows_early(
        [trailing(mixed_low[k * rows : (k + 1) * rows], output_own) for k in range(QUARTERS)]
    )
    both_own = jnp.concatenate(
        [after(branch_own, mixed_low), after(mixer_own, mixed_low)], axis=1
    )
    pre_late = after(branch_pre, mixed_low)
    branch_act, gelu_back_one = jax.vjp(jax.nn.gelu, pre_late)
    branch_slope = gelu_back_one(state_low.astype(f32))[0]
    resid_sum, branch_act, branch_slope, both_own = lax.optimization_barrier(
        (resid_sum, branch_act, branch_slope, both_own)
    )
    resid = inputs + resid_sum

    rs_two, xs_two = normed(resid)
    low_two = (xs_two * gain_two).astype(bf16)
    feed_held = places.gather_rows(low_two)
    feed_rows = jnp.concatenate(feed_held, axis=0)
    gate_pre = trailing(feed_rows, gate_use)
    up_pre = trailing(feed_rows, up_use)
    gate_act, gelu_back_two = jax.vjp(jax.nn.gelu, gate_pre)
    hidden, gate_act, gate_slope = lax.optimization_barrier(
        ((gate_act * up_pre).astype(bf16), gate_act, gelu_back_two(up_pre)[0])
    )
    half = hidden.shape[1] // 2

    def columns(array, core):
        return lax.dynamic_slice_in_dim(array, core * half, half, 1)

    def column_far(grad, rows_in):
        return leading(columns(grad, 1 - c), rows_in).astype(bf16)

    def column_own(grad, rows_in, far):
        total = leading(columns(grad, c), rows_in) + places.core(far).astype(f32)
        return total.astype(bf16)

    def column_scatter(total):
        return lax.psum_scatter(total, "blk", scatter_dimension=0, tiled=True)

    def column_sum(total):
        if high > 1:
            total = total.reshape(high, -1, features)
            total = jnp.take(total, (h - jnp.arange(high)) % high, axis=0)
            total = places.scatter_high(total.reshape(-1, features))
        return total.astype(f32)

    down_far = column_far(hidden, feed_grad)
    down_own = column_own(hidden, feed_grad, down_far)
    down_scattered = column_scatter(down_own)
    hidden_grad = trailing(feed_grad, after(down_use, down_own))
    gate_grad = (hidden_grad * gate_slope).astype(bf16)
    up_grad = (hidden_grad * gate_act).astype(bf16)
    def norm_part(span):
        return plain(gate_grad[span], gate_use) + plain(up_grad[span], up_use)

    norm_far, norm_near = norm_part(slice(two_rows, None)), norm_part(slice(two_rows))
    norm_grad, _ = places.scatter_rows(norm_far, norm_near)
    gate_late, *_ = lax.optimization_barrier((gate_grad, norm_far, norm_near))
    gate_far = column_far(gate_late, feed_rows)
    norm_grad = after(norm_grad, gate_far)
    second_term = jnp.sum(norm_grad * xs_two, axis=0)
    resid_grad = cotangent.astype(f32) + norm_back(rs_two, xs_two, gain_two, norm_grad)

    resid_low = resid_grad.astype(bf16)
    resid_rows = jnp.concatenate(places.gather_rows(resid_low), axis=0)
    gate_last, up_late, hidden_last, _ = lax.optimization_barrier(
        (gate_late, up_grad, hidden, resid_low)
    )
    gate_own = column_own(gate_last, feed_rows, gate_far)
    gate_scattered = column_scatter(gate_own)
    up_far = column_far(up_late, feed_rows)
    output_far = plain(hidden_last[two_rows:], down_use)
    output_near = plain(hidden_last[:two_rows], down_use)
    resid_rows, output_far, output_near, *_ = lax.optimization_barrier(
        (resid_rows, output_far, output_near, up_far, gate_own, down_scattered)
    )
    output, output_joined = places.scatter_rows(output_far, output_near)
    output = (resid + output).astype(bf16)
    mixed_grad = plain(resid_rows, output_own)
    state_grad = (mixed_grad * branch_act).astype(bf16).reshape(QUARTERS, rows, width)
    branch_grad = (mixed_grad * branch_slope).astype(bf16)
    moved, span_back = run_reverse(decays, state_grad)
    leave, other = entering(jnp.stack([span_back[:, 0], moved[:, 0]], axis=1), True)
    up_last = after(up_late, other)
    resid_late, mixed_late, _ = lax.optimization_barrier((resid_rows, mixed_low, other))

    def quarter_half(term, *others):
        slab_in = term.shape[0] // total_dp
        term = term.astype(bf16).reshape(high * 4, 2 * slab_in, width)
        own = lax.dynamic_slice_in_dim(term, c * slab_in, slab_in, 1)
        other = lax.dynamic_slice_in_dim(term, (1 - c) * slab_in, slab_in, 1)
        came = places.core(other)
        half = own + after(came, *others)
        return half.reshape(high, 4, slab_in, width), other, came

    def quarter_rows(half):
        return [
            places.flip_p(lax.dynamic_index_in_dim(half, p ^ m, 1, False), m) for m in range(4)
        ]

    def quarter_high(total):
        if high > 1:
            total = jnp.take(total, (h - jnp.arange(high)) % high, axis=0)
            return places.scatter_high(total.reshape(-1, width))
        return total[0].astype(f32)

    def quarter_near(parts):
        stacked = jnp.stack(parts)

        def by(k):
            return lax.dynamic_index_in_dim(stacked, p ^ ((z + k) % 4), 0, False)

        total = by(0).astype(f32)
        for k in (1, 2, 3):
            total = total + places.along_z(by(k), k).astype(f32)
        return quarter_high(total)

    def quarter_far(parts, other):
        *parts, _ = lax.optimization_barrier((*parts, other))
        stacked = jnp.take(jnp.stack(parts), p ^ straight, axis=0)
        return quarter_high(lax.psum_scatter(stacked, "blk", scatter_dimension=0, tiled=True)[0])

    output_term = leading(resid_late, mixed_late)
    up_own = column_own(up_last, feed_rows, up_far)
    up_scattered = column_scatter(up_own)
    output_half, _, _ = quarter_half(output_term)
    leave, output_half, *_ = lax.optimization_barrier(
        (leave, output_half, output_joined, up_own, gate_scattered)
    )
    output_parts = quarter_rows(output_half)
    crossed, chan_grad, rim_grad, sums = run_backward(
        info, channels, rim, vec, dense, conv_low, state_local, reach, enter, state_grad, moved,
        span_back, leave,
    )

    low_late, branch_late, _ = lax.optimization_barrier((low_rows, branch_grad, rim_grad))
    branch_term = leading(low_late, branch_late)

    came = places.back_rows(rim_grad)
    last = (c == 1) & (z == 3)
    wanted = order + jnp.where(last, 1, 0)
    from_core = jnp.where(z == 3, 1 - c, c)
    offset = (wanted % 4) ^ p
    slot = jnp.where(from_core == 0, offset, (offset & 1) * 2 + offset // 2)
    pick = (slot[:, None] == straight[None, :]).astype(f32)
    here = jnp.where(wanted < 4, 1.0, 0.0)[:, None]

    def picked(select, array):
        return jnp.sum(select[:, :, None, None] * array[None], axis=1)

    returned = picked(pick * here, came)
    if high > 1:
        returned = returned + picked(pick * (1.0 - here), places.back_high(came))
    output_sum = quarter_far(output_parts, came).T
    chan_grad = chan_grad + jnp.pad(returned, ((0, 0), (rows - 8, 0), (0, 0)))
    mixer_grad = chan_grad.astype(bf16).reshape(QUARTERS * rows, width)

    picked_blocks = block_of[None, :] == jnp.arange(heads)[:, None]
    gate_terms = jnp.sum(
        jnp.where(picked_blocks[None, :, None, :], crossed.reshape(2, heads, block_width, width), 0),
        axis=1,
    )
    vector_terms = jnp.concatenate(
        [
            sums,
            jnp.sum(branch_grad.astype(f32), axis=0)[None],
            jnp.sum(mixer_grad.astype(f32), axis=0)[None],
            jnp.zeros((6, width), f32),
        ],
        axis=0,
    )
    slope_back = DECAY * jax.nn.sigmoid(-param)
    vector_terms = vector_terms.at[2].multiply(slope_back)
    small_terms = jnp.concatenate(
        [vector_terms, gate_terms.reshape(2 * block_width, width)], axis=0
    ).astype(bf16)
    small_terms = jnp.pad(small_terms, ((0, share * total_dp - small_terms.shape[0]), (0, 0)))
    branch_term, branch_both = lax.optimization_barrier((branch_term, branch_term.astype(bf16)))
    branch_both = jnp.concatenate(
        [branch_both.reshape(total_dp, slab, width), small_terms.reshape(total_dp, share, width)],
        axis=1,
    ).reshape(-1, width)
    mixer_term = leading(low_rows, mixer_grad)
    mixer_half, mixer_other, mixer_came = quarter_half(mixer_term)
    both_grads = jnp.concatenate([branch_grad, mixer_grad], axis=1)
    both_grads = after(both_grads, mixer_other)
    low_far = trailing(both_grads[two_rows:], both_own).astype(bf16)
    both_near, low_far, mixer_half, _ = lax.optimization_barrier(
        (both_grads[:two_rows], low_far, mixer_half, mixer_came)
    )
    branch_half, _, _ = quarter_half(after(branch_both, low_far))
    branch_parts = quarter_rows(branch_half)
    mixer_parts = quarter_rows(mixer_half)
    low_near = trailing(both_near, both_own)
    low_grad, low_joined = places.scatter_rows(low_far, low_near)
    branch_sum = quarter_far(branch_parts, low_near)
    mixer_sum = quarter_near(mixer_parts)
    mixer_term, second_term, _ = lax.optimization_barrier((mixer_term, second_term, low_grad))
    token_grad = (resid_grad + norm_back(rs_one, xs_one, gain_one, low_grad)).astype(bf16)

    first_term = (
        jnp.sum(branch_term * branch_own.astype(f32), axis=1)
        + jnp.sum(mixer_term * mixer_own.astype(f32), axis=1)
    ) / gain_one
    gain_sums = places.sum_all(jnp.stack([first_term, second_term]))

    branch_sum, small_sum = branch_sum[:slab], branch_sum[slab:]
    small_held = [small_sum]
    for _ in range(high - 1):
        small_held.append(places.along_h(small_held[-1]))
    small_held = jnp.stack(small_held)
    small_held = jnp.concatenate(places.gather_rows(small_held), axis=0)
    small_held = jnp.stack([small_held, places.core(small_held)])
    where = []
    for hh in range(high):
        for a in range(4):
            for core in range(2):
                offset = p ^ a
                crossed_at = (offset & 1) * 2 + offset // 2
                slot = offset if core == 0 else crossed_at
                where.append((((c ^ core) * 4 + slot) * high) + (h - hh + high) % high)
    small_total = jnp.take(
        small_held.reshape(-1, share, width), jnp.stack(where), axis=0
    ).reshape(-1, width)
    vector_total = small_total[:TILE]
    gate_total = small_total[TILE : TILE + 2 * block_width]
    gate_sum, up_sum = column_sum(gate_scattered).T, column_sum(up_scattered).T
    down_sum = column_sum(down_scattered)
    return (
        output,
        token_grad,
        branch_sum,
        mixer_sum,
        vector_total[8],
        vector_total[9],
        vector_total[4:8].T,
        vector_total[3],
        gate_total[:block_width].T,
        gate_total[block_width:].T,
        vector_total[0],
        vector_total[1],
        vector_total[2],
        output_sum,
        gain_sums[0],
        gain_sums[1],
        gate_sum,
        up_sum,
        down_sum,
    )


def solution(mesh):
    places = Places(mesh.shape["dp"], mesh.shape["blk"])
    return jax.shard_map(
        partial(body, places),
        mesh=mesh,
        in_specs=(
            P(("dp", "blk"), None),
            P(("dp", "blk"), None),
            P(),
            P("dp", "blk"),
            P("dp", "blk"),
            P("blk"),
            P("blk"),
            P("blk", None),
            P("blk"),
            P("blk", None),
            P("blk", None),
            P("blk"),
            P("blk"),
            P("blk"),
            P("blk", "dp"),
            P(),
            P(),
            P(None, ("dp", "blk")),
            P(None, ("dp", "blk")),
            P(("dp", "blk"), None),
        ),
        out_specs=(
            P(("dp", "blk"), None),
            P(("dp", "blk"), None),
            P("dp", "blk"),
            P("dp", "blk"),
            P("blk"),
            P("blk"),
            P("blk", None),
            P("blk"),
            P("blk", None),
            P("blk", None),
            P("blk"),
            P("blk"),
            P("blk"),
            P("blk", "dp"),
            P(),
            P(),
            P(None, ("dp", "blk")),
            P(None, ("dp", "blk")),
            P(("dp", "blk"), None),
        ),
        check_vma=False,
    )
```

```python
from functools import partial

import jax
import jax.numpy as jnp
from jax import lax
from jax.experimental import pallas as pl
from jax.experimental.pallas import tpu as pltpu
from jax.sharding import PartitionSpec as P

BUCKET_DP = 4
EPS = 1e-06
DECAY = 8.0
TAPS = 4
QUARTERS = 4
TILE = 16
AXES = ("dp", "blk")
f32 = jnp.float32
bf16 = jnp.bfloat16
VMEM_BYTES = 40 * 2**20

BRANCH_BIAS, MIXER_BIAS, TAP_ROW, CONV_BIAS, DECAY_BIAS, INPUT_BIAS, PARAM = 0, 1, 2, 6, 7, 8, 9
SLOPE = 10


def plain(former, latter):
    return jnp.dot(former, latter, preferred_element_type=f32)


def trailing(former, latter):
    return lax.dot_general(former, latter, (((1,), (1,)), ((), ())), preferred_element_type=f32)


def leading(former, latter):
    return lax.dot_general(former, latter, (((0,), (0,)), ((), ())), preferred_element_type=f32)


class Places:
    def __init__(self, dp, blk):
        assert blk == QUARTERS and dp % (2 * QUARTERS) == 0
        self.n = dp * blk
        self.high = dp // (2 * QUARTERS)

    @staticmethod
    def split(i):
        return i // 32, i // 8 % 4, i // 4 % 2, i % 4

    @staticmethod
    def join(h, p, c, z):
        return ((h * 4 + p) * 2 + c) * 4 + z

    def send(self, x, route):
        pairs = []
        for i in range(self.n):
            to = route(*self.split(i))
            if to is not None:
                pairs.append((i, self.join(*to)))
        return jax.tree.map(lambda a: lax.ppermute(a, AXES, pairs), x)

    def one(self, x):
        return self.send(x, lambda h, p, c, z: (h, p ^ (1 + c), c, z))

    def two(self, x):
        return self.send(x, lambda h, p, c, z: (h, p ^ (2 - c), c, z))

    def flip_p(self, x, bit):
        return x if bit == 0 else self.send(x, lambda h, p, c, z: (h, p ^ bit, c, z))

    def flip_z(self, x, bit):
        return self.send(x, lambda h, p, c, z: (h, p, c, z ^ bit))

    def core(self, x):
        return self.send(x, lambda h, p, c, z: (h, p, 1 - c, z))

    def along_z(self, x, by=1):
        return self.send(x, lambda h, p, c, z: (h, p, c, (z + by) % 4))

    def along_h(self, x):
        return self.send(x, lambda h, p, c, z: ((h + 1) % self.high, p, c, z))

    def next_rows(self, x):
        def route(*at):
            i = self.join(*at) + 1
            return self.split(i) if i < self.n else None

        return self.send(x, route)

    def back_rows(self, x):
        def route(h, p, c, z):
            i = (c * 4 + z + 7) % 8
            return h, p, i // 4, i % 4

        return self.send(x, route)

    def back_high(self, x):
        return self.send(x, lambda h, p, c, z: (h - 1, p, c, z) if h else None)

    def gather_rows(self, x):
        first = self.one(x)
        second = self.two(jnp.concatenate([x, first], axis=0))
        return x, first, second

    def gather_rows_early(self, x):
        first = self.one(x)
        second = self.two(x)
        return x, first, second, self.two(first)

    def scatter_rows(self, far, near):
        rows = near.shape[0] // 2
        came = self.two(far.astype(bf16))
        joined = (near[rows:] + came[rows:].astype(f32)).astype(bf16)
        return near[:rows] + came[:rows].astype(f32) + self.one(joined).astype(f32), joined

    def scatter_rows_early(self, parts):
        far = self.two(parts[3].astype(bf16))
        side = self.two(parts[2].astype(bf16))
        near = self.one((parts[1] + far.astype(f32)).astype(bf16))
        return parts[0] + side.astype(f32) + near.astype(f32)

    def spread(self, x, p, *others):
        groups = [
            [self.join(h, q, c, z) for h in range(self.high) for z in range(4)]
            for q in range(QUARTERS)
            for c in range(2)
        ]
        every = lax.all_gather(x, AXES, axis_index_groups=groups, axis=0, tiled=True)
        slab, width = x.shape

        def pick(m):
            if self.high == 1:
                return lax.dynamic_slice_in_dim(every, (p ^ m) * slab, slab, 0)[None]
            return lax.dynamic_index_in_dim(
                every.reshape(self.high, 4, slab, width), p ^ m, 1, False
            )

        own = [self.flip_p(pick(m), m) for m in range(4)]
        return every, [own, [self.core(after(a, *others)) for a in own]]

    def gather_rest(self, x, axis=0):
        groups = [
            [self.join(h, p, c, z) for c in range(2) for z in range(4) for h in range(self.high)]
            for p in range(QUARTERS)
        ]
        return lax.all_gather(x, AXES, axis_index_groups=groups, axis=axis, tiled=True)

    def scatter_high(self, x):
        if self.high == 1:
            return x
        rows = x.shape[0] // self.high
        piece = [x[k * rows : (k + 1) * rows] for k in range(self.high)]
        total = piece[1]
        for k in range(1, self.high):
            total = self.along_h(total.astype(bf16)).astype(f32) + piece[(k + 1) % self.high]
        return total

    def sum_all(self, x):
        x = x + self.core(x)
        x = x + self.flip_p(x, 1)
        x = x + self.flip_p(x, 2)
        x = x + self.flip_z(x, 1)
        x = x + self.flip_z(x, 2)
        total = x
        for _ in range(self.high - 1):
            x = self.along_h(x)
            total = total + x
        return total


def after(x, *others):
    return lax.optimization_barrier((x, *others))[0]


def swapped(offset):
    return (offset & 1) * 2 + offset // 2


LANES = 128


def wide(mask, width):
    mask = jnp.where(mask, 1.0, 0.0)
    return jnp.concatenate([mask] * (width // LANES), axis=1)


def place_rows(info, chunk, first, count):
    shape = (count, LANES)
    spot = info[chunk, 0] + first + lax.broadcasted_iota(jnp.int32, shape, 0)
    begin = jnp.zeros(shape, jnp.int32)
    for border in (1, 2, 3):
        begin = jnp.where(spot >= info[chunk, border], info[chunk, border], begin)
    return spot - begin, (spot >= 0) & (spot < info[chunk, 4])


def less_one(y):
    series = 1.0 + y * (1.0 / 6.0)
    for k in (5.0, 4.0, 3.0, 2.0):
        series = 1.0 + y * (1.0 / k) * series
    return jnp.where(y > -0.25, -y * series, 1.0 - jnp.exp(y))


def sigmoid(v):
    return 1.0 / (1.0 + jnp.exp(-v))


def scan_rows(a, b, back):
    rows = lax.broadcasted_iota(jnp.int32, a.shape, 0)
    count = a.shape[0]
    step = 1
    while step < count:
        by = count - step if back else step
        keep = rows < count - step if back else rows >= step
        b = jnp.where(keep, a * pltpu.roll(b, by, 0) + b, b)
        a = jnp.where(keep, a * pltpu.roll(a, by, 0), a)
        step *= 2
    return a, b


def forward_kernel(info, chan, rim, vec, dense, low, dec, state, reach, ext, pre):
    chunk = pl.program_id(0)
    rows, width = chan.shape[1:]
    ext[:TILE] = rim[0].astype(f32)
    ext[TILE:] = chan[0].astype(f32)

    def conv(t, _):
        base = pl.multiple_of(t * TILE, TILE)
        near = ext[pl.ds(base, 2 * TILE), :]
        seg, _filled = place_rows(info, chunk, base, TILE)
        total = jnp.broadcast_to(vec[CONV_BIAS : CONV_BIAS + 1, :], (TILE, width))
        for lag in range(TAPS):
            moved = near[TILE - lag : 2 * TILE - lag]
            tap = vec[TAP_ROW + lag : TAP_ROW + lag + 1, :]
            moved = tap * moved
            total = total + (wide(seg >= lag, width) * moved if lag else moved)
        low[0, pl.ds(base, TILE), :] = total.astype(bf16)
        return 0

    lax.fori_loop(0, rows // TILE, conv, 0, unroll=2)
    pre[...] = trailing(low[0], dense[...])

    def tile(t, held):
        base = pl.multiple_of(t * TILE, TILE)
        span = pl.ds(base, TILE)
        seg, filled = place_rows(info, chunk, base, TILE)
        open_decay = sigmoid(pre[span, :width] + vec[DECAY_BIAS : DECAY_BIAS + 1, :])
        open_input = sigmoid(pre[span, width:] + vec[INPUT_BIAS : INPUT_BIAS + 1, :])
        log_decay = open_decay * vec[SLOPE : SLOPE + 1, :]
        decay = wide((seg != 0) & filled, width) * jnp.exp(log_decay)
        factor = wide((seg == 0) & filled, width) + wide((seg != 0) & filled, width) * jnp.sqrt(
            less_one(2.0 * log_decay)
        )
        drive = factor * open_input * low[0, span, :].astype(f32)
        dec[0, span, :] = decay
        entered, passed = held
        for half in range(TILE // 8):
            part = slice(half * 8, half * 8 + 8)
            a, b = scan_rows(decay[part], drive[part], False)
            b = b + a * entered
            a = a * passed
            at = pl.ds(pl.multiple_of(base + half * 8, 8), 8)
            state[0, at, :] = b
            reach[0, at, :] = a
            entered, passed = b[7:8], a[7:8]
        return entered, passed

    lax.fori_loop(
        0,
        rows // TILE,
        tile,
        (jnp.zeros((1, width), f32), jnp.ones((1, width), f32)),
        unroll=2,
    )


def reverse_kernel(dec, grad, moved, reach):
    rows, width = dec.shape[1:]

    def tile(t, held):
        base = pl.multiple_of(rows - TILE - t * TILE, TILE)
        span = pl.ds(base, TILE)
        decay = dec[0, span, :]
        drive = decay * grad[0, span, :].astype(f32)
        entered, passed = held
        for half in reversed(range(TILE // 8)):
            part = slice(half * 8, half * 8 + 8)
            a, b = scan_rows(decay[part], drive[part], True)
            b = b + a * entered
            a = a * passed
            at = pl.ds(pl.multiple_of(base + half * 8, 8), 8)
            moved[0, at, :] = b
            reach[0, at, :] = a
            entered, passed = b[0:1], a[0:1]
        return entered, passed

    lax.fori_loop(
        0,
        rows // TILE,
        tile,
        (jnp.zeros((1, width), f32), jnp.ones((1, width), f32)),
        unroll=2,
    )


def chain_kernel(back, spot, parts, own, total, every):
    p, c, z = spot[0], spot[1], spot[2]
    factor = jnp.ones((1, own.shape[-1]), f32)
    term = jnp.zeros((1, own.shape[-1]), f32)
    count = 8 * QUARTERS
    for i in reversed(range(count)) if back else range(count):
        j, cc, zz = i // 8, i // 4 % 2, i % 4
        every[i, 0:1, :] = factor
        every[i, 1:2, :] = term
        offset = j ^ p
        slot = swapped(offset) if cc else offset
        pair = parts[(z - zz + 4) % 4, c ^ cc, slot]
        term = pair[0:1] * term + pair[1:2]
        factor = pair[0:1] * factor
    total[0:1, :] = factor
    total[1:2, :] = term
    for r in range(QUARTERS):
        j = p ^ jnp.where(c == 0, r, (r & 1) * 2 + r // 2)
        own[r] = every[(j * 2 + c) * 4 + z]


def backward_kernel(
    info, chan, rim, vec, dense, low, state, reach, enter, grad, moved, span_back, leave,
    crossed, chan_grad, rim_grad, sums,
    ext, pre, past, later, conv_grad, gates,
):
    chunk = pl.program_id(0)
    rows, width = chan.shape[1:]
    ext[:TILE] = rim[0].astype(f32)
    ext[TILE:] = chan[0].astype(f32)
    pre[...] = trailing(low[0], dense[...])
    past[0:TILE] = jnp.broadcast_to(enter[0], (TILE, width))
    later[rows : rows + TILE] = jnp.broadcast_to(leave[0], (TILE, width))
    conv_grad[:TILE] = jnp.zeros((TILE, width), f32)
    conv_grad[rows + TILE :] = jnp.zeros((TILE, width), f32)

    @pl.when(chunk == 0)
    def _():
        sums[...] = jnp.zeros_like(sums)
        crossed[...] = jnp.zeros_like(crossed)

    def fill(t, _):
        base = pl.multiple_of(t * TILE, TILE)
        span = pl.ds(base, TILE)
        past[pl.ds(pl.multiple_of(base + TILE, TILE), TILE), :] = (
            state[0, span, :] + reach[0, span, :] * enter[0]
        )
        later[span, :] = moved[0, span, :] + span_back[0, span, :] * leave[0]
        return 0

    lax.fori_loop(0, rows // TILE, fill, 0)

    def add(row, value):
        span = slice(row * 8, row * 8 + 8)
        for half in range(0, TILE, 8):
            sums[span, :] += value[half : half + 8]

    def tile(t, _):
        base = pl.multiple_of(t * TILE, TILE)
        span = pl.ds(base, TILE)
        seg, filled = place_rows(info, chunk, base, TILE)
        restart = wide((seg == 0) & filled, width)
        going = wide((seg != 0) & filled, width)
        before = past[pl.ds(base, 2 * TILE), :][TILE - 1 : 2 * TILE - 1]
        adjoint = grad[0, span, :].astype(f32) + later[pl.ds(base, 2 * TILE), :][1 : TILE + 1]
        open_decay = sigmoid(pre[span, :width] + vec[DECAY_BIAS : DECAY_BIAS + 1, :])
        open_input = sigmoid(pre[span, width:] + vec[INPUT_BIAS : INPUT_BIAS + 1, :])
        slope = vec[SLOPE : SLOPE + 1, :]
        log_decay = open_decay * slope
        decay = jnp.exp(log_decay)
        square = less_one(2.0 * log_decay)
        value = low[0, span, :].astype(f32)
        root = lax.rsqrt(square)
        root = jnp.where(going > 0.0, root, 0.0)
        opened = open_input * adjoint
        direct = (restart + square * root) * opened
        input_grad = direct * value * (1.0 - open_input)
        log_grad = going * decay * (adjoint * before - opened * value * decay * root)
        decay_grad = log_grad * slope * open_decay * (1.0 - open_decay)
        decay_low = decay_grad.astype(bf16)
        input_low = input_grad.astype(bf16)
        gates[span, :width] = decay_low
        gates[span, width:] = input_low
        conv_grad[pl.ds(pl.multiple_of(base + TILE, TILE), TILE), :] = direct
        add(0, decay_low.astype(f32))
        add(1, input_low.astype(f32))
        add(2, log_grad * open_decay)
        return 0

    lax.fori_loop(0, rows // TILE, tile, 0)
    conv_grad[TILE : rows + TILE] += plain(gates[...], dense[...])
    crossed[...] += leading(gates[...], low[0])

    def taps(t, _):
        base = pl.multiple_of(t * TILE, TILE)
        near = conv_grad[pl.ds(base, 2 * TILE), :]
        back = jnp.zeros((TILE, width), f32)
        for lag in range(TAPS):
            seg, _filled = place_rows(info, chunk, base - TILE + lag, TILE)
            tap = vec[TAP_ROW + lag : TAP_ROW + lag + 1, :] * near[lag : TILE + lag]
            back = back + (wide(seg >= lag, width) * tap if lag else tap)

        @pl.when(t == 0)
        def _():
            rim_grad[0] = back[TILE - 8 :]

        @pl.when(t > 0)
        def _():
            at = pl.multiple_of(base - TILE, TILE)
            chan_grad[0, pl.ds(at, TILE), :] = back
            around = ext[pl.ds(at, 2 * TILE), :]
            seg, _filled = place_rows(info, chunk, at, TILE)
            own = near[:TILE]
            add(3, own)
            for lag in range(TAPS):
                moved_in = around[TILE - lag : 2 * TILE - lag]
                moved_in = own * moved_in
                add(4 + lag, wide(seg >= lag, width) * moved_in if lag else moved_in)

        return 0

    lax.fori_loop(0, rows // TILE + 1, taps, 0)


def per_chunk(array):
    shape = array.shape
    return pl.BlockSpec((1, *shape[1:]), lambda i: (i,) + (0,) * (len(shape) - 1))


def whole(array):
    return pl.BlockSpec(array.shape, lambda i: (0,) * len(array.shape))


def in_smem():
    return pl.BlockSpec(memory_space=pltpu.SMEM)


def params():
    return pltpu.CompilerParams(vmem_limit_bytes=VMEM_BYTES)


def run_forward(info, chan, rim, vec, dense):
    count, rows, width = chan.shape
    shape = jax.ShapeDtypeStruct
    outs = [shape(chan.shape, bf16)] + [shape(chan.shape, f32)] * 3
    return pl.pallas_call(
        forward_kernel,
        grid=(count,),
        out_shape=outs,
        in_specs=[in_smem(), per_chunk(chan), per_chunk(rim), whole(vec), whole(dense)],
        out_specs=[per_chunk(o) for o in outs],
        scratch_shapes=[
            pltpu.VMEM((rows + TILE, width), f32),
            pltpu.VMEM((rows, 2 * width), f32),
        ],
        compiler_params=params(),
        cost_estimate=pl.CostEstimate(
            flops=4 * count * rows * width * width,
            bytes_accessed=count * rows * width * 84,
            transcendentals=count * rows * width * 5,
        ),
    )(info, chan, rim, vec, dense)


def run_reverse(dec, grad):
    count, rows, width = dec.shape
    outs = [jax.ShapeDtypeStruct(dec.shape, f32)] * 2
    return pl.pallas_call(
        reverse_kernel,
        grid=(count,),
        out_shape=outs,
        in_specs=[per_chunk(dec), per_chunk(grad)],
        out_specs=[per_chunk(o) for o in outs],
        compiler_params=params(),
        cost_estimate=pl.CostEstimate(
            flops=20 * count * rows * width,
            bytes_accessed=count * rows * width * 14,
            transcendentals=0,
        ),
    )(dec, grad)


def run_chain(spot, parts, back):
    width = parts.shape[-1]
    vmem = pl.BlockSpec(memory_space=pltpu.VMEM)
    return pl.pallas_call(
        partial(chain_kernel, back),
        out_shape=[
            jax.ShapeDtypeStruct((QUARTERS, 2, width), f32),
            jax.ShapeDtypeStruct((2, width), f32),
        ],
        in_specs=[in_smem(), vmem],
        out_specs=[vmem, vmem],
        scratch_shapes=[pltpu.VMEM((8 * QUARTERS, 2, width), f32)],
        compiler_params=params(),
    )(spot, parts)


def run_backward(info, chan, rim, vec, dense, low, state, reach, enter, grad, moved, span, leave):
    count, rows, width = chan.shape
    shape = jax.ShapeDtypeStruct
    outs = [
        shape((2 * width, width), f32),
        shape((count, rows, width), f32),
        shape((count, 8, width), f32),
        shape((64, width), f32),
    ]
    cut = [chan, rim, vec, dense, low, state, reach, enter, grad, moved, span, leave]
    specs = [whole(a) if a is vec or a is dense else per_chunk(a) for a in cut]
    return pl.pallas_call(
        backward_kernel,
        grid=(count,),
        out_shape=outs,
        in_specs=[in_smem(), *specs],
        out_specs=[whole(outs[0]), per_chunk(outs[1]), per_chunk(outs[2]), whole(outs[3])],
        scratch_shapes=[
            pltpu.VMEM((rows + TILE, width), f32),
            pltpu.VMEM((rows, 2 * width), f32),
            pltpu.VMEM((rows + TILE, width), f32),
            pltpu.VMEM((rows + TILE, width), f32),
            pltpu.VMEM((rows + 2 * TILE, width), f32),
            pltpu.VMEM((rows, 2 * width), bf16),
        ],
        compiler_params=params(),
        cost_estimate=pl.CostEstimate(
            flops=8 * count * rows * width * width,
            bytes_accessed=count * rows * width * 144,
            transcendentals=count * rows * width * 6,
        ),
    )(info, *cut)


def laid_kernel(cuts, at, *refs):
    pieces, outs = refs[: -len(cuts)], refs[-len(cuts) :]
    each = pieces[0].shape[0]
    for i, piece in enumerate(pieces):
        for k in range(each):
            first = 0
            for rows, out in zip(cuts, outs):
                to = pl.multiple_of(at[i * each + k] * rows, TILE)

                def move(t, _, piece=piece, k=k, to=to, first=first, out=out):
                    step = pl.multiple_of(t * TILE, TILE)
                    out[pl.ds(pl.multiple_of(to + step, TILE), TILE), :] = piece[
                        k, pl.ds(pl.multiple_of(first + step, TILE), TILE), :
                    ]
                    return 0

                lax.fori_loop(0, rows // TILE, move, 0)
                first += rows


def lay(pieces, at, cuts):
    count = at.shape[0]
    width = pieces[0].shape[-1]
    vmem = pl.BlockSpec(memory_space=pltpu.VMEM)
    return pl.pallas_call(
        partial(laid_kernel, cuts),
        out_shape=[jax.ShapeDtypeStruct((count * rows, width), pieces[0].dtype) for rows in cuts],
        in_specs=[in_smem(), *[vmem for _ in pieces]],
        out_specs=[vmem for _ in cuts],
        compiler_params=params(),
        cost_estimate=pl.CostEstimate(
            flops=0, bytes_accessed=4 * count * sum(cuts) * width, transcendentals=0
        ),
    )(at, *pieces)


def normed(values):
    rs = lax.rsqrt(jnp.mean(values * values, axis=-1, keepdims=True) + EPS)
    return rs, values * rs


def norm_back(rs, xs, gain, grad):
    scaled = gain * grad
    return rs * (scaled - xs * jnp.mean(xs * scaled, axis=-1, keepdims=True))


def body(
    places,
    tokens,
    cotangent,
    lengths,
    branch_weight,
    mixer_weight,
    branch_bias,
    mixer_bias,
    conv_taps,
    conv_bias,
    decay_weight,
    input_weight,
    decay_bias,
    input_bias,
    decay_param,
    output_weight,
    first_gain,
    second_gain,
    gate_weight,
    up_weight,
    down_weight,
):
    rows, features = tokens.shape
    slab, width = mixer_weight.shape
    block_width = decay_weight.shape[1]
    heads = width // block_width
    high = places.high
    dp_at, z = lax.axis_index("dp"), lax.axis_index("blk")
    h, p, c = dp_at // 8, dp_at // 2 % 4, dp_at % 2
    spot = jnp.stack([p, c, z]).astype(jnp.int32)

    straight = jnp.arange(QUARTERS, dtype=jnp.int32)
    order = p ^ jnp.where(c == 0, straight, (straight & 1) * 2 + straight // 2)
    chunk = ((h * 4 + order) * 2 + c) * 4 + z
    bucket_rows = BUCKET_DP * QUARTERS * rows
    start = chunk * rows
    bucket = (start + bucket_rows // 2) // bucket_rows
    begin = jnp.maximum(0, bucket * bucket_rows - bucket_rows // 2)
    ends = jnp.cumsum(jnp.take(lengths, bucket, axis=0), axis=1)
    info = jnp.concatenate([(start - begin)[:, None], ends], axis=1).astype(jnp.int32)

    inputs = tokens.astype(f32)
    gain_one, gain_two = first_gain.astype(f32), second_gain.astype(f32)
    rs_one, xs_one = normed(inputs)
    low_one = (xs_one * gain_one).astype(bf16)
    rim_rows = places.next_rows(low_one[rows - TILE :])

    def quarter(x, cuts, *others):
        every, pieces = places.spread(x, p, *others)
        at = [
            (jnp.arange(high) * 4 + (p ^ m)) * 2 + core for core in (c, 1 - c) for m in range(4)
        ]
        return every, lay([*pieces[0], *pieces[1]], jnp.concatenate(at).astype(jnp.int32), cuts)

    small = jnp.concatenate(
        [
            jnp.stack([branch_bias, mixer_bias]),
            conv_taps.T,
            jnp.stack([conv_bias, decay_bias, input_bias, decay_param]),
            jnp.zeros((TILE - PARAM - 1, width), bf16),
            decay_weight.T,
            input_weight.T,
        ],
        axis=0,
    )
    total_dp = 8 * high
    share = -(-small.shape[0] // (total_dp * TILE)) * TILE
    small = jnp.pad(small, ((0, share * total_dp - small.shape[0]), (0, 0)))
    small = lax.dynamic_slice_in_dim(small, dp_at * share, share, 0)
    held = places.gather_rows_early(jnp.concatenate([rim_rows, low_one], axis=0))
    low_rows = jnp.concatenate([a[TILE:] for a in held], axis=0)
    rim_low = jnp.concatenate([a[:TILE] for a in held], axis=0)
    early, (mixer_own, small) = quarter(
        jnp.concatenate([mixer_weight, small], axis=0), (slab, share), held[2]
    )
    vectors = small[:TILE].astype(f32)
    gate_turned = small[TILE : TILE + 2 * block_width]
    middle, (branch_own, output_own) = quarter(
        after(jnp.concatenate([branch_weight, output_weight.T], axis=0), early, held[3]),
        (slab, slab),
    )
    param = vectors[PARAM]
    vec = jnp.concatenate(
        [vectors[:SLOPE], -DECAY * jax.nn.softplus(-param)[None], vectors[SLOPE + 1 :]], axis=0
    )
    block_of = jnp.arange(width, dtype=jnp.int32) // block_width
    same = block_of[:, None] == block_of[None, :]
    dense = jnp.concatenate(
        [
            jnp.where(same, jnp.tile(gate_turned[:block_width], (heads, 1)), 0),
            jnp.where(same, jnp.tile(gate_turned[block_width:], (heads, 1)), 0),
        ],
        axis=0,
    ).astype(bf16)

    channels = (plain(low_rows, mixer_own) + vec[MIXER_BIAS]).astype(bf16)
    rim = (plain(rim_low, mixer_own) + vec[MIXER_BIAS]).astype(bf16)
    grad_near = places.one(after(cotangent, mixer_own))
    channels = after(channels, grad_near).reshape(QUARTERS, rows, width)
    rim = rim.reshape(QUARTERS, TILE, width)
    conv_low, decays, state_local, reach = run_forward(info, channels, rim, vec, dense)
    grad_late = after(cotangent, conv_low)
    grad_held = (cotangent, grad_near, places.two(grad_late), places.flip_p(grad_late, 3))
    feed_grad = jnp.concatenate(grad_held, axis=0)
    gate_use = places.gather_rest(after(gate_weight.T, mixer_own))
    up_use = places.gather_rest(after(up_weight.T, mixer_own))
    down_use = places.gather_rest(after(down_weight, conv_low))
    branch_pre = plain(low_rows, branch_own) + vec[BRANCH_BIAS]

    def entering(parts, back):
        other = places.core(parts)
        pair = jnp.stack([parts, other])
        every = jnp.stack([pair] + [places.along_z(pair, k) for k in (1, 2, 3)])
        own, total = run_chain(spot, every, back)
        if high == 1:
            return own[:, 1:2], other
        held = [total]
        for _ in range(high - 1):
            held.append(places.along_h(held[-1]))
        state = jnp.zeros((1, width), f32)
        for hop in range(high - 1):
            source = high - 1 - hop if back else hop
            far = (h - source + high) % high
            picked = lax.dynamic_index_in_dim(jnp.stack(held), far, 0, False)
            ahead = source > h if back else source < h
            state = jnp.where(ahead, picked[0:1] * state + picked[1:2], state)
        return own[:, 1:2] + own[:, 0:1] * state[None], other

    enter, _ = entering(jnp.stack([reach[:, -1], state_local[:, -1]], axis=1), False)
    state_low = (state_local + reach * enter).astype(bf16).reshape(QUARTERS * rows, width)
    mixed_low = (jax.nn.gelu(branch_pre) * state_low.astype(f32)).astype(bf16)

    two_rows = 2 * rows
    mixed_low = after(mixed_low, grad_held[2], grad_held[3])
    resid_sum = places.scatter_rows_early(
        [trailing(mixed_low[k * rows : (k + 1) * rows], output_own) for k in range(QUARTERS)]
    )
    both_own = jnp.concatenate(
        [after(branch_own, mixed_low), after(mixer_own, mixed_low)], axis=1
    )
    pre_late = after(branch_pre, mixed_low)
    branch_act, gelu_back_one = jax.vjp(jax.nn.gelu, pre_late)
    branch_slope = gelu_back_one(state_low.astype(f32))[0]
    resid_sum, branch_act, branch_slope, both_own = lax.optimization_barrier(
        (resid_sum, branch_act, branch_slope, both_own)
    )
    resid = inputs + resid_sum

    rs_two, xs_two = normed(resid)
    low_two = (xs_two * gain_two).astype(bf16)
    feed_held = places.gather_rows(low_two)
    feed_rows = jnp.concatenate(feed_held, axis=0)
    gate_pre = trailing(feed_rows, gate_use)
    up_pre = trailing(feed_rows, up_use)
    gate_act, gelu_back_two = jax.vjp(jax.nn.gelu, gate_pre)
    hidden, gate_act, gate_slope = lax.optimization_barrier(
        (
            (gate_act * up_pre).astype(bf16),
            gate_act.astype(bf16),
            gelu_back_two(up_pre)[0].astype(bf16),
        )
    )
    half = hidden.shape[1] // 2

    def columns(array, core):
        return lax.dynamic_slice_in_dim(array, core * half, half, 1)

    def column_far(grad, rows_in):
        return leading(columns(grad, 1 - c), rows_in).astype(bf16)

    def column_own(grad, rows_in, far):
        total = leading(columns(grad, c), rows_in) + places.core(far).astype(f32)
        return total.astype(bf16)

    def column_scatter(total):
        return lax.psum_scatter(total, "blk", scatter_dimension=0, tiled=True)

    def column_sum(total):
        if high > 1:
            total = total.reshape(high, -1, features)
            total = jnp.take(total, (h - jnp.arange(high)) % high, axis=0)
            total = places.scatter_high(total.reshape(-1, features))
        return total.astype(f32)

    down_far = column_far(hidden, feed_grad)
    hidden_grad = trailing(feed_grad, after(down_use, down_far))
    gate_grad = (hidden_grad * gate_slope.astype(f32)).astype(bf16)
    up_grad = (hidden_grad * gate_act.astype(f32)).astype(bf16)
    def norm_part(span):
        return plain(gate_grad[span], gate_use) + plain(up_grad[span], up_use)

    norm_far = norm_part(slice(two_rows, None)).astype(bf16)
    gate_grad, up_grad, hidden_late, norm_far = lax.optimization_barrier(
        (gate_grad, up_grad, hidden, norm_far)
    )
    down_own = column_own(hidden_late, feed_grad, down_far)
    down_scattered = column_scatter(down_own)
    norm_near = norm_part(slice(two_rows))
    norm_grad, _ = places.scatter_rows(norm_far, norm_near)
    gate_late, *_ = lax.optimization_barrier((gate_grad, norm_near, down_own))
    gate_far = column_far(gate_late, feed_rows)
    norm_grad = after(norm_grad, gate_far)
    second_term = jnp.sum(norm_grad * xs_two, axis=0)
    resid_grad = cotangent.astype(f32) + norm_back(rs_two, xs_two, gain_two, norm_grad)

    resid_low = resid_grad.astype(bf16)
    resid_rows = jnp.concatenate(places.gather_rows(resid_low), axis=0)
    gate_last, up_late, hidden_last, _ = lax.optimization_barrier(
        (gate_late, up_grad, hidden, resid_low)
    )
    gate_own = column_own(gate_last, feed_rows, gate_far)
    gate_scattered = column_scatter(gate_own)
    up_far = column_far(up_late, feed_rows)
    output_far = plain(hidden_last[two_rows:], down_use)
    output_near = plain(hidden_last[:two_rows], down_use)
    resid_rows, output_far, output_near, *_ = lax.optimization_barrier(
        (resid_rows, output_far, output_near, up_far, gate_own, down_scattered)
    )
    output, output_joined = places.scatter_rows(output_far, output_near)
    output = (resid + output).astype(bf16)
    mixed_grad = plain(resid_rows, output_own)
    state_grad = (mixed_grad * branch_act).astype(bf16).reshape(QUARTERS, rows, width)
    branch_grad = (mixed_grad * branch_slope).astype(bf16)
    moved, span_back = run_reverse(decays, state_grad)
    leave, other = entering(jnp.stack([span_back[:, 0], moved[:, 0]], axis=1), True)
    up_last = after(up_late, other)
    resid_late, mixed_late, _ = lax.optimization_barrier((resid_rows, mixed_low, other))

    def quarter_half(term, *others):
        slab_in = term.shape[0] // total_dp
        term = term.astype(bf16).reshape(high * 4, 2 * slab_in, width)
        own = lax.dynamic_slice_in_dim(term, c * slab_in, slab_in, 1)
        other = lax.dynamic_slice_in_dim(term, (1 - c) * slab_in, slab_in, 1)
        came = places.core(other)
        half = own + after(came, *others)
        return half.reshape(high, 4, slab_in, width), other, came

    def quarter_rows(half):
        return [
            places.flip_p(lax.dynamic_index_in_dim(half, p ^ m, 1, False), m) for m in range(4)
        ]

    def quarter_high(total):
        if high > 1:
            total = jnp.take(total, (h - jnp.arange(high)) % high, axis=0)
            return places.scatter_high(total.reshape(-1, width))
        return total[0].astype(f32)

    def quarter_near(parts):
        stacked = jnp.stack(parts)

        def by(k):
            return lax.dynamic_index_in_dim(stacked, p ^ ((z + k) % 4), 0, False)

        came = [places.along_z(by(k), k) for k in (1, 2, 3)]
        total = by(0).astype(f32)
        for a in came:
            total = total + a.astype(f32)
        return quarter_high(total), came

    def quarter_far(parts, other):
        *parts, _ = lax.optimization_barrier((*parts, other))
        stacked = jnp.take(jnp.stack(parts), p ^ straight, axis=0)
        return quarter_high(lax.psum_scatter(stacked, "blk", scatter_dimension=0, tiled=True)[0])

    output_term = leading(resid_late, mixed_late)
    up_own = column_own(up_last, feed_rows, up_far)
    up_scattered = column_scatter(up_own)
    output_half, _, _ = quarter_half(output_term)
    leave, output_half, *_ = lax.optimization_barrier(
        (leave, output_half, output_joined, up_own, gate_scattered)
    )
    output_parts = quarter_rows(output_half)
    crossed, chan_grad, rim_grad, sums8 = run_backward(
        info, channels, rim, vec, dense, conv_low, state_local, reach, enter, state_grad, moved,
        span_back, leave,
    )

    low_late, branch_late, _ = lax.optimization_barrier((low_rows, branch_grad, rim_grad))
    branch_term = leading(low_late, branch_late)

    came = places.back_rows(rim_grad)
    last = (c == 1) & (z == 3)
    wanted = order + jnp.where(last, 1, 0)
    from_core = jnp.where(z == 3, 1 - c, c)
    offset = (wanted % 4) ^ p
    slot = jnp.where(from_core == 0, offset, (offset & 1) * 2 + offset // 2)
    pick = (slot[:, None] == straight[None, :]).astype(f32)
    here = jnp.where(wanted < 4, 1.0, 0.0)[:, None]

    def picked(select, array):
        return jnp.sum(select[:, :, None, None] * array[None], axis=1)

    returned = picked(pick * here, came)
    if high > 1:
        returned = returned + picked(pick * (1.0 - here), places.back_high(came))
    output_sum = quarter_far(output_parts, came).T
    chan_grad = chan_grad + jnp.pad(returned, ((0, 0), (rows - 8, 0), (0, 0)))
    mixer_grad = chan_grad.astype(bf16).reshape(QUARTERS * rows, width)

    picked_blocks = block_of[None, :] == jnp.arange(heads)[:, None]
    gate_terms = jnp.sum(
        jnp.where(picked_blocks[None, :, None, :], crossed.reshape(2, heads, block_width, width), 0),
        axis=1,
    )
    vector_terms = jnp.concatenate(
        [
            jnp.sum(sums8.reshape(8, 8, width), axis=1),
            jnp.sum(branch_grad.astype(f32), axis=0)[None],
            jnp.sum(mixer_grad.astype(f32), axis=0)[None],
            jnp.zeros((6, width), f32),
        ],
        axis=0,
    )
    slope_back = DECAY * jax.nn.sigmoid(-param)
    vector_terms = vector_terms.at[2].multiply(slope_back)
    small_terms = jnp.concatenate(
        [vector_terms, gate_terms.reshape(2 * block_width, width)], axis=0
    ).astype(bf16)
    small_terms = jnp.pad(small_terms, ((0, share * total_dp - small_terms.shape[0]), (0, 0)))
    branch_term, branch_both = lax.optimization_barrier((branch_term, branch_term.astype(bf16)))
    branch_both = jnp.concatenate(
        [branch_both.reshape(total_dp, slab, width), small_terms.reshape(total_dp, share, width)],
        axis=1,
    ).reshape(-1, width)
    mixer_term = leading(low_rows, mixer_grad)
    mixer_half, mixer_other, mixer_came = quarter_half(mixer_term)
    both_grads = jnp.concatenate([branch_grad, mixer_grad], axis=1)
    both_grads = after(both_grads, mixer_other)
    low_far = trailing(both_grads[two_rows:], both_own).astype(bf16)
    both_near, low_far, mixer_half, _ = lax.optimization_barrier(
        (both_grads[:two_rows], low_far, mixer_half, mixer_came)
    )
    branch_half, _, _ = quarter_half(after(branch_both, low_far, up_scattered))
    branch_parts = quarter_rows(branch_half)
    mixer_parts = quarter_rows(mixer_half)
    low_near = trailing(both_near, both_own)
    low_grad, low_joined = places.scatter_rows(low_far, low_near)
    branch_sum = quarter_far(branch_parts, low_near)
    mixer_sum, mixer_last = quarter_near(mixer_parts)
    mixer_term, second_term, _ = lax.optimization_barrier((mixer_term, second_term, low_grad))
    low_grad = after(low_grad, *mixer_last)
    token_grad = (resid_grad + norm_back(rs_one, xs_one, gain_one, low_grad)).astype(bf16)

    first_term = (
        jnp.sum(branch_term * branch_own.astype(f32), axis=1)
        + jnp.sum(mixer_term * mixer_own.astype(f32), axis=1)
    ) / gain_one
    gain_sums = places.sum_all(jnp.stack([first_term, second_term]))

    branch_sum, small_sum = branch_sum[:slab], branch_sum[slab:]
    small_held = [small_sum]
    for _ in range(high - 1):
        small_held.append(places.along_h(small_held[-1]))
    small_held = jnp.stack(small_held)
    small_held = jnp.concatenate(places.gather_rows(small_held), axis=0)
    small_held = jnp.stack([small_held, places.core(small_held)])
    where = []
    for hh in range(high):
        for a in range(4):
            for core in range(2):
                offset = p ^ a
                crossed_at = (offset & 1) * 2 + offset // 2
                slot = offset if core == 0 else crossed_at
                where.append((((c ^ core) * 4 + slot) * high) + (h - hh + high) % high)
    small_total = jnp.take(
        small_held.reshape(-1, share, width), jnp.stack(where), axis=0
    ).reshape(-1, width)
    vector_total = small_total[:TILE]
    gate_total = small_total[TILE : TILE + 2 * block_width]
    gate_sum, up_sum = column_sum(gate_scattered).T, column_sum(up_scattered).T
    down_sum = column_sum(down_scattered)
    return (
        output,
        token_grad,
        branch_sum,
        mixer_sum,
        vector_total[8],
        vector_total[9],
        vector_total[4:8].T,
        vector_total[3],
        gate_total[:block_width].T,
        gate_total[block_width:].T,
        vector_total[0],
        vector_total[1],
        vector_total[2],
        output_sum,
        gain_sums[0],
        gain_sums[1],
        gate_sum,
        up_sum,
        down_sum,
    )


def solution(mesh):
    places = Places(mesh.shape["dp"], mesh.shape["blk"])
    return jax.shard_map(
        partial(body, places),
        mesh=mesh,
        in_specs=(
            P(("dp", "blk"), None),
            P(("dp", "blk"), None),
            P(),
            P("dp", "blk"),
            P("dp", "blk"),
            P("blk"),
            P("blk"),
            P("blk", None),
            P("blk"),
            P("blk", None),
            P("blk", None),
            P("blk"),
            P("blk"),
            P("blk"),
            P("blk", "dp"),
            P(),
            P(),
            P(None, ("dp", "blk")),
            P(None, ("dp", "blk")),
            P(("dp", "blk"), None),
        ),
        out_specs=(
            P(("dp", "blk"), None),
            P(("dp", "blk"), None),
            P("dp", "blk"),
            P("dp", "blk"),
            P("blk"),
            P("blk"),
            P("blk", None),
            P("blk"),
            P("blk", None),
            P("blk", None),
            P("blk"),
            P("blk"),
            P("blk"),
            P("blk", "dp"),
            P(),
            P(),
            P(None, ("dp", "blk")),
            P(None, ("dp", "blk")),
            P(("dp", "blk"), None),
        ),
        check_vma=False,
    )
```

```python
from functools import partial

import jax
import jax.numpy as jnp
from jax import lax
from jax.experimental import pallas as pl
from jax.experimental.pallas import tpu as pltpu
from jax.sharding import PartitionSpec as P

BUCKET_DP = 4
EPS = 1e-06
DECAY = 8.0
TAPS = 4
QUARTERS = 4
TILE = 16
AXES = ("dp", "blk")
f32 = jnp.float32
bf16 = jnp.bfloat16
VMEM_BYTES = 40 * 2**20

BRANCH_BIAS, MIXER_BIAS, TAP_ROW, CONV_BIAS, DECAY_BIAS, INPUT_BIAS, PARAM = 0, 1, 2, 6, 7, 8, 9
SLOPE = 10


def plain(former, latter):
    return jnp.dot(former, latter, preferred_element_type=f32)


def trailing(former, latter):
    return lax.dot_general(former, latter, (((1,), (1,)), ((), ())), preferred_element_type=f32)


def leading(former, latter):
    return lax.dot_general(former, latter, (((0,), (0,)), ((), ())), preferred_element_type=f32)


class Places:
    def __init__(self, dp, blk):
        assert blk == QUARTERS and dp % (2 * QUARTERS) == 0
        self.n = dp * blk
        self.high = dp // (2 * QUARTERS)

    @staticmethod
    def split(i):
        return i // 32, i // 8 % 4, i // 4 % 2, i % 4

    @staticmethod
    def join(h, p, c, z):
        return ((h * 4 + p) * 2 + c) * 4 + z

    def send(self, x, route):
        pairs = []
        for i in range(self.n):
            to = route(*self.split(i))
            if to is not None:
                pairs.append((i, self.join(*to)))
        return jax.tree.map(lambda a: lax.ppermute(a, AXES, pairs), x)

    def one(self, x):
        return self.send(x, lambda h, p, c, z: (h, p ^ (1 + c), c, z))

    def two(self, x):
        return self.send(x, lambda h, p, c, z: (h, p ^ (2 - c), c, z))

    def flip_p(self, x, bit):
        return x if bit == 0 else self.send(x, lambda h, p, c, z: (h, p ^ bit, c, z))

    def flip_z(self, x, bit):
        return self.send(x, lambda h, p, c, z: (h, p, c, z ^ bit))

    def core(self, x):
        return self.send(x, lambda h, p, c, z: (h, p, 1 - c, z))

    def along_z(self, x, by=1):
        return self.send(x, lambda h, p, c, z: (h, p, c, (z + by) % 4))

    def along_h(self, x):
        return self.send(x, lambda h, p, c, z: ((h + 1) % self.high, p, c, z))

    def next_rows(self, x):
        def route(*at):
            i = self.join(*at) + 1
            return self.split(i) if i < self.n else None

        return self.send(x, route)

    def back_rows(self, x):
        def route(h, p, c, z):
            i = (c * 4 + z + 7) % 8
            return h, p, i // 4, i % 4

        return self.send(x, route)

    def back_high(self, x):
        return self.send(x, lambda h, p, c, z: (h - 1, p, c, z) if h else None)

    def gather_rows(self, x):
        first = self.one(x)
        second = self.two(jnp.concatenate([x, first], axis=0))
        return x, first, second

    def gather_rows_early(self, x):
        first = self.one(x)
        second = self.two(x)
        return x, first, second, self.two(first)

    def scatter_rows(self, far, near):
        rows = near.shape[0] // 2
        came = self.two(far.astype(bf16))
        joined = (near[rows:] + came[rows:].astype(f32)).astype(bf16)
        return near[:rows] + came[:rows].astype(f32) + self.one(joined).astype(f32), joined

    def scatter_rows_early(self, parts):
        far = self.two(parts[3].astype(bf16))
        side = self.two(parts[2].astype(bf16))
        near = self.one((parts[1] + far.astype(f32)).astype(bf16))
        return parts[0] + side.astype(f32) + near.astype(f32)

    def spread(self, x, p, *others):
        groups = [
            [self.join(h, q, c, z) for h in range(self.high) for z in range(4)]
            for q in range(QUARTERS)
            for c in range(2)
        ]
        every = lax.all_gather(x, AXES, axis_index_groups=groups, axis=0, tiled=True)
        slab, width = x.shape

        def pick(m):
            if self.high == 1:
                return lax.dynamic_slice_in_dim(every, (p ^ m) * slab, slab, 0)[None]
            return lax.dynamic_index_in_dim(
                every.reshape(self.high, 4, slab, width), p ^ m, 1, False
            )

        own = [self.flip_p(pick(m), m) for m in range(4)]
        return every, [own, [self.core(after(a, *others)) for a in own]]

    def gather_rest(self, x, axis=0):
        groups = [
            [self.join(h, p, c, z) for c in range(2) for z in range(4) for h in range(self.high)]
            for p in range(QUARTERS)
        ]
        return lax.all_gather(x, AXES, axis_index_groups=groups, axis=axis, tiled=True)

    def scatter_high(self, x):
        if self.high == 1:
            return x
        rows = x.shape[0] // self.high
        piece = [x[k * rows : (k + 1) * rows] for k in range(self.high)]
        total = piece[1]
        for k in range(1, self.high):
            total = self.along_h(total.astype(bf16)).astype(f32) + piece[(k + 1) % self.high]
        return total

    def sum_all(self, x):
        x = x + self.core(x)
        x = x + self.flip_p(x, 1)
        x = x + self.flip_p(x, 2)
        x = x + self.flip_z(x, 1)
        x = x + self.flip_z(x, 2)
        total = x
        for _ in range(self.high - 1):
            x = self.along_h(x)
            total = total + x
        return total


def after(x, *others):
    return lax.optimization_barrier((x, *others))[0]


def swapped(offset):
    return (offset & 1) * 2 + offset // 2


LANES = 128


def wide(mask, width):
    mask = jnp.where(mask, 1.0, 0.0)
    return jnp.concatenate([mask] * (width // LANES), axis=1)


def place_rows(info, chunk, first, count):
    shape = (count, LANES)
    spot = info[chunk, 0] + first + lax.broadcasted_iota(jnp.int32, shape, 0)
    begin = jnp.zeros(shape, jnp.int32)
    for border in (1, 2, 3):
        begin = jnp.where(spot >= info[chunk, border], info[chunk, border], begin)
    return spot - begin, (spot >= 0) & (spot < info[chunk, 4])


def less_one(y):
    series = 1.0 + y * (1.0 / 6.0)
    for k in (5.0, 4.0, 3.0, 2.0):
        series = 1.0 + y * (1.0 / k) * series
    return jnp.where(y > -0.25, -y * series, 1.0 - jnp.exp(y))


def sigmoid(v):
    return 1.0 / (1.0 + jnp.exp(-v))


def scan_rows(a, b, back):
    rows = lax.broadcasted_iota(jnp.int32, a.shape, 0)
    count = a.shape[0]
    step = 1
    while step < count:
        by = count - step if back else step
        keep = rows < count - step if back else rows >= step
        b = jnp.where(keep, a * pltpu.roll(b, by, 0) + b, b)
        a = jnp.where(keep, a * pltpu.roll(a, by, 0), a)
        step *= 2
    return a, b


def forward_kernel(info, chan, rim, vec, dense, low, dec, state, reach, ext, pre):
    chunk = pl.program_id(0)
    rows, width = chan.shape[1:]
    ext[:TILE] = rim[0].astype(f32)
    ext[TILE:] = chan[0].astype(f32)

    def conv(t, _):
        base = pl.multiple_of(t * TILE, TILE)
        near = ext[pl.ds(base, 2 * TILE), :]
        seg, _filled = place_rows(info, chunk, base, TILE)
        total = jnp.broadcast_to(vec[CONV_BIAS : CONV_BIAS + 1, :], (TILE, width))
        for lag in range(TAPS):
            moved = near[TILE - lag : 2 * TILE - lag]
            tap = vec[TAP_ROW + lag : TAP_ROW + lag + 1, :]
            moved = tap * moved
            total = total + (wide(seg >= lag, width) * moved if lag else moved)
        low[0, pl.ds(base, TILE), :] = total.astype(bf16)
        return 0

    lax.fori_loop(0, rows // TILE, conv, 0, unroll=2)
    pre[...] = trailing(low[0], dense[...])

    def tile(t, held):
        base = pl.multiple_of(t * TILE, TILE)
        span = pl.ds(base, TILE)
        seg, filled = place_rows(info, chunk, base, TILE)
        open_decay = sigmoid(pre[span, :width] + vec[DECAY_BIAS : DECAY_BIAS + 1, :])
        open_input = sigmoid(pre[span, width:] + vec[INPUT_BIAS : INPUT_BIAS + 1, :])
        log_decay = open_decay * vec[SLOPE : SLOPE + 1, :]
        decay = wide((seg != 0) & filled, width) * jnp.exp(log_decay)
        factor = wide((seg == 0) & filled, width) + wide((seg != 0) & filled, width) * jnp.sqrt(
            less_one(2.0 * log_decay)
        )
        drive = factor * open_input * low[0, span, :].astype(f32)
        dec[0, span, :] = decay
        entered, passed = held
        for half in range(TILE // 8):
            part = slice(half * 8, half * 8 + 8)
            a, b = scan_rows(decay[part], drive[part], False)
            b = b + a * entered
            a = a * passed
            at = pl.ds(pl.multiple_of(base + half * 8, 8), 8)
            state[0, at, :] = b
            reach[0, at, :] = a
            entered, passed = b[7:8], a[7:8]
        return entered, passed

    lax.fori_loop(
        0,
        rows // TILE,
        tile,
        (jnp.zeros((1, width), f32), jnp.ones((1, width), f32)),
        unroll=2,
    )


def reverse_kernel(dec, grad, moved, reach):
    rows, width = dec.shape[1:]

    def tile(t, held):
        base = pl.multiple_of(rows - TILE - t * TILE, TILE)
        span = pl.ds(base, TILE)
        decay = dec[0, span, :]
        drive = decay * grad[0, span, :].astype(f32)
        entered, passed = held
        for half in reversed(range(TILE // 8)):
            part = slice(half * 8, half * 8 + 8)
            a, b = scan_rows(decay[part], drive[part], True)
            b = b + a * entered
            a = a * passed
            at = pl.ds(pl.multiple_of(base + half * 8, 8), 8)
            moved[0, at, :] = b
            reach[0, at, :] = a
            entered, passed = b[0:1], a[0:1]
        return entered, passed

    lax.fori_loop(
        0,
        rows // TILE,
        tile,
        (jnp.zeros((1, width), f32), jnp.ones((1, width), f32)),
        unroll=2,
    )


def chain_kernel(back, spot, parts, own, total, every):
    p, c, z = spot[0], spot[1], spot[2]
    factor = jnp.ones((1, own.shape[-1]), f32)
    term = jnp.zeros((1, own.shape[-1]), f32)
    count = 8 * QUARTERS
    for i in reversed(range(count)) if back else range(count):
        j, cc, zz = i // 8, i // 4 % 2, i % 4
        every[i, 0:1, :] = factor
        every[i, 1:2, :] = term
        offset = j ^ p
        slot = swapped(offset) if cc else offset
        pair = parts[(z - zz + 4) % 4, c ^ cc, slot]
        term = pair[0:1] * term + pair[1:2]
        factor = pair[0:1] * factor
    total[0:1, :] = factor
    total[1:2, :] = term
    for r in range(QUARTERS):
        j = p ^ jnp.where(c == 0, r, (r & 1) * 2 + r // 2)
        own[r] = every[(j * 2 + c) * 4 + z]


def backward_kernel(
    info, chan, rim, vec, dense, low, state, reach, enter, grad, moved, span_back, leave,
    crossed, chan_grad, rim_grad, sums,
    ext, pre, past, later, conv_grad, gates,
):
    chunk = pl.program_id(0)
    rows, width = chan.shape[1:]
    ext[:TILE] = rim[0].astype(f32)
    ext[TILE:] = chan[0].astype(f32)
    pre[...] = trailing(low[0], dense[...])
    past[0:TILE] = jnp.broadcast_to(enter[0], (TILE, width))
    later[rows : rows + TILE] = jnp.broadcast_to(leave[0], (TILE, width))
    conv_grad[:TILE] = jnp.zeros((TILE, width), f32)
    conv_grad[rows + TILE :] = jnp.zeros((TILE, width), f32)

    @pl.when(chunk == 0)
    def _():
        sums[...] = jnp.zeros_like(sums)
        crossed[...] = jnp.zeros_like(crossed)

    def fill(t, _):
        base = pl.multiple_of(t * TILE, TILE)
        span = pl.ds(base, TILE)
        past[pl.ds(pl.multiple_of(base + TILE, TILE), TILE), :] = (
            state[0, span, :] + reach[0, span, :] * enter[0]
        )
        later[span, :] = moved[0, span, :] + span_back[0, span, :] * leave[0]
        return 0

    lax.fori_loop(0, rows // TILE, fill, 0)

    def add(row, value):
        span = slice(row * 8, row * 8 + 8)
        for half in range(0, TILE, 8):
            sums[span, :] += value[half : half + 8]

    def tile(t, _):
        base = pl.multiple_of(t * TILE, TILE)
        span = pl.ds(base, TILE)
        seg, filled = place_rows(info, chunk, base, TILE)
        restart = wide((seg == 0) & filled, width)
        going = wide((seg != 0) & filled, width)
        before = past[pl.ds(base, 2 * TILE), :][TILE - 1 : 2 * TILE - 1]
        adjoint = grad[0, span, :].astype(f32) + later[pl.ds(base, 2 * TILE), :][1 : TILE + 1]
        open_decay = sigmoid(pre[span, :width] + vec[DECAY_BIAS : DECAY_BIAS + 1, :])
        open_input = sigmoid(pre[span, width:] + vec[INPUT_BIAS : INPUT_BIAS + 1, :])
        slope = vec[SLOPE : SLOPE + 1, :]
        log_decay = open_decay * slope
        decay = jnp.exp(log_decay)
        square = less_one(2.0 * log_decay)
        value = low[0, span, :].astype(f32)
        root = lax.rsqrt(square)
        root = jnp.where(going * square > 0.0, root, 0.0)
        opened = open_input * adjoint
        direct = (restart + square * root) * opened
        input_grad = direct * value * (1.0 - open_input)
        log_grad = going * decay * (adjoint * before - opened * value * decay * root)
        decay_grad = log_grad * slope * open_decay * (1.0 - open_decay)
        decay_low = decay_grad.astype(bf16)
        input_low = input_grad.astype(bf16)
        gates[span, :width] = decay_low
        gates[span, width:] = input_low
        conv_grad[pl.ds(pl.multiple_of(base + TILE, TILE), TILE), :] = direct
        add(0, decay_low.astype(f32))
        add(1, input_low.astype(f32))
        add(2, log_grad * open_decay)
        return 0

    lax.fori_loop(0, rows // TILE, tile, 0)
    conv_grad[TILE : rows + TILE] += plain(gates[...], dense[...])
    crossed[...] += leading(gates[...], low[0])

    def taps(t, _):
        base = pl.multiple_of(t * TILE, TILE)
        near = conv_grad[pl.ds(base, 2 * TILE), :]
        back = jnp.zeros((TILE, width), f32)
        for lag in range(TAPS):
            seg, _filled = place_rows(info, chunk, base - TILE + lag, TILE)
            tap = vec[TAP_ROW + lag : TAP_ROW + lag + 1, :] * near[lag : TILE + lag]
            back = back + (wide(seg >= lag, width) * tap if lag else tap)

        @pl.when(t == 0)
        def _():
            rim_grad[0] = back[TILE - 8 :]

        @pl.when(t > 0)
        def _():
            at = pl.multiple_of(base - TILE, TILE)
            chan_grad[0, pl.ds(at, TILE), :] = back
            around = ext[pl.ds(at, 2 * TILE), :]
            seg, _filled = place_rows(info, chunk, at, TILE)
            own = near[:TILE]
            add(3, own)
            for lag in range(TAPS):
                moved_in = around[TILE - lag : 2 * TILE - lag]
                moved_in = own * moved_in
                add(4 + lag, wide(seg >= lag, width) * moved_in if lag else moved_in)

        return 0

    lax.fori_loop(0, rows // TILE + 1, taps, 0)


def per_chunk(array):
    shape = array.shape
    return pl.BlockSpec((1, *shape[1:]), lambda i: (i,) + (0,) * (len(shape) - 1))


def whole(array):
    return pl.BlockSpec(array.shape, lambda i: (0,) * len(array.shape))


def in_smem():
    return pl.BlockSpec(memory_space=pltpu.SMEM)


def params():
    return pltpu.CompilerParams(vmem_limit_bytes=VMEM_BYTES)


def run_forward(info, chan, rim, vec, dense):
    count, rows, width = chan.shape
    shape = jax.ShapeDtypeStruct
    outs = [shape(chan.shape, bf16)] + [shape(chan.shape, f32)] * 3
    return pl.pallas_call(
        forward_kernel,
        grid=(count,),
        out_shape=outs,
        in_specs=[in_smem(), per_chunk(chan), per_chunk(rim), whole(vec), whole(dense)],
        out_specs=[per_chunk(o) for o in outs],
        scratch_shapes=[
            pltpu.VMEM((rows + TILE, width), f32),
            pltpu.VMEM((rows, 2 * width), f32),
        ],
        compiler_params=params(),
        cost_estimate=pl.CostEstimate(
            flops=4 * count * rows * width * width,
            bytes_accessed=count * rows * width * 84,
            transcendentals=count * rows * width * 5,
        ),
    )(info, chan, rim, vec, dense)


def run_reverse(dec, grad):
    count, rows, width = dec.shape
    outs = [jax.ShapeDtypeStruct(dec.shape, f32)] * 2
    return pl.pallas_call(
        reverse_kernel,
        grid=(count,),
        out_shape=outs,
        in_specs=[per_chunk(dec), per_chunk(grad)],
        out_specs=[per_chunk(o) for o in outs],
        compiler_params=params(),
        cost_estimate=pl.CostEstimate(
            flops=20 * count * rows * width,
            bytes_accessed=count * rows * width * 14,
            transcendentals=0,
        ),
    )(dec, grad)


def run_chain(spot, parts, back):
    width = parts.shape[-1]
    vmem = pl.BlockSpec(memory_space=pltpu.VMEM)
    return pl.pallas_call(
        partial(chain_kernel, back),
        out_shape=[
            jax.ShapeDtypeStruct((QUARTERS, 2, width), f32),
            jax.ShapeDtypeStruct((2, width), f32),
        ],
        in_specs=[in_smem(), vmem],
        out_specs=[vmem, vmem],
        scratch_shapes=[pltpu.VMEM((8 * QUARTERS, 2, width), f32)],
        compiler_params=params(),
    )(spot, parts)


def run_backward(info, chan, rim, vec, dense, low, state, reach, enter, grad, moved, span, leave):
    count, rows, width = chan.shape
    shape = jax.ShapeDtypeStruct
    outs = [
        shape((2 * width, width), f32),
        shape((count, rows, width), f32),
        shape((count, 8, width), f32),
        shape((64, width), f32),
    ]
    cut = [chan, rim, vec, dense, low, state, reach, enter, grad, moved, span, leave]
    specs = [whole(a) if a is vec or a is dense else per_chunk(a) for a in cut]
    return pl.pallas_call(
        backward_kernel,
        grid=(count,),
        out_shape=outs,
        in_specs=[in_smem(), *specs],
        out_specs=[whole(outs[0]), per_chunk(outs[1]), per_chunk(outs[2]), whole(outs[3])],
        scratch_shapes=[
            pltpu.VMEM((rows + TILE, width), f32),
            pltpu.VMEM((rows, 2 * width), f32),
            pltpu.VMEM((rows + TILE, width), f32),
            pltpu.VMEM((rows + TILE, width), f32),
            pltpu.VMEM((rows + 2 * TILE, width), f32),
            pltpu.VMEM((rows, 2 * width), bf16),
        ],
        compiler_params=params(),
        cost_estimate=pl.CostEstimate(
            flops=8 * count * rows * width * width,
            bytes_accessed=count * rows * width * 144,
            transcendentals=count * rows * width * 6,
        ),
    )(info, *cut)


def laid_kernel(cuts, at, *refs):
    pieces, outs = refs[: -len(cuts)], refs[-len(cuts) :]
    each = pieces[0].shape[0]
    for i, piece in enumerate(pieces):
        for k in range(each):
            first = 0
            for rows, out in zip(cuts, outs):
                to = pl.multiple_of(at[i * each + k] * rows, TILE)

                def move(t, _, piece=piece, k=k, to=to, first=first, out=out):
                    step = pl.multiple_of(t * TILE, TILE)
                    out[pl.ds(pl.multiple_of(to + step, TILE), TILE), :] = piece[
                        k, pl.ds(pl.multiple_of(first + step, TILE), TILE), :
                    ]
                    return 0

                lax.fori_loop(0, rows // TILE, move, 0)
                first += rows


def lay(pieces, at, cuts):
    count = at.shape[0]
    width = pieces[0].shape[-1]
    vmem = pl.BlockSpec(memory_space=pltpu.VMEM)
    return pl.pallas_call(
        partial(laid_kernel, cuts),
        out_shape=[jax.ShapeDtypeStruct((count * rows, width), pieces[0].dtype) for rows in cuts],
        in_specs=[in_smem(), *[vmem for _ in pieces]],
        out_specs=[vmem for _ in cuts],
        compiler_params=params(),
        cost_estimate=pl.CostEstimate(
            flops=0, bytes_accessed=4 * count * sum(cuts) * width, transcendentals=0
        ),
    )(at, *pieces)


def normed(values):
    rs = lax.rsqrt(jnp.mean(values * values, axis=-1, keepdims=True) + EPS)
    return rs, values * rs


def norm_back(rs, xs, gain, grad):
    scaled = gain * grad
    return rs * (scaled - xs * jnp.mean(xs * scaled, axis=-1, keepdims=True))


def body(
    places,
    tokens,
    cotangent,
    lengths,
    branch_weight,
    mixer_weight,
    branch_bias,
    mixer_bias,
    conv_taps,
    conv_bias,
    decay_weight,
    input_weight,
    decay_bias,
    input_bias,
    decay_param,
    output_weight,
    first_gain,
    second_gain,
    gate_weight,
    up_weight,
    down_weight,
):
    rows, features = tokens.shape
    slab, width = mixer_weight.shape
    block_width = decay_weight.shape[1]
    heads = width // block_width
    high = places.high
    dp_at, z = lax.axis_index("dp"), lax.axis_index("blk")
    h, p, c = dp_at // 8, dp_at // 2 % 4, dp_at % 2
    spot = jnp.stack([p, c, z]).astype(jnp.int32)

    straight = jnp.arange(QUARTERS, dtype=jnp.int32)
    order = p ^ jnp.where(c == 0, straight, (straight & 1) * 2 + straight // 2)
    chunk = ((h * 4 + order) * 2 + c) * 4 + z
    bucket_rows = BUCKET_DP * QUARTERS * rows
    start = chunk * rows
    bucket = (start + bucket_rows // 2) // bucket_rows
    begin = jnp.maximum(0, bucket * bucket_rows - bucket_rows // 2)
    ends = jnp.cumsum(jnp.take(lengths, bucket, axis=0), axis=1)
    info = jnp.concatenate([(start - begin)[:, None], ends], axis=1).astype(jnp.int32)

    inputs = tokens.astype(f32)
    gain_one, gain_two = first_gain.astype(f32), second_gain.astype(f32)
    rs_one, xs_one = normed(inputs)
    low_one = (xs_one * gain_one).astype(bf16)
    rim_rows = places.next_rows(low_one[rows - TILE :])

    def quarter(x, cuts, *others):
        every, pieces = places.spread(x, p, *others)
        at = [
            (jnp.arange(high) * 4 + (p ^ m)) * 2 + core for core in (c, 1 - c) for m in range(4)
        ]
        return every, lay([*pieces[0], *pieces[1]], jnp.concatenate(at).astype(jnp.int32), cuts)

    small = jnp.concatenate(
        [
            jnp.stack([branch_bias, mixer_bias]),
            conv_taps.T,
            jnp.stack([conv_bias, decay_bias, input_bias, decay_param]),
            jnp.zeros((TILE - PARAM - 1, width), bf16),
            decay_weight.T,
            input_weight.T,
        ],
        axis=0,
    )
    total_dp = 8 * high
    share = -(-small.shape[0] // (total_dp * TILE)) * TILE
    small = jnp.pad(small, ((0, share * total_dp - small.shape[0]), (0, 0)))
    small = lax.dynamic_slice_in_dim(small, dp_at * share, share, 0)
    held = places.gather_rows_early(jnp.concatenate([rim_rows, low_one], axis=0))
    low_rows = jnp.concatenate([a[TILE:] for a in held], axis=0)
    rim_low = jnp.concatenate([a[:TILE] for a in held], axis=0)
    early, (mixer_own, small) = quarter(
        jnp.concatenate([mixer_weight, small], axis=0), (slab, share), held[2]
    )
    vectors = small[:TILE].astype(f32)
    gate_turned = small[TILE : TILE + 2 * block_width]
    middle, (branch_own, output_own) = quarter(
        after(jnp.concatenate([branch_weight, output_weight.T], axis=0), early, held[3]),
        (slab, slab),
    )
    param = vectors[PARAM]
    vec = jnp.concatenate(
        [vectors[:SLOPE], -DECAY * jax.nn.softplus(-param)[None], vectors[SLOPE + 1 :]], axis=0
    )
    block_of = jnp.arange(width, dtype=jnp.int32) // block_width
    same = block_of[:, None] == block_of[None, :]
    dense = jnp.concatenate(
        [
            jnp.where(same, jnp.tile(gate_turned[:block_width], (heads, 1)), 0),
            jnp.where(same, jnp.tile(gate_turned[block_width:], (heads, 1)), 0),
        ],
        axis=0,
    ).astype(bf16)

    channels = (plain(low_rows, mixer_own) + vec[MIXER_BIAS]).astype(bf16)
    rim = (plain(rim_low, mixer_own) + vec[MIXER_BIAS]).astype(bf16)
    grad_near = places.one(after(cotangent, mixer_own))
    channels = after(channels, grad_near).reshape(QUARTERS, rows, width)
    rim = rim.reshape(QUARTERS, TILE, width)
    conv_low, decays, state_local, reach = run_forward(info, channels, rim, vec, dense)
    grad_late = after(cotangent, conv_low)
    grad_held = (cotangent, grad_near, places.two(grad_late), places.flip_p(grad_late, 3))
    feed_grad = jnp.concatenate(grad_held, axis=0)
    gate_use = places.gather_rest(after(gate_weight.T, mixer_own))
    up_use = places.gather_rest(after(up_weight.T, mixer_own))
    down_use = places.gather_rest(after(down_weight, conv_low))
    branch_pre = plain(low_rows, branch_own) + vec[BRANCH_BIAS]

    def entering(parts, back):
        other = places.core(parts)
        pair = jnp.stack([parts, other])
        every = jnp.stack([pair] + [places.along_z(pair, k) for k in (1, 2, 3)])
        own, total = run_chain(spot, every, back)
        if high == 1:
            return own[:, 1:2], other
        held = [total]
        for _ in range(high - 1):
            held.append(places.along_h(held[-1]))
        state = jnp.zeros((1, width), f32)
        for hop in range(high - 1):
            source = high - 1 - hop if back else hop
            far = (h - source + high) % high
            picked = lax.dynamic_index_in_dim(jnp.stack(held), far, 0, False)
            ahead = source > h if back else source < h
            state = jnp.where(ahead, picked[0:1] * state + picked[1:2], state)
        return own[:, 1:2] + own[:, 0:1] * state[None], other

    enter, _ = entering(jnp.stack([reach[:, -1], state_local[:, -1]], axis=1), False)
    state_low = (state_local + reach * enter).astype(bf16).reshape(QUARTERS * rows, width)
    mixed_low = (jax.nn.gelu(branch_pre) * state_low.astype(f32)).astype(bf16)

    two_rows = 2 * rows
    mixed_low = after(mixed_low, grad_held[2], grad_held[3])
    resid_sum = places.scatter_rows_early(
        [trailing(mixed_low[k * rows : (k + 1) * rows], output_own) for k in range(QUARTERS)]
    )
    both_own = jnp.concatenate(
        [after(branch_own, mixed_low), after(mixer_own, mixed_low)], axis=1
    )
    pre_late = after(branch_pre, mixed_low)
    branch_act, gelu_back_one = jax.vjp(jax.nn.gelu, pre_late)
    branch_slope = gelu_back_one(state_low.astype(f32))[0]
    resid_sum, branch_act, branch_slope, both_own = lax.optimization_barrier(
        (resid_sum, branch_act, branch_slope, both_own)
    )
    resid = inputs + resid_sum

    rs_two, xs_two = normed(resid)
    low_two = (xs_two * gain_two).astype(bf16)
    feed_held = places.gather_rows(low_two)
    feed_rows = jnp.concatenate(feed_held, axis=0)
    gate_pre = trailing(feed_rows, gate_use)
    up_pre = trailing(feed_rows, up_use)
    gate_act, gelu_back_two = jax.vjp(jax.nn.gelu, gate_pre)
    hidden, gate_act, gate_slope = lax.optimization_barrier(
        (
            (gate_act * up_pre).astype(bf16),
            gate_act.astype(bf16),
            gelu_back_two(up_pre)[0].astype(bf16),
        )
    )
    half = hidden.shape[1] // 2

    def columns(array, core):
        return lax.dynamic_slice_in_dim(array, core * half, half, 1)

    def column_far(grad, rows_in):
        return leading(columns(grad, 1 - c), rows_in).astype(bf16)

    def column_own(grad, rows_in, far):
        total = leading(columns(grad, c), rows_in) + places.core(far).astype(f32)
        return total.astype(bf16)

    def column_scatter(total):
        return lax.psum_scatter(total, "blk", scatter_dimension=0, tiled=True)

    def column_sum(total):
        if high > 1:
            total = total.reshape(high, -1, features)
            total = jnp.take(total, (h - jnp.arange(high)) % high, axis=0)
            total = places.scatter_high(total.reshape(-1, features))
        return total.astype(f32)

    down_far = column_far(hidden, feed_grad)
    hidden_grad = trailing(feed_grad, after(down_use, down_far))
    gate_grad = (hidden_grad * gate_slope.astype(f32)).astype(bf16)
    up_grad = (hidden_grad * gate_act.astype(f32)).astype(bf16)
    def norm_part(span):
        return plain(gate_grad[span], gate_use) + plain(up_grad[span], up_use)

    norm_far = norm_part(slice(two_rows, None)).astype(bf16)
    gate_grad, up_grad, hidden_late, norm_far = lax.optimization_barrier(
        (gate_grad, up_grad, hidden, norm_far)
    )
    down_own = column_own(hidden_late, feed_grad, down_far)
    down_scattered = column_scatter(down_own)
    norm_near = norm_part(slice(two_rows))
    norm_grad, _ = places.scatter_rows(norm_far, norm_near)
    gate_late, *_ = lax.optimization_barrier((gate_grad, norm_near, down_own))
    gate_far = column_far(gate_late, feed_rows)
    norm_grad = after(norm_grad, gate_far)
    second_term = jnp.sum(norm_grad * xs_two, axis=0)
    resid_grad = cotangent.astype(f32) + norm_back(rs_two, xs_two, gain_two, norm_grad)

    resid_low = resid_grad.astype(bf16)
    resid_rows = jnp.concatenate(places.gather_rows(resid_low), axis=0)
    gate_last, up_late, hidden_last, _ = lax.optimization_barrier(
        (gate_late, up_grad, hidden, resid_low)
    )
    gate_own = column_own(gate_last, feed_rows, gate_far)
    gate_scattered = column_scatter(gate_own)
    up_far = column_far(up_late, feed_rows)
    output_far = plain(hidden_last[two_rows:], down_use)
    output_near = plain(hidden_last[:two_rows], down_use)
    resid_rows, output_far, output_near, *_ = lax.optimization_barrier(
        (resid_rows, output_far, output_near, up_far, gate_own, down_scattered)
    )
    output, output_joined = places.scatter_rows(output_far, output_near)
    output = (resid + output).astype(bf16)
    mixed_grad = plain(resid_rows, output_own)
    state_grad = (mixed_grad * branch_act).astype(bf16).reshape(QUARTERS, rows, width)
    branch_grad = (mixed_grad * branch_slope).astype(bf16)
    moved, span_back = run_reverse(decays, state_grad)
    leave, other = entering(jnp.stack([span_back[:, 0], moved[:, 0]], axis=1), True)
    up_last = after(up_late, other)
    resid_late, mixed_late, _ = lax.optimization_barrier((resid_rows, mixed_low, other))

    def quarter_half(term, *others):
        slab_in = term.shape[0] // total_dp
        term = term.astype(bf16).reshape(high * 4, 2 * slab_in, width)
        own = lax.dynamic_slice_in_dim(term, c * slab_in, slab_in, 1)
        other = lax.dynamic_slice_in_dim(term, (1 - c) * slab_in, slab_in, 1)
        came = places.core(other)
        half = own + after(came, *others)
        return half.reshape(high, 4, slab_in, width), other, came

    def quarter_rows(half):
        return [
            places.flip_p(lax.dynamic_index_in_dim(half, p ^ m, 1, False), m) for m in range(4)
        ]

    def quarter_high(total):
        if high > 1:
            total = jnp.take(total, (h - jnp.arange(high)) % high, axis=0)
            return places.scatter_high(total.reshape(-1, width))
        return total[0].astype(f32)

    def quarter_near(parts):
        stacked = jnp.stack(parts)

        def by(k):
            return lax.dynamic_index_in_dim(stacked, p ^ ((z + k) % 4), 0, False)

        came = [places.along_z(by(k), k) for k in (1, 2, 3)]
        total = by(0).astype(f32)
        for a in came:
            total = total + a.astype(f32)
        return quarter_high(total), came

    def quarter_far(parts, other):
        *parts, _ = lax.optimization_barrier((*parts, other))
        stacked = jnp.take(jnp.stack(parts), p ^ straight, axis=0)
        return quarter_high(lax.psum_scatter(stacked, "blk", scatter_dimension=0, tiled=True)[0])

    output_term = leading(resid_late, mixed_late)
    up_own = column_own(up_last, feed_rows, up_far)
    up_scattered = column_scatter(up_own)
    output_half, _, _ = quarter_half(output_term)
    leave, output_half, *_ = lax.optimization_barrier(
        (leave, output_half, output_joined, up_own, gate_scattered)
    )
    output_parts = quarter_rows(output_half)
    crossed, chan_grad, rim_grad, sums8 = run_backward(
        info, channels, rim, vec, dense, conv_low, state_local, reach, enter, state_grad, moved,
        span_back, leave,
    )

    low_late, branch_late, _ = lax.optimization_barrier((low_rows, branch_grad, rim_grad))
    branch_term = leading(low_late, branch_late)

    came = places.back_rows(rim_grad)
    last = (c == 1) & (z == 3)
    wanted = order + jnp.where(last, 1, 0)
    from_core = jnp.where(z == 3, 1 - c, c)
    offset = (wanted % 4) ^ p
    slot = jnp.where(from_core == 0, offset, (offset & 1) * 2 + offset // 2)
    pick = (slot[:, None] == straight[None, :]).astype(f32)
    here = jnp.where(wanted < 4, 1.0, 0.0)[:, None]

    def picked(select, array):
        return jnp.sum(select[:, :, None, None] * array[None], axis=1)

    returned = picked(pick * here, came)
    if high > 1:
        returned = returned + picked(pick * (1.0 - here), places.back_high(came))
    output_sum = quarter_far(output_parts, came).T
    chan_grad = chan_grad + jnp.pad(returned, ((0, 0), (rows - 8, 0), (0, 0)))
    mixer_grad = chan_grad.astype(bf16).reshape(QUARTERS * rows, width)

    picked_blocks = block_of[None, :] == jnp.arange(heads)[:, None]
    gate_terms = jnp.sum(
        jnp.where(picked_blocks[None, :, None, :], crossed.reshape(2, heads, block_width, width), 0),
        axis=1,
    )
    vector_terms = jnp.concatenate(
        [
            jnp.sum(sums8.reshape(8, 8, width), axis=1),
            jnp.sum(branch_grad.astype(f32), axis=0)[None],
            jnp.sum(mixer_grad.astype(f32), axis=0)[None],
            jnp.zeros((6, width), f32),
        ],
        axis=0,
    )
    slope_back = DECAY * jax.nn.sigmoid(-param)
    vector_terms = vector_terms.at[2].multiply(slope_back)
    small_terms = jnp.concatenate(
        [vector_terms, gate_terms.reshape(2 * block_width, width)], axis=0
    ).astype(bf16)
    small_terms = jnp.pad(small_terms, ((0, share * total_dp - small_terms.shape[0]), (0, 0)))
    branch_term, branch_both = lax.optimization_barrier((branch_term, branch_term.astype(bf16)))
    branch_both = jnp.concatenate(
        [branch_both.reshape(total_dp, slab, width), small_terms.reshape(total_dp, share, width)],
        axis=1,
    ).reshape(-1, width)
    mixer_term = leading(low_rows, mixer_grad)
    mixer_half, mixer_other, mixer_came = quarter_half(mixer_term)
    both_grads = jnp.concatenate([branch_grad, mixer_grad], axis=1)
    both_grads = after(both_grads, mixer_other)
    low_far = trailing(both_grads[two_rows:], both_own).astype(bf16)
    both_near, low_far, mixer_half, _ = lax.optimization_barrier(
        (both_grads[:two_rows], low_far, mixer_half, mixer_came)
    )
    branch_half, _, _ = quarter_half(after(branch_both, low_far, up_scattered))
    branch_parts = quarter_rows(branch_half)
    mixer_parts = quarter_rows(mixer_half)
    low_near = trailing(both_near, both_own)
    low_grad, low_joined = places.scatter_rows(low_far, low_near)
    branch_sum = quarter_far(branch_parts, low_near)
    mixer_sum, mixer_last = quarter_near(mixer_parts)
    mixer_term, second_term, _ = lax.optimization_barrier((mixer_term, second_term, low_grad))
    low_grad = after(low_grad, *mixer_last)
    token_grad = (resid_grad + norm_back(rs_one, xs_one, gain_one, low_grad)).astype(bf16)

    first_term = (
        jnp.sum(branch_term * branch_own.astype(f32), axis=1)
        + jnp.sum(mixer_term * mixer_own.astype(f32), axis=1)
    ) / gain_one
    gain_sums = places.sum_all(jnp.stack([first_term, second_term]))

    branch_sum, small_sum = branch_sum[:slab], branch_sum[slab:]
    small_held = [small_sum]
    for _ in range(high - 1):
        small_held.append(places.along_h(small_held[-1]))
    small_held = jnp.stack(small_held)
    small_held = jnp.concatenate(places.gather_rows(small_held), axis=0)
    small_held = jnp.stack([small_held, places.core(small_held)])
    where = []
    for hh in range(high):
        for a in range(4):
            for core in range(2):
                offset = p ^ a
                crossed_at = (offset & 1) * 2 + offset // 2
                slot = offset if core == 0 else crossed_at
                where.append((((c ^ core) * 4 + slot) * high) + (h - hh + high) % high)
    small_total = jnp.take(
        small_held.reshape(-1, share, width), jnp.stack(where), axis=0
    ).reshape(-1, width)
    vector_total = small_total[:TILE]
    gate_total = small_total[TILE : TILE + 2 * block_width]
    gate_sum, up_sum = column_sum(gate_scattered).T, column_sum(up_scattered).T
    down_sum = column_sum(down_scattered)
    return (
        output,
        token_grad,
        branch_sum,
        mixer_sum,
        vector_total[8],
        vector_total[9],
        vector_total[4:8].T,
        vector_total[3],
        gate_total[:block_width].T,
        gate_total[block_width:].T,
        vector_total[0],
        vector_total[1],
        vector_total[2],
        output_sum,
        gain_sums[0],
        gain_sums[1],
        gate_sum,
        up_sum,
        down_sum,
    )


def solution(mesh):
    places = Places(mesh.shape["dp"], mesh.shape["blk"])
    return jax.shard_map(
        partial(body, places),
        mesh=mesh,
        in_specs=(
            P(("dp", "blk"), None),
            P(("dp", "blk"), None),
            P(),
            P("dp", "blk"),
            P("dp", "blk"),
            P("blk"),
            P("blk"),
            P("blk", None),
            P("blk"),
            P("blk", None),
            P("blk", None),
            P("blk"),
            P("blk"),
            P("blk"),
            P("blk", "dp"),
            P(),
            P(),
            P(None, ("dp", "blk")),
            P(None, ("dp", "blk")),
            P(("dp", "blk"), None),
        ),
        out_specs=(
            P(("dp", "blk"), None),
            P(("dp", "blk"), None),
            P("dp", "blk"),
            P("dp", "blk"),
            P("blk"),
            P("blk"),
            P("blk", None),
            P("blk"),
            P("blk", None),
            P("blk", None),
            P("blk"),
            P("blk"),
            P("blk"),
            P("blk", "dp"),
            P(),
            P(),
            P(None, ("dp", "blk")),
            P(None, ("dp", "blk")),
            P(("dp", "blk"), None),
        ),
        check_vma=False,
    )
```
